32 devices in a mesh: dom: 8 (over y, x, core), sub: 4 (over z).
Axes of the slice: x: 2, y: 2, z: 4, core: 2. Of those that a mesh axis runs over, the one named last changes fastest.
Arguments:
- solution: float32 [8, 8, 8, 16384], P(None, None, None, ('dom', 'sub')), may hold values from -6 to 6
- forcing: float32 [8, 8, 8, 16384], P(None, None, None, ('dom', 'sub')), may hold values from -600 to 600
- metric: float32 [7, 8, 8, 8, 16384], P(None, None, None, None, ('dom', 'sub')), may hold values from -2.5 to 100, as said below
- entity_ids: int32 [26, 16384], P(None, ('dom', 'sub')), may hold values from 0 to 49151, as said below
- new_owner: int32 [16384], P(('dom', 'sub')), may hold values from 0 to 31, as said below
Outputs:
- smoothed: float32 [8, 8, 8, 16384], P(None, None, None, ('dom', 'sub'))
- moved_metric: float32 [7, 8, 8, 8, 16384], P(None, None, None, None, ('dom', 'sub'))
The draws below stay inside these ranges and needn't reach their ends.
Inputs may be any that keep to these rules, and one draw needn't show every extreme that they name: `new_owner`: an element stays on its device or goes to one of the device's four neighbours: the previous or next device along dom with the same sub index, or the previous or next along sub with the same dom index, indices wrapping around. Two neighbouring devices hand each other equally many elements, at most 64; in every draw some pair of neighbours along dom and some pair along sub hand each other exactly 64. `entity_ids`: face and edge ids come in blocks of 1536 consecutive ids, corner ids in blocks of 512; block b is summed by device b. Every face id is carried by exactly 2 element faces, every edge id by exactly 4 element edges, every corner id by exactly 8 element corners, their shared nodes lining up in the listed order. An id carried by a device's elements lies in the device's own block or in that of the next device along dom, along sub, or along both (indices wrapping around); every device's elements carry exactly 128 faces, 480 edges and 448 corners of the next block along dom, exactly 128 faces, 480 edges and 448 corners of the next block along sub, and exactly 32 edges, 64 corners and no face of the next block along both. metric[0], metric[1], metric[2] and metric[6] are positive; at every node |metric[3]| <= 0.5 sqrt(metric[0] metric[1]), |metric[4]| <= 0.5 sqrt(metric[0] metric[2]), |metric[5]| <= 0.5 sqrt(metric[1] metric[2]).
All inputs are finite; a program needn't handle non-finite values.
Results may differ from the reference program's by a relative error of at most 0.00005.
Values sent between devices are 32-bit elements; how exact they have to be, the bound alone decides.
No kernel may reach another device: no remote copies, remote signals or barrier semaphores. Data moves between devices by JAX's collectives and lax.ppermute only.
A program may use at most 128 MiB of HBM per device.

```python
import math
import jax
import jax.numpy as jnp
import numpy as np
from jax import lax

NP = 8
EX = 4
EY = 4
EZ = 32
E_DEV = 512
MOVE = 64
ELEMS = 16384
N_DOM = 8
N_SUB = 4


def device_grid():
    dev_total = N_DOM * N_SUB
    devices = jnp.arange(dev_total, dtype=jnp.int32)
    return (devices, devices // N_SUB, devices % N_SUB)


def draw_new_owner(key, part):
    dev_total = N_DOM * N_SUB
    devices, dom_place, sub_place = device_grid()
    base_key = jax.random.fold_in(key, 7)
    dom_key, sub_key, pick_dom, pick_sub, order_key = jax.random.split(base_key, 5)
    lowest = (MOVE + 1) // 2
    dom_pairs = jax.random.randint(dom_key, (dev_total,), lowest, MOVE + 1).astype(jnp.int32)
    dom_pairs = dom_pairs.at[jax.random.randint(pick_dom, (), 0, dev_total)].set(MOVE)
    sub_pairs = jax.random.randint(sub_key, (dev_total,), lowest, MOVE + 1).astype(jnp.int32)
    sub_pairs = sub_pairs.at[jax.random.randint(pick_sub, (), 0, dev_total)].set(MOVE)
    prev_dom = (dom_place + N_DOM - 1) % N_DOM * N_SUB + sub_place
    next_dom = (dom_place + 1) % N_DOM * N_SUB + sub_place
    prev_sub = dom_place * N_SUB + (sub_place + N_SUB - 1) % N_SUB
    next_sub = dom_place * N_SUB + (sub_place + 1) % N_SUB
    counts = jnp.stack([dom_pairs[prev_dom], dom_pairs, sub_pairs[prev_sub], sub_pairs], axis=1)
    targets = jnp.stack([prev_dom, next_dom, prev_sub, next_sub], axis=1)
    bounds = jnp.cumsum(counts, axis=1).astype(jnp.int32)
    ranks = jnp.arange(E_DEV, dtype=jnp.int32)
    direction = jnp.sum((ranks[None, :, None] >= bounds[:, None, :]).astype(jnp.int32), axis=2)
    picked = jnp.take_along_axis(targets, jnp.clip(direction, 0, 3), axis=1)
    chosen_owner = jnp.where(direction < 4, picked, devices[:, None]).astype(jnp.int32)
    orders = jax.vmap(lambda sub_key_one: jax.random.permutation(sub_key_one, E_DEV).astype(jnp.int32))(jax.random.split(order_key, dev_total))
    owners = jnp.zeros((dev_total, E_DEV), jnp.int32).at[devices[:, None], orders].set(chosen_owner)
    return owners.reshape(-1)


def draw_entity_ids(key, part):
    dev_total = N_DOM * N_SUB
    devices, dom_place, sub_place = device_grid()
    base_key = jax.random.fold_in(key, 21)
    layout_key, face_key, edge_key, corner_key = jax.random.split(base_key, 4)

    def permutations(perm_key, length):
        return jax.vmap(lambda one_key: jax.random.permutation(one_key, length).astype(jnp.int32))(jax.random.split(perm_key, dev_total))
    layout = permutations(layout_key, E_DEV)
    slot_values = jnp.broadcast_to(jnp.arange(E_DEV, dtype=jnp.int32)[None, :], (dev_total, E_DEV))
    slot_of = jnp.zeros((dev_total, E_DEV), jnp.int32).at[devices[:, None], layout].set(slot_values)
    coord_x = dom_place[:, None] * EX + layout // (EY * EZ)
    coord_y = sub_place[:, None] * EY + layout // EZ % EY
    coord_z = layout % EZ
    face_perm = permutations(face_key, 3 * E_DEV)
    edge_perm = permutations(edge_key, 3 * E_DEV)
    corner_perm = permutations(corner_key, E_DEV)

    def owned(shift_x, shift_y, shift_z, axis_index, per_elem, perm_table):
        owner_x = (coord_x + shift_x) % (EX * N_DOM)
        owner_y = (coord_y + shift_y) % (EY * N_SUB)
        owner_z = (coord_z + shift_z) % EZ
        owner_dev = owner_x // EX * N_SUB + owner_y // EY
        owner_local = (owner_x % EX * EY + owner_y % EY) * EZ + owner_z
        owner_slot = slot_of[owner_dev, owner_local]
        owner_row = owner_slot * per_elem + axis_index
        return owner_dev * (per_elem * E_DEV) + perm_table[owner_dev, owner_row]
    rows_out = []
    for face_index in range(6):
        axis_index = face_index // 2
        offset = face_index % 2
        shifts = [0, 0, 0]
        shifts[axis_index] = offset
        rows_out.append(owned(shifts[0], shifts[1], shifts[2], axis_index, 3, face_perm))
    for edge_index in range(12):
        axis_index = edge_index // 4
        first_bit = edge_index % 4 // 2
        second_bit = edge_index % 2
        if axis_index == 0:
            shifts = (0, first_bit, second_bit)
        elif axis_index == 1:
            shifts = (first_bit, 0, second_bit)
        else:
            shifts = (first_bit, second_bit, 0)
        rows_out.append(owned(shifts[0], shifts[1], shifts[2], axis_index, 3, edge_perm))
    for corner_index in range(8):
        rows_out.append(owned(corner_index // 4, corner_index // 2 % 2, corner_index % 2, 0, 1, corner_perm))
    return jnp.stack(rows_out).reshape(26, dev_total * E_DEV).astype(jnp.int32)


def draw_metric(key, part):
    array_shape = (NP, NP, NP, ELEMS)
    subkeys = [jax.random.fold_in(key, 100 + layer_index) for layer_index in range(7)]
    factors = [jnp.exp(jax.random.uniform(subkeys[layer_index], array_shape, jnp.float32, math.log(0.2), math.log(5.0))) for layer_index in range(3)]
    mass_term = jnp.exp(jax.random.uniform(subkeys[6], array_shape, jnp.float32, math.log(5.0), math.log(100.0)))
    spreads = [jax.random.uniform(subkeys[3 + layer_index], array_shape, jnp.float32, -0.45, 0.45) for layer_index in range(3)]
    cross_rs = spreads[0] * jnp.sqrt(factors[0] * factors[1])
    cross_rt = spreads[1] * jnp.sqrt(factors[0] * factors[2])
    cross_st = spreads[2] * jnp.sqrt(factors[1] * factors[2])
    return jnp.stack([factors[0], factors[1], factors[2], cross_rs, cross_rt, cross_st, mass_term]).astype(jnp.float32)


def levels(key, dims, shards, smallest, high):
    def one(dim, blocks):
        heights = jax.random.uniform(jax.random.fold_in(jax.random.fold_in(key, 6), dim), (blocks,), jnp.float32, smallest / len(shards), high / len(shards))
        return jnp.repeat(jnp.exp(heights), dims[dim] // blocks).reshape((-1,) + (1,) * (len(dims) - dim - 1))

    gain = one(*shards[0])
    for cut in shards[1:]:
        gain = gain * one(*cut)
    return gain


def scatter_about(key, shape, scale, bound, cuts=(), held_as=jnp.bfloat16):
    drawn = jax.random.normal(key, shape, jnp.float32) * scale
    if len(cuts) > 0:
        drawn = levels(key, shape, cuts, -0.22, 0.18) * drawn
    return jnp.clip(drawn, min=-bound, max=bound).astype(held_as)


def setup_inputs(seed: int = 0) -> dict:
    splits = jax.random.split(jax.random.key(seed), 6)
    return {
        "solution": scatter_about(splits[0], (NP, NP, NP, ELEMS), 1.0, 6.0, ((3, 32),), jnp.float32),
        "forcing": scatter_about(splits[1], (NP, NP, NP, ELEMS), 100.0, 600.0, ((3, 32),), jnp.float32),
        "metric": draw_metric(jax.random.fold_in(splits[5], 71), 0),
        "entity_ids": draw_entity_ids(jax.random.fold_in(splits[5], 71), 0),
        "new_owner": draw_new_owner(jax.random.fold_in(splits[5], 71), 0),
    }


RELAX = 0.6


def derivative_table(order):
    count = order + 1
    points = -np.cos(np.pi * np.arange(count) / order)
    legendre = np.zeros((count, count))
    for sweep in range(80):
        legendre[:, 0] = 1.0
        legendre[:, 1] = points
        for degree in range(2, count):
            legendre[:, degree] = ((2 * degree - 1) * points * legendre[:, degree - 1] - (degree - 1) * legendre[:, degree - 2]) / degree
        points = points - (points * legendre[:, order] - legendre[:, order - 1]) / (count * legendre[:, order])
    legendre[:, 0] = 1.0
    legendre[:, 1] = points
    for degree in range(2, count):
        legendre[:, degree] = ((2 * degree - 1) * points * legendre[:, degree - 1] - (degree - 1) * legendre[:, degree - 2]) / degree
    values = legendre[:, order]
    identity = np.eye(count)
    spread = points[:, None] - points[None, :] + identity
    table = values[:, None] / values[None, :] / spread
    table = table * (1.0 - identity)
    table[0, 0] = -order * count / 4.0
    table[order, order] = order * count / 4.0
    return jnp.asarray(table, dtype=jnp.float32)


def element_apply(solution, metric, derivative):
    highest = lax.Precision.HIGHEST
    grad_r = jnp.einsum('ai,ijke->ajke', derivative, solution, precision=highest)
    grad_s = jnp.einsum('bj,ijke->ibke', derivative, solution, precision=highest)
    grad_t = jnp.einsum('ck,ijke->ijce', derivative, solution, precision=highest)
    flux_r = metric[0] * grad_r + metric[3] * grad_s + metric[4] * grad_t
    flux_s = metric[3] * grad_r + metric[1] * grad_s + metric[5] * grad_t
    flux_t = metric[4] * grad_r + metric[5] * grad_s + metric[2] * grad_t
    image = jnp.einsum('ai,ajke->ijke', derivative, flux_r, precision=highest)
    image = image + jnp.einsum('bj,ibke->ijke', derivative, flux_s, precision=highest)
    image = image + jnp.einsum('ck,ijce->ijke', derivative, flux_t, precision=highest)
    image = image + metric[6] * solution
    squared = derivative * derivative
    diagonal = jnp.einsum('ai,ajke->ijke', squared, metric[0], precision=highest)
    diagonal = diagonal + jnp.einsum('bj,ibke->ijke', squared, metric[1], precision=highest)
    diagonal = diagonal + jnp.einsum('ck,ijce->ijke', squared, metric[2], precision=highest)
    along = jnp.diagonal(derivative)
    along_i = along[:, None, None, None]
    along_j = along[None, :, None, None]
    along_k = along[None, None, :, None]
    diagonal = diagonal + 2.0 * along_i * along_j * metric[3] + 2.0 * along_i * along_k * metric[4] + 2.0 * along_j * along_k * metric[5]
    diagonal = diagonal + metric[6]
    return image, diagonal


def shared_slots(final_index):
    inside = slice(1, final_index)
    end_points = (0, final_index)
    face_slots = [(0, inside, inside), (final_index, inside, inside), (inside, 0, inside), (inside, final_index, inside), (inside, inside, 0), (inside, inside, final_index)]
    edge_slots = [(inside, first_end, second_end) for first_end in end_points for second_end in end_points]
    edge_slots = edge_slots + [(first_end, inside, second_end) for first_end in end_points for second_end in end_points]
    edge_slots = edge_slots + [(first_end, second_end, inside) for first_end in end_points for second_end in end_points]
    corner_slots = [(first_end, second_end, third_end) for first_end in end_points for second_end in end_points for third_end in end_points]
    return face_slots, edge_slots, corner_slots


def shared_parts(element_cube):
    face_slots, edge_slots, corner_slots = shared_slots(element_cube.shape[0] - 1)
    face_part = jnp.stack([element_cube[slot_index] for slot_index in face_slots])
    edge_part = jnp.stack([element_cube[slot_index] for slot_index in edge_slots])
    corners = jnp.stack([element_cube[slot_index] for slot_index in corner_slots])
    return face_part, edge_part, corners


def place_shared(element_cube, face_part, edge_part, corners):
    face_slots, edge_slots, corner_slots = shared_slots(element_cube.shape[0] - 1)
    for number, slot_index in enumerate(face_slots):
        element_cube = element_cube.at[slot_index].set(face_part[number])
    for number, slot_index in enumerate(edge_slots):
        element_cube = element_cube.at[slot_index].set(edge_part[number])
    for number, slot_index in enumerate(corner_slots):
        element_cube = element_cube.at[slot_index].set(corners[number])
    return element_cube


def assemble_kind(part, ids, segments):
    kind_count = part.shape[0]
    elem_total = part.shape[-1]
    by_element = jnp.moveaxis(part, -1, 1)
    inner_shape = by_element.shape[2:]
    flattened = by_element.reshape(kind_count * elem_total, -1)
    segment_ids = ids.reshape(-1).astype(jnp.int32)
    totals = jax.ops.segment_sum(flattened, segment_ids, num_segments=segments)
    returned = jnp.take(totals, segment_ids, axis=0).reshape((kind_count, elem_total) + inner_shape)
    return jnp.moveaxis(returned, 1, -1)


def new_positions(new_owner, dom_total, sub_total, per_dev):
    dev_total = dom_total * sub_total
    elem_total = dev_total * per_dev
    element = jnp.arange(elem_total, dtype=jnp.int32)
    home_device = (element // per_dev).astype(jnp.int32)
    dom_place = home_device // sub_total
    sub_place = home_device % sub_total
    neighbours = [((dom_place + dom_total - 1) % dom_total) * sub_total + sub_place, ((dom_place + 1) % dom_total) * sub_total + sub_place, dom_place * sub_total + (sub_place + sub_total - 1) % sub_total, dom_place * sub_total + (sub_place + 1) % sub_total]
    departed = new_owner != home_device
    out_dir = jnp.zeros((elem_total,), jnp.int32)
    rank_in = jnp.zeros((elem_total,), jnp.int32)
    for direction, neighbour in enumerate(neighbours):
        chosen = departed & (new_owner == neighbour)
        ranked = (jnp.cumsum(chosen.reshape(dev_total, per_dev).astype(jnp.int32), axis=1) - 1).astype(jnp.int32).reshape(-1)
        out_dir = jnp.where(chosen, jnp.int32(direction), out_dir).astype(jnp.int32)
        rank_in = jnp.where(chosen, ranked, rank_in).astype(jnp.int32)
    in_dir = (out_dir + 1 - 2 * (out_dir % 2)).astype(jnp.int32)
    arrivals = jnp.zeros((dev_total, 4), jnp.int32).at[new_owner, in_dir].add(departed.astype(jnp.int32))
    offsets = (jnp.cumsum(arrivals, axis=1) - arrivals).astype(jnp.int32)
    hole_index = (offsets[new_owner, in_dir] + rank_in).astype(jnp.int32)
    leaving = departed.reshape(dev_total, per_dev)
    hole_rank = (jnp.cumsum(leaving.astype(jnp.int32), axis=1) - 1).astype(jnp.int32)
    peers = jnp.arange(dev_total, dtype=jnp.int32)
    slot_values = jnp.broadcast_to(jnp.arange(per_dev, dtype=jnp.int32)[None, :], (dev_total, per_dev))
    hole_slot = jnp.zeros((dev_total, per_dev), jnp.int32).at[peers[:, None], jnp.where(leaving, hole_rank, per_dev)].set(slot_values, mode="drop")
    target = new_owner * per_dev + hole_slot[new_owner, jnp.clip(hole_index, 0, per_dev - 1)]
    return jnp.where(departed, target, element).astype(jnp.int32)


def reference(solution, forcing, metric, entity_ids, new_owner):
    elem_total = solution.shape[-1]
    derivative = derivative_table(NP - 1)
    image, diagonal = element_apply(solution, metric, derivative)
    both = jnp.stack([image, diagonal], axis=3)
    face_part, edge_part, corners = shared_parts(both)
    face_part = assemble_kind(face_part, entity_ids[0:6], 3 * elem_total)
    edge_part = assemble_kind(edge_part, entity_ids[6:18], 3 * elem_total)
    corners = assemble_kind(corners, entity_ids[18:26], elem_total)
    assembled = place_shared(both, face_part, edge_part, corners)
    relaxed = solution + RELAX * (forcing - assembled[:, :, :, 0]) / assembled[:, :, :, 1]
    position = new_positions(new_owner, N_DOM, N_SUB, E_DEV)
    smoothed = jnp.zeros_like(relaxed).at[..., position].set(relaxed)
    moved_metric = jnp.zeros_like(metric).at[..., position].set(metric)
    return smoothed, moved_metric
```

```python
import functools

import jax
import jax.numpy as jnp
import numpy as np
from jax import lax
from jax.experimental import pallas as pl
from jax.experimental.pallas import tpu as pltpu
from jax.sharding import PartitionSpec as P

EX = 4
EY = 4
EZ = 32
MOVE = 64
RELAX = 0.6
LANES = 128
INNER = 6
CHUNKS = (4, 3)

NT = (((1,), (1,)), ((), ()))
VMEM = pl.BlockSpec(memory_space=pltpu.VMEM)
F32 = jnp.float32
BF16 = jnp.bfloat16
I32 = jnp.int32


def derivative_table(order):
    count = order + 1
    points = -np.cos(np.pi * np.arange(count) / order)
    legendre = np.zeros((count, count))
    for sweep in range(80):
        legendre[:, 0] = 1.0
        legendre[:, 1] = points
        for degree in range(2, count):
            legendre[:, degree] = (
                (2 * degree - 1) * points * legendre[:, degree - 1]
                - (degree - 1) * legendre[:, degree - 2]
            ) / degree
        points = points - (points * legendre[:, order] - legendre[:, order - 1]) / (
            count * legendre[:, order]
        )
    legendre[:, 0] = 1.0
    legendre[:, 1] = points
    for degree in range(2, count):
        legendre[:, degree] = (
            (2 * degree - 1) * points * legendre[:, degree - 1]
            - (degree - 1) * legendre[:, degree - 2]
        ) / degree
    values = legendre[:, order]
    identity = np.eye(count)
    spread = points[:, None] - points[None, :] + identity
    table = values[:, None] / values[None, :] / spread
    table = table * (1.0 - identity)
    table[0, 0] = -order * count / 4.0
    table[order, order] = order * count / 4.0
    return table.astype(np.float32)


def split_np(matrix):
    high = matrix.astype(jnp.bfloat16).astype(np.float32)
    low = (matrix - high).astype(jnp.bfloat16)
    return np.concatenate([high.astype(jnp.bfloat16), low, high.astype(jnp.bfloat16)], axis=1)


def split(values):
    high = values.astype(BF16)
    low = (values - high.astype(F32)).astype(BF16)
    return high, low


def triple(values):
    high, low = split(values)
    return jnp.concatenate([high, high, low], axis=0)


def dot(left, right):
    return jnp.dot(left, right, preferred_element_type=F32)


def dot_nt(left, right):
    return lax.dot_general(left, right, NT, preferred_element_type=F32)


def iota(shape, dim):
    return lax.broadcasted_iota(I32, shape, dim)


def one_hot_rows(index_row, start, count):
    size = index_row.shape[1]
    out = []
    for base in range(0, count, LANES):
        local = (index_row - (start + base)).astype(BF16)
        rows = iota((LANES, size), 0).astype(BF16)
        out.append(
            jnp.where(rows == local, jnp.ones((LANES, size), BF16), jnp.zeros((LANES, size), BF16))
        )
    return out[0] if len(out) == 1 else jnp.concatenate(out, axis=0)


def exclusive_count(masks):
    size = masks.shape[1]
    upper = jnp.where(iota((size, size), 0) < iota((size, size), 1), 1.0, 0.0).astype(BF16)
    return dot(masks.astype(BF16), upper)


def gather_tiles(tiles, low, high):
    out = None
    for number, tile in enumerate(tiles):
        got = jnp.take_along_axis(tile, low, axis=1)
        out = got if out is None else jnp.where(high == number, got, out)
    return out


def devices():
    dom_count = lax.axis_size("dom")
    sub_count = lax.axis_size("sub")
    dom = lax.axis_index("dom")
    sub = lax.axis_index("sub")
    dom_ahead = lax.rem(dom + 1, dom_count)
    dom_behind = lax.rem(dom + dom_count - 1, dom_count)
    sub_ahead = lax.rem(sub + 1, sub_count)
    sub_behind = lax.rem(sub + sub_count - 1, sub_count)
    return jnp.stack(
        [
            dom_behind * sub_count + sub,
            dom_ahead * sub_count + sub,
            dom * sub_count + sub_behind,
            dom * sub_count + sub_ahead,
            dom * sub_count + sub,
            dom_ahead * sub_count + sub_ahead,
        ]
    ).astype(I32)


def pack_pair(values):
    half = values.shape[0] // 2
    top, bottom = values[:half], values[half:]
    left = iota(top.shape, 1) < MOVE
    first = jnp.where(left, top, pltpu.roll(bottom, MOVE, 1))
    second = jnp.where(left, pltpu.roll(top, MOVE, 1), bottom)
    return first, second


def unpack_pair(first, second):
    left = iota(first.shape, 1) < MOVE
    top = jnp.where(left, first, pltpu.roll(second, MOVE, 1))
    bottom = jnp.where(left, pltpu.roll(first, MOVE, 1), second)
    return jnp.concatenate([top, bottom], axis=0)


def pick_columns(values, source_row):
    rows, size = values.shape
    source = jnp.broadcast_to(source_row, (rows, LANES))
    tiles = [values[:, c : c + LANES] for c in range(0, size, LANES)]
    return gather_tiles(tiles, source & (LANES - 1), source >> 7)


def move_plan(owner, place):
    size = owner.shape[1]
    own = place[4]
    line = iota((8, size), 0)
    target = jnp.where(
        line == 0,
        place[0],
        jnp.where(line == 1, place[1], jnp.where(line == 2, place[2], place[3])),
    )
    nobody = jnp.broadcast_to(owner, (8, size))
    away = nobody != own
    masks = jnp.where(away & (((nobody == target) & (line < 4)) | (line == 4)), 1.0, 0.0)
    ranks = exclusive_count(masks)
    counts = jnp.sum(masks, axis=1, keepdims=True)
    hole = ranks[4:5]
    gone = masks[4:5] > 0.5
    column = jnp.full((1, size), -1.0, F32)
    landing = jnp.full((1, size), -1.0, F32)
    offset = jnp.zeros((1, 1), F32)
    for way in range(4):
        column = jnp.where(masks[way : way + 1] > 0.5, way * MOVE + ranks[way : way + 1], column)
        ahead = hole - offset
        here = gone & (ahead >= 0.0) & (ahead < counts[way : way + 1])
        landing = jnp.where(here, way * MOVE + ahead, landing)
        offset = offset + counts[way : way + 1]
    spots = one_hot_rows(column.astype(I32), 0, 4 * MOVE)
    element = iota((8, size), 1)
    parts = jnp.where(iota((8, size), 0) == 0, element >> 4, element & 15)
    found = dot_nt(parts.astype(BF16), spots)
    source = found[0:1] * 16.0 + found[1:2]
    return source.astype(I32), landing.astype(I32)


def pack_metric_kernel(place, owner, metric, *refs):
    source_ref, landing_ref = refs[0], refs[1]
    outs = refs[2:]
    step = pl.program_id(0)

    @pl.when(step == 0)
    def _():
        source, landing = move_plan(owner[...], place)
        source_ref[...] = source
        landing_ref[...] = landing

    values = metric[...]
    source = source_ref[...]
    start = 0
    packed = []
    for pair in range(2):
        picked = pick_columns(values, source[:, pair * LANES : (pair + 1) * LANES])
        packed.extend(pack_pair(picked))
    for number, count in enumerate(CHUNKS):

        @pl.when((step >= start) & (step < start + count))
        def _(number=number):
            for way in range(4):
                outs[number * 4 + way][...] = packed[way]

        start += count


def pack_metric(place, owner, metric_rows):
    rows, size = metric_rows.shape
    total = sum(CHUNKS)
    block = rows // total
    half = block // 2
    whole = lambda g: (0, 0)
    out_shape = [
        jax.ShapeDtypeStruct((1, 4 * MOVE), I32),
        jax.ShapeDtypeStruct((1, size), I32),
    ]
    out_specs = [pl.BlockSpec((1, 4 * MOVE), whole), pl.BlockSpec((1, size), whole)]
    start = 0
    for count in CHUNKS:
        for way in range(4):
            out_shape.append(jax.ShapeDtypeStruct((count * half, LANES), F32))
            out_specs.append(
                pl.BlockSpec(
                    (half, LANES),
                    lambda g, start=start, count=count: (jnp.clip(g - start, 0, count - 1), 0),
                )
            )
        start += count
    return pl.pallas_call(
        pack_metric_kernel,
        grid=(total,),
        in_specs=[
            pl.BlockSpec(memory_space=pltpu.SMEM),
            pl.BlockSpec((1, size), whole),
            pl.BlockSpec((block, size), lambda g: (g, 0)),
        ],
        out_specs=out_specs,
        out_shape=out_shape,
        name="pack_metric",
        cost_estimate=pl.CostEstimate(flops=10**6, bytes_accessed=11 * 10**6, transcendentals=0),
        compiler_params=pltpu.CompilerParams(vmem_limit_bytes=24 << 20),
    )(place, owner, metric_rows)


def land(values, landing_row, pairs):
    rows, size = values.shape
    out = []
    for c in range(0, size, LANES):
        spot = jnp.broadcast_to(landing_row[:, c : c + LANES], (rows, LANES))
        got = gather_tiles(pairs, spot & (LANES - 1), spot >> 7)
        out.append(jnp.where(spot < 0, values[:, c : c + LANES], got))
    return jnp.concatenate(out, axis=1)


def land_kernel(landing, values, first, second, third, fourth, *rest):
    pairs = [unpack_pair(first[...], second[...]), unpack_pair(third[...], fourth[...])]
    rest[-1][...] = land(values[...], landing[...], pairs)


def land_rows(landing, values, arrived, block, start, count, before, name):
    rows, size = values.shape
    half = block // 2
    arrival = pl.BlockSpec((half, LANES), lambda g: (g, 0))
    in_specs = [
        pl.BlockSpec((1, size), lambda g: (0, 0)),
        pl.BlockSpec((block, size), lambda g: (g + start, 0)),
    ] + [arrival] * 4
    operands = [landing, values, *arrived]
    aliases = {}
    if before is not None:
        in_specs.append(pl.BlockSpec(memory_space=pl.ANY))
        operands.append(before)
        aliases = {6: 0}
    return pl.pallas_call(
        land_kernel,
        grid=(count,),
        in_specs=in_specs,
        out_specs=pl.BlockSpec((block, size), lambda g: (g + start, 0)),
        out_shape=jax.ShapeDtypeStruct((rows, size), F32),
        input_output_aliases=aliases,
        name=name,
        cost_estimate=pl.CostEstimate(
            flops=10**6, bytes_accessed=count * block * size * 10, transcendentals=0
        ),
        compiler_params=pltpu.CompilerParams(vmem_limit_bytes=24 << 20),
    )(*operands)


FACE_DOM = EY * EZ
FACE_SUB = EX * EZ
EDGE_DOM = EZ * (4 * EY - 1)
EDGE_SUB = EZ * (4 * EX - 1)
CORNER_DOM = EZ * (4 * EY - 2)
CORNER_SUB = EZ * (4 * EX - 2)


def up(count):
    return -(-count // LANES) * LANES


def table_starts(hosted):
    faces = (0, hosted[0], hosted[0] + up(FACE_DOM), hosted[0] + up(FACE_DOM) + up(FACE_SUB))
    edges = (0, hosted[1], hosted[1] + up(EDGE_DOM), hosted[1] + up(EDGE_DOM) + up(EDGE_SUB))
    corners = (
        0,
        hosted[2],
        hosted[2] + up(CORNER_DOM),
        hosted[2] + up(CORNER_DOM) + up(CORNER_SUB),
    )
    return (faces, edges, corners)


KINDS = (6, 12, 8)
FACE_ROWS = 2 * INNER * 8
EDGE_ROWS = 16
CORNER_ROWS = 4


def shared_columns(ids, place, hosted):
    lines, size = ids.shape
    line = iota((lines, 1), 0)
    per = jnp.where(line < 6, hosted[0], jnp.where(line < 18, hosted[1], hosted[2]))
    owns, rows, masks = [], jnp.zeros((lines, size), I32), []
    for device in (place[4], place[1], place[3], place[5]):
        local = ids - device * per
        inside = (local >= 0) & (local < per)
        rows = jnp.where(inside, local, rows)
        owns.append(inside)
    starts = table_starts(hosted)
    lower = (iota((lines, lines), 1) < iota((lines, lines), 0)) & (
        (iota((lines, lines), 0) < 6) == (iota((lines, lines), 1) < 6)
    )
    lower = lower & ((iota((lines, lines), 0) < 18) == (iota((lines, lines), 1) < 18))
    lower = jnp.where(lower, 1.0, 0.0).astype(BF16)
    column = rows
    marks = jnp.concatenate([jnp.where(inside, 1.0, 0.0) for inside in owns[1:]], axis=0)
    ranks = exclusive_count(marks)
    for number in range(3):
        inside = owns[1 + number]
        mark = marks[number * lines : (number + 1) * lines]
        above = jnp.sum(dot(lower, mark.astype(BF16)), axis=1, keepdims=True)
        rank = (ranks[number * lines : (number + 1) * lines] + above).astype(I32)
        base = jnp.where(
            line < 6,
            starts[0][1 + number],
            jnp.where(line < 18, starts[1][1 + number], starts[2][1 + number]),
        )
        column = jnp.where(inside, base + rank, column)
    return column, rows


def scatter_two(parts, column_row, tiles):
    high, low = split(parts)
    both = jnp.concatenate([high, low], axis=0)
    size = column_row.shape[1]
    tile = jnp.broadcast_to((column_row >> 7).astype(BF16), both.shape)
    zero = jnp.zeros(both.shape, BF16)
    left = jnp.concatenate([jnp.where(tile == h, both, zero) for h in range(tiles)], axis=0)
    return dot_nt(left, one_hot_rows(column_row & (LANES - 1), 0, LANES))


def face_rows(face, inner):
    end = 7 * (face % 2)
    if face < 2:
        return pl.ds(end * 64 + inner * 8, 8)
    if face < 4:
        return pl.ds(inner * 64 + end * 8, 8)
    return pl.ds(inner * 64 + end, 8, stride=8)


def all_lanes(ref, rows):
    return jnp.concatenate([ref[c, rows, :] for c in range(ref.shape[0])], axis=1)


def face_nodes(ref, face):
    return jnp.concatenate(
        [all_lanes(ref, face_rows(face, inner)) for inner in range(1, INNER + 1)], axis=0
    )


def edge_place(edge):
    ends = (7 * (edge % 4 // 2), 7 * (edge % 2))
    if edge < 4:
        return ends[0] * 8 + ends[1], 64
    if edge < 8:
        return ends[0] * 64 + ends[1], 8
    return ends[0] * 64 + ends[1] * 8, 1


def edge_rows(edge):
    start, stride = edge_place(edge)
    return pl.ds(start, 8) if stride == 1 else pl.ds(start, 8, stride=stride)


def corner_place(corner):
    return (corner // 4) * 448 + (corner // 2 % 2) * 56 + (corner % 2) * 7


def apply_kernel(
    place,
    ids,
    solution,
    metric,
    grad_left,
    image_left,
    square_left,
    after,
    image_ref,
    diagonal_ref,
    column_ref,
    face_table,
    edge_table,
    corner_table,
    dom_out,
    sub_out,
    both_out,
    flux_r,
    *,
    table,
):
    del after
    step = pl.program_id(0)
    width = solution.shape[1]
    size = image_ref.shape[0] * LANES
    tiles_here = width // LANES

    def write(ref, rows, values, add=False):
        for c in range(tiles_here):
            tile = step * tiles_here + c
            part = values[:, c * LANES : (c + 1) * LANES]
            ref[tile, rows, :] = ref[tile, rows, :] + part if add else part

    count = table.shape[0]
    plane = count * count

    field = [solution[i * plane : (i + 1) * plane, :] for i in range(count)]
    node = iota((count, width), 0)
    ends = (0, count - 1)
    end_value = {0: float(table[0, 0]), count - 1: float(table[count - 1, count - 1])}
    ends_k = jnp.where(
        node == 0, end_value[0], jnp.where(node == count - 1, end_value[count - 1], 0.0)
    )
    for i in range(count):
        rows = slice(i * plane, (i + 1) * plane)
        part = [metric[c * count * plane + i * plane : c * count * plane + (i + 1) * plane, :] for c in range(7)]
        grad_r = sum(float(table[i, s]) * field[s] for s in range(count))
        grads = dot(grad_left[...], triple(field[i]))
        grad_s, grad_t = grads[:plane], grads[plane:]
        flux_r[rows, :] = part[0] * grad_r + part[3] * grad_s + part[4] * grad_t
        flux_s = part[3] * grad_r + part[1] * grad_s + part[5] * grad_t
        flux_t = part[4] * grad_r + part[5] * grad_s + part[2] * grad_t
        image = dot(image_left[...], triple(jnp.concatenate([flux_s, flux_t], axis=0)))
        write(image_ref, rows, image + part[6] * field[i])
        diagonal = dot(square_left[...], triple(jnp.concatenate([part[1], part[2]], axis=0)))
        diagonal = diagonal + part[6]
        cross = []
        for j in range(count):
            lines = slice(j * count, (j + 1) * count)
            term = None
            if j in ends:
                term = part[5][lines] * (ends_k * (2.0 * end_value[j]))
            if i in ends:
                extra = part[4][lines] * (ends_k * (2.0 * end_value[i]))
                if j in ends:
                    extra = extra + part[3][lines] * (2.0 * end_value[i] * end_value[j])
                term = extra if term is None else term + extra
            cross.append(diagonal[lines] if term is None else diagonal[lines] + term)
        write(diagonal_ref, rows, jnp.concatenate(cross, axis=0))
    for i in range(count):
        rows = slice(i * plane, (i + 1) * plane)
        more = sum(float(table[a, i]) * flux_r[a * plane : (a + 1) * plane, :] for a in range(count))
        write(image_ref, rows, more, add=True)
        square = sum(
            float(table[a, i] * table[a, i]) * metric[a * plane : (a + 1) * plane, :]
            for a in range(count)
        )
        write(diagonal_ref, rows, square, add=True)

    @pl.when(step == pl.num_programs(0) - 1)
    def _():
        hosted = (3 * size, 3 * size, size)
        starts = table_starts(hosted)
        column, row = shared_columns(ids[...], place, hosted)
        column_ref[...] = column
        row_high = (row >> 4).astype(F32)
        row_low = (row & 15).astype(F32)
        face_parts = []
        spot = iota((48, size), 0)
        for face in range(6):
            values = face_nodes(image_ref, face)
            values = jnp.where(spot == 0, row_high[face : face + 1], values)
            values = jnp.where(spot == 7, row_low[face : face + 1], values)
            values = jnp.concatenate([values, face_nodes(diagonal_ref, face)], axis=0)
            face_parts.append(jnp.concatenate(split(values), axis=0))
        faces_end = starts[0][3]
        for base in range(0, faces_end, 2 * LANES):
            total = None
            for face in range(6):
                more = dot_nt(
                    face_parts[face], one_hot_rows(column[face : face + 1], base, 2 * LANES)
                )
                total = more if total is None else total + more
            total = total[:FACE_ROWS] + total[FACE_ROWS:]
            for side in range(2):
                tile = total[:, side * LANES : (side + 1) * LANES]
                place_column = base + side * LANES
                if place_column < starts[0][1]:
                    face_table[:, place_column : place_column + LANES] = tile
                elif place_column < starts[0][2]:
                    dom_out[0:FACE_ROWS, :] = tile
                else:
                    sub_out[0:FACE_ROWS, :] = tile
        tiles = (starts[1][3] + LANES) // LANES
        total = None
        line = iota((8, size), 0)
        for edge in range(12):
            values = all_lanes(image_ref, edge_rows(edge))
            values = jnp.where(line == 0, row_high[6 + edge : 7 + edge], values)
            values = jnp.where(line == 7, row_low[6 + edge : 7 + edge], values)
            values = jnp.concatenate([values, all_lanes(diagonal_ref, edge_rows(edge))], axis=0)
            more = scatter_two(values, column[6 + edge : 7 + edge], tiles)
            total = more if total is None else total + more
        for number in range(tiles):
            first = number * 2 * EDGE_ROWS
            tile = total[first : first + EDGE_ROWS] + total[first + EDGE_ROWS : first + 2 * EDGE_ROWS]
            place_column = number * LANES
            if place_column < starts[1][1]:
                edge_table[:, place_column : place_column + LANES] = tile
            elif place_column < starts[1][2]:
                base = FACE_ROWS + (place_column - starts[1][1]) // LANES * EDGE_ROWS
                dom_out[base : base + EDGE_ROWS, :] = tile
            elif place_column < starts[1][3]:
                base = FACE_ROWS + (place_column - starts[1][2]) // LANES * EDGE_ROWS
                sub_out[base : base + EDGE_ROWS, :] = tile
            else:
                both_out[0:EDGE_ROWS, :] = tile
        tiles = (starts[2][3] + LANES) // LANES
        total = None
        for corner in range(8):
            at = corner_place(corner)
            values = jnp.concatenate(
                [
                    all_lanes(image_ref, slice(at, at + 1)),
                    all_lanes(diagonal_ref, slice(at, at + 1)),
                    row_high[18 + corner : 19 + corner],
                    row_low[18 + corner : 19 + corner],
                    jnp.zeros((4, size), F32),
                ],
                axis=0,
            )
            more = scatter_two(values, column[18 + corner : 19 + corner], tiles)
            total = more if total is None else total + more
        for number in range(tiles):
            tile = total[number * 16 : number * 16 + 8] + total[number * 16 + 8 : number * 16 + 16]
            place_column = number * LANES
            if place_column < starts[2][1]:
                corner_table[:, place_column : place_column + LANES] = tile
            elif place_column < starts[2][2]:
                base = CORNER_BASE + (place_column - starts[2][1]) // LANES * CORNER_ROWS
                dom_out[base : base + CORNER_ROWS, :] = tile[:CORNER_ROWS]
            elif place_column < starts[2][3]:
                base = CORNER_BASE + (place_column - starts[2][2]) // LANES * CORNER_ROWS
                sub_out[base : base + CORNER_ROWS, :] = tile[:CORNER_ROWS]
            else:
                both_out[EDGE_ROWS : EDGE_ROWS + 8, :] = tile


EDGE_TILES = up(EDGE_DOM) // LANES
CORNER_TILES = up(CORNER_DOM) // LANES
CORNER_BASE = FACE_ROWS + EDGE_TILES * EDGE_ROWS
MESSAGE_ROWS = CORNER_BASE + CORNER_TILES * CORNER_ROWS
BOTH_ROWS = EDGE_ROWS + 8


def apply_and_pack(place, ids, field, metric_rows, after, table):
    nodes, size = field.shape
    width = size // 2
    count = table.shape[0]
    eye = np.eye(count, dtype=np.float32)
    grad = np.concatenate([np.kron(table, eye), np.kron(eye, table)], axis=0)
    square = (table * table).astype(np.float32)
    squares = np.concatenate([np.kron(square, eye), np.kron(eye, square)], axis=0)
    lefts = [split_np(grad), split_np(grad.T), split_np(squares.T)]
    whole = lambda g: (0, 0)

    def out(*shape, dtype=F32):
        return jax.ShapeDtypeStruct(shape, dtype), pl.BlockSpec(shape, lambda g: (0,) * len(shape))

    outs = [
        out(size // LANES, nodes, LANES),
        out(size // LANES, nodes, LANES),
        out(sum(KINDS), size, dtype=I32),
        out(FACE_ROWS, 3 * size),
        out(EDGE_ROWS, 3 * size),
        out(8, size),
        out(MESSAGE_ROWS, LANES),
        out(MESSAGE_ROWS, LANES),
        out(BOTH_ROWS, LANES),
    ]
    return pl.pallas_call(
        functools.partial(apply_kernel, table=table),
        grid=(size // width,),
        in_specs=[
            pl.BlockSpec(memory_space=pltpu.SMEM),
            pl.BlockSpec(ids.shape, whole),
            pl.BlockSpec((nodes, width), lambda g: (0, g)),
            pl.BlockSpec((metric_rows.shape[0], width), lambda g: (0, g)),
        ]
        + [pl.BlockSpec(left.shape, whole) for left in lefts]
        + [pl.BlockSpec(memory_space=pl.ANY)],
        out_specs=[spec for _, spec in outs],
        out_shape=[shape for shape, _ in outs],
        scratch_shapes=[pltpu.VMEM((nodes, width), F32)],
        name="apply_and_pack",
        cost_estimate=pl.CostEstimate(flops=10**9, bytes_accessed=12 * 10**6, transcendentals=0),
        compiler_params=pltpu.CompilerParams(vmem_limit_bytes=48 << 20),
    )(place, ids, field, metric_rows, *[jnp.asarray(left) for left in lefts], after)


def arrived_rows(high, low):
    return (high * 16.0 + low).astype(I32)


def add_kernel(face_in, edge_in, corner_in, dom, sub, both, faces, edges, corners, dom_back, sub_back, both_back):
    values = jnp.concatenate([dom[0:FACE_ROWS, :], sub[0:FACE_ROWS, :]], axis=1)
    row = arrived_rows(values[0:1], values[7:8])
    parts = jnp.concatenate(split(values), axis=0)
    for base in range(0, faces.shape[1], 2 * LANES):
        more = dot_nt(parts, one_hot_rows(row, base, 2 * LANES))
        faces[:, base : base + 2 * LANES] = (
            face_in[:, base : base + 2 * LANES] + more[:FACE_ROWS] + more[FACE_ROWS:]
        )
    tiles = [faces[:, c : c + LANES] for c in range(0, faces.shape[1], LANES)]
    for side, back in enumerate((dom_back, sub_back)):
        spot = jnp.broadcast_to(row[:, side * LANES : (side + 1) * LANES], (FACE_ROWS, LANES))
        back[0:FACE_ROWS, :] = gather_tiles(tiles, spot & (LANES - 1), spot >> 7)
    places = [(ref, FACE_ROWS + q * EDGE_ROWS) for ref in (dom, sub) for q in range(EDGE_TILES)]
    places.append((both, 0))
    values = jnp.concatenate([ref[at : at + EDGE_ROWS, :] for ref, at in places], axis=1)
    row = arrived_rows(values[0:1], values[7:8])
    count = edges.shape[1] // LANES
    total = scatter_two(values, row, count)
    tiles = []
    for number in range(count):
        first = number * 2 * EDGE_ROWS
        tile = total[first : first + EDGE_ROWS] + total[first + EDGE_ROWS : first + 2 * EDGE_ROWS]
        tile = tile + edge_in[:, number * LANES : (number + 1) * LANES]
        edges[:, number * LANES : (number + 1) * LANES] = tile
        tiles.append(tile)
    backs = {id(dom): dom_back, id(sub): sub_back, id(both): both_back}
    for number, (ref, at) in enumerate(places):
        spot = jnp.broadcast_to(
            row[:, number * LANES : (number + 1) * LANES], (EDGE_ROWS, LANES)
        )
        backs[id(ref)][at : at + EDGE_ROWS, :] = gather_tiles(tiles, spot & (LANES - 1), spot >> 7)
    places = [(ref, CORNER_BASE + q * CORNER_ROWS) for ref in (dom, sub) for q in range(CORNER_TILES)]
    places.append((both, EDGE_ROWS))
    values = jnp.concatenate([ref[at : at + CORNER_ROWS, :] for ref, at in places], axis=1)
    values = jnp.concatenate([values, jnp.zeros_like(values)], axis=0)
    row = arrived_rows(values[2:3], values[3:4])
    count = corners.shape[1] // LANES
    total = scatter_two(values, row, count)
    tiles = []
    for number in range(count):
        tile = total[number * 16 : number * 16 + 8] + total[number * 16 + 8 : number * 16 + 16]
        tile = tile + corner_in[:, number * LANES : (number + 1) * LANES]
        corners[:, number * LANES : (number + 1) * LANES] = tile
        tiles.append(tile)
    for number, (ref, at) in enumerate(places):
        spot = jnp.broadcast_to(row[:, number * LANES : (number + 1) * LANES], (8, LANES))
        got = gather_tiles(tiles, spot & (LANES - 1), spot >> 7)
        backs[id(ref)][at : at + CORNER_ROWS, :] = got[:CORNER_ROWS]


def add_and_read(faces, edges, corners, dom, sub, both):
    shapes = [faces, edges, corners, dom, sub, both]
    return pl.pallas_call(
        add_kernel,
        in_specs=[VMEM] * 6,
        out_specs=[VMEM] * 6,
        out_shape=[jax.ShapeDtypeStruct(a.shape, F32) for a in shapes],
        name="add_and_read",
        cost_estimate=pl.CostEstimate(flops=10**8, bytes_accessed=2 * 10**6, transcendentals=0),
        compiler_params=pltpu.CompilerParams(vmem_limit_bytes=24 << 20),
    )(*shapes)


def relax_kernel(
    column_ref, faces, edges, corners, dom, sub, both, image, diagonal, field, forcing, source,
    relaxed, *rest,
):
    size = relaxed.shape[1]
    *outs, full_image, full_diagonal = rest
    full_image[...] = image[...]
    full_diagonal[...] = diagonal[...]

    def spots(line, rows, c):
        spot = jnp.broadcast_to(column_ref[line : line + 1, c : c + LANES], (rows, LANES))
        return spot & (LANES - 1), spot >> 7

    def put(ref, c, rows, values):
        ref[c, rows, :] = jnp.where(inside, values, ref[c, rows, :])

    tiles = [faces[:, c : c + LANES] for c in range(0, faces.shape[1], LANES)]
    tiles += [dom[0:FACE_ROWS, :], sub[0:FACE_ROWS, :]]
    line = iota((8, LANES), 0)
    inside = (line > 0) & (line < 7)
    for c in range(0, size, LANES):
        for face in range(6):
            low, high = spots(face, FACE_ROWS, c)
            got = gather_tiles(tiles, low, high)
            for number in range(INNER):
                rows = face_rows(face, number + 1)
                put(full_image, c // LANES, rows, got[number * 8 : number * 8 + 8])
                put(full_diagonal, c // LANES, rows, got[48 + number * 8 : 56 + number * 8])
    tiles = [edges[:, c : c + LANES] for c in range(0, edges.shape[1], LANES)]
    for ref in (dom, sub):
        tiles += [
            ref[FACE_ROWS + q * EDGE_ROWS : FACE_ROWS + (q + 1) * EDGE_ROWS, :]
            for q in range(EDGE_TILES)
        ]
    tiles.append(both[0:EDGE_ROWS, :])
    for c in range(0, size, LANES):
        for edge in range(12):
            low, high = spots(6 + edge, EDGE_ROWS, c)
            got = gather_tiles(tiles, low, high)
            put(full_image, c // LANES, edge_rows(edge), got[:8])
            put(full_diagonal, c // LANES, edge_rows(edge), got[8:])
    tiles = [corners[0:8, c : c + LANES] for c in range(0, corners.shape[1], LANES)]
    for ref in (dom, sub):
        tiles += [
            ref[CORNER_BASE + q * CORNER_ROWS : CORNER_BASE + (q + 1) * CORNER_ROWS, :]
            for q in range(CORNER_TILES)
        ]
    tiles.append(both[EDGE_ROWS : EDGE_ROWS + 8, :])
    tiles = [jnp.concatenate([t[0:2]] * 4, axis=0) for t in tiles]
    for c in range(0, size, LANES):
        lanes = slice(c, c + LANES)
        for group in range(2):
            spot = jnp.concatenate(
                [
                    jnp.broadcast_to(column_ref[n : n + 1, lanes], (2, LANES))
                    for n in range(18 + group * 4, 22 + group * 4)
                ],
                axis=0,
            )
            got = gather_tiles(tiles, spot & (LANES - 1), spot >> 7)
            for number in range(4):
                at = corner_place(group * 4 + number)
                full_image[c // LANES, at : at + 1, :] = got[2 * number : 2 * number + 1]
                full_diagonal[c // LANES, at : at + 1, :] = got[2 * number + 1 : 2 * number + 2]
    for c in range(0, size, LANES):
        lanes = slice(c, c + LANES)
        step = (forcing[:, lanes] - full_image[c // LANES]) / full_diagonal[c // LANES]
        relaxed[:, lanes] = field[:, lanes] + RELAX * step
    for pair in range(2):
        picked = pick_columns(relaxed[...], source[:, pair * LANES : (pair + 1) * LANES])
        first, second = pack_pair(picked)
        outs[2 * pair][...] = first
        outs[2 * pair + 1][...] = second


def relax_and_pack(column, faces, edges, corners, dom, sub, both, image, diagonal, field, forcing, source):
    nodes, size = field.shape
    message = jax.ShapeDtypeStruct((nodes // 2, LANES), F32)
    return pl.pallas_call(
        relax_kernel,
        in_specs=[VMEM] * 12,
        out_specs=[VMEM] * 5,
        out_shape=[jax.ShapeDtypeStruct((nodes, size), F32)] + [message] * 4,
        scratch_shapes=[pltpu.VMEM((size // LANES, nodes, LANES), F32)] * 2,
        name="relax_and_pack",
        cost_estimate=pl.CostEstimate(flops=10**7, bytes_accessed=10**7, transcendentals=0),
        compiler_params=pltpu.CompilerParams(vmem_limit_bytes=32 << 20),
    )(column, faces, edges, corners, dom, sub, both, image, diagonal, field, forcing, source)


def shifted(value, dom_steps, sub_steps):
    dom_count = lax.axis_size("dom")
    sub_count = lax.axis_size("sub")
    if sub_steps == 0:
        pairs = [(d, (d + dom_steps) % dom_count) for d in range(dom_count)]
        return lax.ppermute(value, "dom", pairs)
    if dom_steps == 0:
        pairs = [(s, (s + sub_steps) % sub_count) for s in range(sub_count)]
        return lax.ppermute(value, "sub", pairs)
    pairs = [
        (
            d * sub_count + s,
            (d + dom_steps) % dom_count * sub_count + (s + sub_steps) % sub_count,
        )
        for d in range(dom_count)
        for s in range(sub_count)
    ]
    return lax.ppermute(value, ("dom", "sub"), pairs)


def exchanged(messages):
    to_prev_dom, to_next_dom, to_prev_sub, to_next_sub = messages
    from_prev_sub = shifted(to_next_sub, 0, 1)
    from_next_sub = shifted(to_prev_sub, 0, -1)
    from_prev_dom = shifted(to_next_dom, 1, 0)
    from_next_dom = shifted(to_prev_dom, -1, 0)
    return (from_prev_dom, from_next_dom, from_prev_sub, from_next_sub)


def on_device(solution, forcing, metric, entity_ids, new_owner):
    size = solution.shape[-1]
    place = devices()
    table = derivative_table(solution.shape[0] - 1)
    field = solution.reshape(-1, size)
    metric_rows = metric.reshape(-1, size)
    components = metric.shape[0]
    block = metric_rows.shape[0] // components
    source, landing, *messages = pack_metric(place, new_owner.reshape(1, size), metric_rows)
    arrived = [exchanged(messages[4 * n : 4 * n + 4]) for n in range(len(CHUNKS))]

    image, diagonal, column, faces, edges, corners, dom, sub, both = apply_and_pack(
        place, entity_ids, field, metric_rows, landing, table
    )
    both = shifted(both, 1, 1)
    sub = shifted(sub, 0, 1)
    dom = shifted(dom, 1, 0)
    faces, edges, corners, dom, sub, both = add_and_read(faces, edges, corners, dom, sub, both)
    both = shifted(both, -1, -1)
    sub = shifted(sub, 0, -1)
    dom = shifted(dom, -1, 0)
    relaxed, *leaving = relax_and_pack(
        column, faces, edges, corners, dom, sub, both, image, diagonal,
        field, forcing.reshape(-1, size), source,
    )
    got = exchanged(leaving)
    moved, start = None, 0
    for count, part in zip(CHUNKS, arrived):
        moved = land_rows(landing, metric_rows, part, block, start, count, moved, "land_metric")
        start += count
    smoothed = land_rows(landing, relaxed, got, block, 0, 1, None, "land_field")
    return smoothed.reshape(solution.shape), moved.reshape(metric.shape)


def solution(mesh):
    placed = (
        P(None, None, None, ("dom", "sub")),
        P(None, None, None, ("dom", "sub")),
        P(None, None, None, None, ("dom", "sub")),
        P(None, ("dom", "sub")),
        P(("dom", "sub")),
    )
    return jax.shard_map(
        on_device,
        mesh=mesh,
        in_specs=placed,
        out_specs=(P(None, None, None, ("dom", "sub")), P(None, None, None, None, ("dom", "sub"))),
        check_vma=False,
    )
```

```python
import functools

import jax
import jax.numpy as jnp
import numpy as np
from jax import lax
from jax.experimental import pallas as pl
from jax.experimental.pallas import tpu as pltpu
from jax.sharding import PartitionSpec as P

EX = 4
EY = 4
EZ = 32
MOVE = 64
RELAX = 0.6
LANES = 128
INNER = 6
EARLY = 4

NT = (((1,), (1,)), ((), ()))
VMEM = pl.BlockSpec(memory_space=pltpu.VMEM)
ANY = pl.BlockSpec(memory_space=pl.ANY)
SMEM = pl.BlockSpec(memory_space=pltpu.SMEM)
QUICK = pl.CostEstimate(flops=1000, bytes_accessed=1000, transcendentals=0)
HBM = pl.BlockSpec(memory_space=pltpu.HBM)
LARGE = pltpu.CompilerParams(vmem_limit_bytes=24 << 20)
SMALL = pltpu.CompilerParams(vmem_limit_bytes=16 << 20)
STRIP = 64
F32 = jnp.float32
BF16 = jnp.bfloat16
I32 = jnp.int32


def derivative_table(order):
    count = order + 1
    points = -np.cos(np.pi * np.arange(count) / order)
    legendre = np.zeros((count, count))
    for sweep in range(80):
        legendre[:, 0] = 1.0
        legendre[:, 1] = points
        for degree in range(2, count):
            legendre[:, degree] = (
                (2 * degree - 1) * points * legendre[:, degree - 1]
                - (degree - 1) * legendre[:, degree - 2]
            ) / degree
        points = points - (points * legendre[:, order] - legendre[:, order - 1]) / (
            count * legendre[:, order]
        )
    legendre[:, 0] = 1.0
    legendre[:, 1] = points
    for degree in range(2, count):
        legendre[:, degree] = (
            (2 * degree - 1) * points * legendre[:, degree - 1]
            - (degree - 1) * legendre[:, degree - 2]
        ) / degree
    values = legendre[:, order]
    identity = np.eye(count)
    spread = points[:, None] - points[None, :] + identity
    table = values[:, None] / values[None, :] / spread
    table = table * (1.0 - identity)
    table[0, 0] = -order * count / 4.0
    table[order, order] = order * count / 4.0
    return table.astype(np.float32)


def split_np(matrix):
    high = matrix.astype(jnp.bfloat16).astype(np.float32)
    low = (matrix - high).astype(jnp.bfloat16)
    return np.concatenate([high.astype(jnp.bfloat16), low, high.astype(jnp.bfloat16)], axis=1)


def split(values):
    high = values.astype(BF16)
    low = (values - high.astype(F32)).astype(BF16)
    return high, low


def triple(values):
    high, low = split(values)
    return jnp.concatenate([high, high, low], axis=0)


def dot(left, right):
    return jnp.dot(left, right, preferred_element_type=F32)


def dot_nt(left, right):
    return lax.dot_general(left, right, NT, preferred_element_type=F32)


def iota(shape, dim):
    return lax.broadcasted_iota(I32, shape, dim)


def one_hot_rows(index_row, start, count):
    size = index_row.shape[1]
    out = []
    for base in range(0, count, LANES):
        local = (index_row - (start + base)).astype(BF16)
        rows = iota((LANES, size), 0).astype(BF16)
        out.append(
            jnp.where(rows == local, jnp.ones((LANES, size), BF16), jnp.zeros((LANES, size), BF16))
        )
    return out[0] if len(out) == 1 else jnp.concatenate(out, axis=0)


def exclusive_count(masks):
    size = masks.shape[1]
    upper = jnp.where(iota((size, size), 0) < iota((size, size), 1), 1.0, 0.0).astype(BF16)
    return dot(masks.astype(BF16), upper)


def gather_tiles(tiles, low, high):
    out = None
    for number, tile in enumerate(tiles):
        got = jnp.take_along_axis(tile, low, axis=1)
        out = got if out is None else jnp.where(high == number, got, out)
    return out


def devices():
    dom_count = lax.axis_size("dom")
    sub_count = lax.axis_size("sub")
    dom = lax.axis_index("dom")
    sub = lax.axis_index("sub")
    dom_ahead = lax.rem(dom + 1, dom_count)
    dom_behind = lax.rem(dom + dom_count - 1, dom_count)
    sub_ahead = lax.rem(sub + 1, sub_count)
    sub_behind = lax.rem(sub + sub_count - 1, sub_count)
    return jnp.stack(
        [
            dom_behind * sub_count + sub,
            dom_ahead * sub_count + sub,
            dom * sub_count + sub_behind,
            dom * sub_count + sub_ahead,
            dom * sub_count + sub,
            dom_ahead * sub_count + sub_ahead,
        ]
    ).astype(I32)


def pack_pair(top, bottom):
    left = iota(top.shape, 1) < MOVE
    first = jnp.where(left, top, pltpu.roll(bottom, MOVE, 1))
    second = jnp.where(left, pltpu.roll(top, MOVE, 1), bottom)
    return first, second


def pick_columns(ref, rows, low, high):
    tiles = [ref[rows, c : c + LANES] for c in range(0, ref.shape[1], LANES)]
    return gather_tiles(tiles, low, high)


def pack_block(ref, start, block, source_row, outs, to):
    half = block // 2
    source = jnp.broadcast_to(source_row, (STRIP, LANES))
    low, high = source & (LANES - 1), source >> 7
    for row in range(0, half, STRIP):
        top = pick_columns(ref, slice(start + row, start + row + STRIP), low, high)
        bottom = pick_columns(ref, slice(start + half + row, start + half + row + STRIP), low, high)
        for out, message in zip(outs, pack_pair(top, bottom)):
            out[to + row : to + row + STRIP, :] = message


def land_block(ref, start, block, landing_row, messages, at, out, to):
    half = block // 2
    size = ref.shape[1]
    spots = []
    for c in range(0, size, LANES):
        spot = jnp.broadcast_to(landing_row[:, c : c + LANES], (STRIP, LANES))
        spots.append((spot < 0, spot & (LANES - 1), spot >> 7))
    for row in range(0, half, STRIP):
        parts = [message[at + row : at + row + STRIP, :] for message in messages]
        pairs = [pack_pair(parts[0], parts[1]), pack_pair(parts[2], parts[3])]
        for side in range(2):
            tiles = [pair[side] for pair in pairs]
            first = start + side * half + row
            last = to + side * half + row
            for number, (stays, low, high) in enumerate(spots):
                lanes = slice(number * LANES, (number + 1) * LANES)
                got = gather_tiles(tiles, low, high)
                out[last : last + STRIP, lanes] = jnp.where(
                    stays, ref[first : first + STRIP, lanes], got
                )


def move_plan(owner, place):
    size = owner.shape[1]
    own = place[4]
    line = iota((8, size), 0)
    target = jnp.where(
        line == 0,
        place[0],
        jnp.where(line == 1, place[1], jnp.where(line == 2, place[2], place[3])),
    )
    nobody = jnp.broadcast_to(owner, (8, size))
    away = nobody != own
    masks = jnp.where(away & (((nobody == target) & (line < 4)) | (line == 4)), 1.0, 0.0)
    ranks = exclusive_count(masks)
    counts = jnp.sum(masks, axis=1, keepdims=True)
    hole = ranks[4:5]
    gone = masks[4:5] > 0.5
    column = jnp.full((1, size), -1.0, F32)
    landing = jnp.full((1, size), -1.0, F32)
    offset = jnp.zeros((1, 1), F32)
    for way in range(4):
        column = jnp.where(masks[way : way + 1] > 0.5, way * MOVE + ranks[way : way + 1], column)
        ahead = hole - offset
        here = gone & (ahead >= 0.0) & (ahead < counts[way : way + 1])
        landing = jnp.where(here, way * MOVE + ahead, landing)
        offset = offset + counts[way : way + 1]
    spots = one_hot_rows(column.astype(I32), 0, 4 * MOVE)
    element = iota((8, size), 1)
    parts = jnp.where(iota((8, size), 0) == 0, element >> 4, element & 15)
    found = dot_nt(parts.astype(BF16), spots)
    source = found[0:1] * 16.0 + found[1:2]
    return source.astype(I32), landing.astype(I32)


def fetch(source, target, sems, number, start, count, to):
    return pltpu.make_async_copy(
        source.at[pl.ds(start, count), :], target.at[pl.ds(to, count), :], sems.at[number]
    )


def send_parts(metric, first, source, outs, held, sems, block):
    half = block // 2
    for number in range(held.shape[0] // block):
        fetch(metric, held, sems, number, (first + number) * block, block, number * block).wait()
        pack_block(held, number * block, block, source, outs, number * half)


def fetch_parts(metric, first, held, sems, block):
    for number in range(held.shape[0] // block):
        fetch(metric, held, sems, number, (first + number) * block, block, number * block).start()


def plan_and_pack_kernel(place, owner, metric, source_ref, landing_ref, *rest, block):
    *outs, held, sems = rest
    fetch_parts(metric, 0, held, sems, block)
    source, landing = move_plan(owner[...], place)
    source_ref[...] = source
    landing_ref[...] = landing
    send_parts(metric, 0, source[:, LANES:], outs, held, sems, block)


def pack_kernel(source, metric, after, *rest, first, pair, block):
    del after
    *outs, held, sems = rest
    fetch_parts(metric, first, held, sems, block)
    lanes = slice(pair * LANES, (pair + 1) * LANES)
    send_parts(metric, first, source[:, lanes], outs, held, sems, block)


def sent_shapes(count, block, size):
    outs = [jax.ShapeDtypeStruct((count * block // 2, LANES), F32)] * 2
    scratch = [pltpu.VMEM((count * block, size), F32), pltpu.SemaphoreType.DMA((count,))]
    return outs, scratch


def plan_and_pack(place, owner, metric_rows, block):
    size = metric_rows.shape[1]
    outs, scratch = sent_shapes(EARLY, block, size)
    plan = [jax.ShapeDtypeStruct((1, 4 * MOVE), I32), jax.ShapeDtypeStruct((1, size), I32)]
    return pl.pallas_call(
        functools.partial(plan_and_pack_kernel, block=block),
        in_specs=[SMEM, VMEM, HBM],
        out_specs=[VMEM] * 4,
        out_shape=plan + outs,
        scratch_shapes=scratch,
        name="plan_and_pack",
        cost_estimate=QUICK,
        compiler_params=LARGE,
    )(place, owner, metric_rows)


def pack(source, metric_rows, first, count, pair, block, after, name):
    outs, scratch = sent_shapes(count, block, metric_rows.shape[1])
    return pl.pallas_call(
        functools.partial(pack_kernel, first=first, pair=pair, block=block),
        in_specs=[VMEM, HBM, ANY],
        out_specs=[VMEM] * 2,
        out_shape=outs,
        scratch_shapes=scratch,
        name=name,
        cost_estimate=QUICK,
        compiler_params=LARGE,
    )(source, metric_rows, after)


def land_metric_kernel(landing, metric, *rest, first, block):
    messages = rest[:4]
    out, held, ready, sems, out_sems = rest[-5:]
    count = held.shape[0] // block
    fetch_parts(metric, first, held, sems, block)
    for number in range(count):
        start = number * block
        fetch(metric, held, sems, number, (first + number) * block, block, start).wait()
        land_block(held, start, block, landing[...], messages, start // 2, ready, start)
        fetch(ready, out, out_sems, number, start, block, (first + number) * block).start()
    for number in range(count):
        start = number * block
        fetch(ready, out, out_sems, number, start, block, (first + number) * block).wait()


def land_metric(landing, metric_rows, arrived, first, count, block, before, after, name):
    size = metric_rows.shape[1]
    operands = [landing, metric_rows, *arrived, after]
    specs = [VMEM, HBM] + [VMEM] * 4 + [ANY]
    aliases = {}
    if before is not None:
        operands.append(before)
        specs.append(HBM)
        aliases = {7: 0}
    return pl.pallas_call(
        functools.partial(land_metric_kernel, first=first, block=block),
        in_specs=specs,
        out_specs=HBM,
        out_shape=jax.ShapeDtypeStruct(metric_rows.shape, F32),
        scratch_shapes=[
            pltpu.VMEM((count * block, size), F32),
            pltpu.VMEM((count * block, size), F32),
            pltpu.SemaphoreType.DMA((count,)),
            pltpu.SemaphoreType.DMA((count,)),
        ],
        input_output_aliases=aliases,
        name=name,
        cost_estimate=QUICK,
        compiler_params=LARGE,
    )(*operands)


def land_field_kernel(landing, relaxed, first, second, third, fourth, out):
    rows = relaxed.shape[0]
    land_block(relaxed, 0, rows, landing[...], (first, second, third, fourth), 0, out, 0)


def land_field(landing, relaxed, arrived):
    return pl.pallas_call(
        land_field_kernel,
        in_specs=[VMEM] * 6,
        out_specs=VMEM,
        out_shape=jax.ShapeDtypeStruct(relaxed.shape, F32),
        name="land_field",
        cost_estimate=QUICK,
        compiler_params=SMALL,
    )(landing, relaxed, *arrived)


FACE_DOM = EY * EZ
FACE_SUB = EX * EZ
EDGE_DOM = EZ * (4 * EY - 1)
EDGE_SUB = EZ * (4 * EX - 1)
CORNER_DOM = EZ * (4 * EY - 2)
CORNER_SUB = EZ * (4 * EX - 2)


def up(count):
    return -(-count // LANES) * LANES


EDGE_TILES = up(EDGE_DOM) // LANES
CORNER_TILES = up(CORNER_DOM) // LANES


def table_starts(hosted):
    edge_dom, edge_sub = hosted[1], hosted[1] + EDGE_TILES * LANES
    corner_dom, corner_sub = hosted[2], hosted[2] + CORNER_TILES * LANES
    return (
        (0, hosted[0], hosted[0] + up(FACE_DOM), hosted[0]),
        (0, edge_dom, edge_sub, edge_sub + EDGE_SUB),
        (0, corner_dom, corner_sub, corner_sub + CORNER_SUB),
    )


KINDS = (6, 12, 8)
FACE_ROWS = 2 * INNER * 8
EDGE_ROWS = 16
CORNER_ROWS = 4
CORNER_BASE = FACE_ROWS + EDGE_TILES * EDGE_ROWS
MESSAGE_ROWS = CORNER_BASE + CORNER_TILES * CORNER_ROWS


def shared_columns(ids, place, hosted):
    lines, size = ids.shape
    line = iota((lines, 1), 0)
    per = jnp.where(line < 6, hosted[0], jnp.where(line < 18, hosted[1], hosted[2]))
    owns, rows, masks = [], jnp.zeros((lines, size), I32), []
    for device in (place[4], place[1], place[3], place[5]):
        local = ids - device * per
        inside = (local >= 0) & (local < per)
        rows = jnp.where(inside, local, rows)
        owns.append(inside)
    starts = table_starts(hosted)
    lower = (iota((lines, lines), 1) < iota((lines, lines), 0)) & (
        (iota((lines, lines), 0) < 6) == (iota((lines, lines), 1) < 6)
    )
    lower = lower & ((iota((lines, lines), 0) < 18) == (iota((lines, lines), 1) < 18))
    lower = jnp.where(lower, 1.0, 0.0).astype(BF16)
    column = rows
    marks = jnp.concatenate([jnp.where(inside, 1.0, 0.0) for inside in owns[1:]], axis=0)
    ranks = exclusive_count(marks)
    for number in range(3):
        inside = owns[1 + number]
        mark = marks[number * lines : (number + 1) * lines]
        above = jnp.sum(dot(lower, mark.astype(BF16)), axis=1, keepdims=True)
        rank = (ranks[number * lines : (number + 1) * lines] + above).astype(I32)
        base = jnp.where(
            line < 6,
            starts[0][1 + number],
            jnp.where(line < 18, starts[1][1 + number], starts[2][1 + number]),
        )
        column = jnp.where(inside, base + rank, column)
    return column, rows


def scatter_two(parts, column_row, tiles):
    high, low = split(parts)
    both = jnp.concatenate([high, low], axis=0)
    size = column_row.shape[1]
    tile = jnp.broadcast_to((column_row >> 7).astype(BF16), both.shape)
    zero = jnp.zeros(both.shape, BF16)
    left = jnp.concatenate([jnp.where(tile == h, both, zero) for h in range(tiles)], axis=0)
    return dot_nt(left, one_hot_rows(column_row & (LANES - 1), 0, LANES))


def face_rows(face, inner):
    end = 7 * (face % 2)
    if face < 2:
        return pl.ds(end * 64 + inner * 8, 8)
    if face < 4:
        return pl.ds(inner * 64 + end * 8, 8)
    return pl.ds(inner * 64 + end, 8, stride=8)


def all_lanes(ref, rows):
    return jnp.concatenate([ref[c, rows, :] for c in range(ref.shape[0])], axis=1)


def face_nodes(ref, face):
    return jnp.concatenate(
        [all_lanes(ref, face_rows(face, inner)) for inner in range(1, INNER + 1)], axis=0
    )


def edge_place(edge):
    ends = (7 * (edge % 4 // 2), 7 * (edge % 2))
    if edge < 4:
        return ends[0] * 8 + ends[1], 64
    if edge < 8:
        return ends[0] * 64 + ends[1], 8
    return ends[0] * 64 + ends[1] * 8, 1


def edge_rows(edge):
    start, stride = edge_place(edge)
    return pl.ds(start, 8) if stride == 1 else pl.ds(start, 8, stride=stride)


def corner_place(corner):
    return (corner // 4) * 448 + (corner // 2 % 2) * 56 + (corner % 2) * 7


def apply_kernel(
    place,
    ids,
    solution,
    metric_hbm,
    grad_left,
    image_left,
    square_left,
    after,
    image_ref,
    diagonal_ref,
    column_ref,
    face_table,
    edge_table,
    corner_table,
    dom_out,
    sub_out,
    metric,
    flux_r,
    sems,
    *,
    table,
):
    del after
    size = image_ref.shape[0] * LANES
    count = table.shape[0]
    plane = count * count
    nodes = count * plane
    halves = 2
    part_rows = nodes // halves
    copies = [
        [
            fetch(metric_hbm, metric, sems, h * 7 + c, c * nodes + h * part_rows, part_rows,
                  c * nodes + h * part_rows)
            for c in range(7)
        ]
        for h in range(halves)
    ]
    for group in copies:
        for copy in group:
            copy.start()

    width = 2 * LANES
    node = iota((count, width), 0)
    ends = (0, count - 1)
    end_value = {0: float(table[0, 0]), count - 1: float(table[count - 1, count - 1])}
    ends_k = jnp.where(
        node == 0, end_value[0], jnp.where(node == count - 1, end_value[count - 1], 0.0)
    )
    for i in range(count):
        if i % (count // halves) == 0:
            for copy in copies[i // (count // halves)]:
                copy.wait()
        rows = slice(i * plane, (i + 1) * plane)
        for base in range(0, size, width):
            lanes = slice(base, base + width)

            grads = dot(grad_left[...], triple(solution[rows, lanes]))
            fluxes, weights = [[], []], [[], []]
            strip = 2 * count
            for start in range(0, plane, strip):
                at = slice(start, start + strip)
                part = [
                    metric[c * nodes + i * plane + start : c * nodes + i * plane + start + strip, lanes]
                    for c in range(6)
                ]
                grad_r = sum(
                    float(table[i, q])
                    * solution[q * plane + start : q * plane + start + strip, lanes]
                    for q in range(count)
                )
                grad_s, grad_t = grads[start : start + strip], grads[plane + start : plane + start + strip]
                flux_r[i * plane + start : i * plane + start + strip, lanes] = (
                    part[0] * grad_r + part[3] * grad_s + part[4] * grad_t
                )
                fluxes[0].append(split(part[3] * grad_r + part[1] * grad_s + part[5] * grad_t))
                fluxes[1].append(split(part[4] * grad_r + part[5] * grad_s + part[2] * grad_t))
                weights[0].append(split(part[1]))
                weights[1].append(split(part[2]))

            def stacked(pieces):
                pieces = pieces[0] + pieces[1]
                high = [piece[0] for piece in pieces]
                return jnp.concatenate(high + high + [piece[1] for piece in pieces], axis=0)

            image = dot(image_left[...], stacked(fluxes))
            diagonal = dot(square_left[...], stacked(weights))
            for j in range(count):
                lines = slice(j * count, (j + 1) * count)
                first = i * plane + j * count

                def here(c):
                    return metric[c * nodes + first : c * nodes + first + count, lanes]

                mass = here(6)
                total = diagonal[lines] + mass
                if j in ends:
                    total = total + here(5) * (ends_k * (2.0 * end_value[j]))
                if i in ends:
                    total = total + here(4) * (ends_k * (2.0 * end_value[i]))
                    if j in ends:
                        total = total + here(3) * (2.0 * end_value[i] * end_value[j])
                value = image[lines] + mass * solution[first : first + count, lanes]
                for c in range(width // LANES):
                    side = slice(c * LANES, (c + 1) * LANES)
                    image_ref[base // LANES + c, first : first + count, :] = value[:, side]
                    diagonal_ref[base // LANES + c, first : first + count, :] = total[:, side]
    for i in range(count):
        rows = slice(i * plane, (i + 1) * plane)
        for c in range(size // LANES):
            lanes = slice(c * LANES, (c + 1) * LANES)
            image_ref[c, rows, :] += sum(
                float(table[a, i]) * flux_r[a * plane : (a + 1) * plane, lanes]
                for a in range(count)
            )
            diagonal_ref[c, rows, :] += sum(
                float(table[a, i] * table[a, i]) * metric[a * plane : (a + 1) * plane, lanes]
                for a in range(count)
            )

    def _():
        hosted = (3 * size, 3 * size, size)
        starts = table_starts(hosted)
        column, row = shared_columns(ids[...], place, hosted)
        column_ref[...] = column
        row_high = (row >> 4).astype(F32)
        row_low = (row & 15).astype(F32)
        face_parts = []
        spot = iota((48, size), 0)
        for face in range(6):
            values = face_nodes(image_ref, face)
            values = jnp.where(spot == 0, row_high[face : face + 1], values)
            values = jnp.where(spot == 7, row_low[face : face + 1], values)
            values = jnp.concatenate([values, face_nodes(diagonal_ref, face)], axis=0)
            face_parts.append(jnp.concatenate(split(values), axis=0))
        faces_end = starts[0][2] + up(FACE_SUB)
        for base in range(0, faces_end, 2 * LANES):
            total = None
            for face in range(6):
                more = dot_nt(
                    face_parts[face], one_hot_rows(column[face : face + 1], base, 2 * LANES)
                )
                total = more if total is None else total + more
            total = total[:FACE_ROWS] + total[FACE_ROWS:]
            for side in range(2):
                tile = total[:, side * LANES : (side + 1) * LANES]
                place_column = base + side * LANES
                if place_column < starts[0][1]:
                    face_table[:, place_column : place_column + LANES] = tile
                elif place_column < starts[0][2]:
                    dom_out[0:FACE_ROWS, :] = tile
                else:
                    sub_out[0:FACE_ROWS, :] = tile
        tiles = starts[1][2] // LANES + EDGE_TILES
        total = None
        line = iota((8, size), 0)
        for edge in range(12):
            values = all_lanes(image_ref, edge_rows(edge))
            values = jnp.where(line == 0, row_high[6 + edge : 7 + edge], values)
            values = jnp.where(line == 7, row_low[6 + edge : 7 + edge], values)
            values = jnp.concatenate([values, all_lanes(diagonal_ref, edge_rows(edge))], axis=0)
            more = scatter_two(values, column[6 + edge : 7 + edge], tiles)
            total = more if total is None else total + more
        for number in range(tiles):
            first = number * 2 * EDGE_ROWS
            tile = total[first : first + EDGE_ROWS] + total[first + EDGE_ROWS : first + 2 * EDGE_ROWS]
            place_column = number * LANES
            if place_column < starts[1][1]:
                edge_table[:, place_column : place_column + LANES] = tile
            elif place_column < starts[1][2]:
                base = FACE_ROWS + (place_column - starts[1][1]) // LANES * EDGE_ROWS
                dom_out[base : base + EDGE_ROWS, :] = tile
            else:
                base = FACE_ROWS + (place_column - starts[1][2]) // LANES * EDGE_ROWS
                sub_out[base : base + EDGE_ROWS, :] = tile
        tiles = starts[2][2] // LANES + CORNER_TILES
        total = None
        for corner in range(8):
            at = corner_place(corner)
            values = jnp.concatenate(
                [
                    all_lanes(image_ref, slice(at, at + 1)),
                    all_lanes(diagonal_ref, slice(at, at + 1)),
                    row_high[18 + corner : 19 + corner],
                    row_low[18 + corner : 19 + corner],
                    jnp.zeros((4, size), F32),
                ],
                axis=0,
            )
            more = scatter_two(values, column[18 + corner : 19 + corner], tiles)
            total = more if total is None else total + more
        for number in range(tiles):
            tile = total[number * 16 : number * 16 + 8] + total[number * 16 + 8 : number * 16 + 16]
            place_column = number * LANES
            if place_column < starts[2][1]:
                corner_table[:, place_column : place_column + LANES] = tile
            elif place_column < starts[2][2]:
                base = CORNER_BASE + (place_column - starts[2][1]) // LANES * CORNER_ROWS
                dom_out[base : base + CORNER_ROWS, :] = tile[:CORNER_ROWS]
            else:
                base = CORNER_BASE + (place_column - starts[2][2]) // LANES * CORNER_ROWS
                sub_out[base : base + CORNER_ROWS, :] = tile[:CORNER_ROWS]

    _()


def apply_and_pack(place, ids, field, metric_rows, after, table):
    nodes, size = field.shape
    count = table.shape[0]
    eye = np.eye(count, dtype=np.float32)
    grad = np.concatenate([np.kron(table, eye), np.kron(eye, table)], axis=0)
    square = (table * table).astype(np.float32)
    squares = np.concatenate([np.kron(square, eye), np.kron(eye, square)], axis=0)
    lefts = [split_np(grad), split_np(grad.T), split_np(squares.T)]

    def out(*shape, dtype=F32):
        return jax.ShapeDtypeStruct(shape, dtype)

    outs = [
        out(size // LANES, nodes, LANES),
        out(size // LANES, nodes, LANES),
        out(sum(KINDS), size, dtype=I32),
        out(FACE_ROWS, 3 * size),
        out(EDGE_ROWS, 3 * size),
        out(8, size),
        out(MESSAGE_ROWS, LANES),
        out(MESSAGE_ROWS, LANES),
    ]
    return pl.pallas_call(
        functools.partial(apply_kernel, table=table),
        in_specs=[SMEM, VMEM, VMEM, HBM, VMEM, VMEM, VMEM, ANY],
        out_specs=[VMEM] * len(outs),
        out_shape=outs,
        scratch_shapes=[
            pltpu.VMEM(metric_rows.shape, F32),
            pltpu.VMEM((nodes, size), F32),
            pltpu.SemaphoreType.DMA((14,)),
        ],
        name="apply_and_pack",
        cost_estimate=QUICK,
        compiler_params=LARGE,
    )(place, ids, field, metric_rows, *[jnp.asarray(left) for left in lefts], after)


def message_parts(kind):
    if kind == 0:
        return [0], FACE_ROWS
    if kind == 1:
        return [FACE_ROWS + q * EDGE_ROWS for q in range(EDGE_TILES)], EDGE_ROWS
    return [CORNER_BASE + q * CORNER_ROWS for q in range(CORNER_TILES)], CORNER_ROWS


def message_tiles(ref, kind):
    places, rows = message_parts(kind)
    return [ref[at : at + rows, :] for at in places]


def table_tiles(ref):
    return [ref[:, c : c + LANES] for c in range(0, ref.shape[1], LANES)]


def message_values(ref, kind, limit):
    values = jnp.concatenate(message_tiles(ref, kind), axis=1)
    first = 2 if kind == 2 else 0
    second = 3 if kind == 2 else 7
    row = (values[first : first + 1] * 16.0 + values[second : second + 1]).astype(I32)
    row = jnp.where(iota(row.shape, 1) < limit, row, -1)
    if kind == 2:
        values = jnp.concatenate([values, jnp.zeros_like(values)], axis=0)
    return values, row


def add_message(ref, tables, outs, limits):
    values, row = message_values(ref, 0, limits[0])
    parts = jnp.concatenate(split(values), axis=0)
    for base in range(0, outs[0].shape[1], 2 * LANES):
        lanes = slice(base, base + 2 * LANES)
        more = dot_nt(parts, one_hot_rows(row, base, 2 * LANES))
        outs[0][:, lanes] = tables[0][:, lanes] + more[:FACE_ROWS] + more[FACE_ROWS:]
    for kind in (1, 2):
        values, row = message_values(ref, kind, limits[kind])
        rows = values.shape[0]
        count = outs[kind].shape[1] // LANES
        total = scatter_two(values, row, count)
        for number in range(count):
            lanes = slice(number * LANES, (number + 1) * LANES)
            first = number * 2 * rows
            more = total[first : first + rows] + total[first + rows : first + 2 * rows]
            outs[kind][:, lanes] = tables[kind][:, lanes] + more


def read_message(ref, tables, back):
    for kind in range(3):
        places, rows = message_parts(kind)
        row = jnp.maximum(message_values(ref, kind, 1 << 20)[1], 0)
        tiles = table_tiles(tables[kind])
        depth = tiles[0].shape[0]
        for number, at in enumerate(places):
            spot = jnp.broadcast_to(row[:, number * LANES : (number + 1) * LANES], (depth, LANES))
            got = gather_tiles(tiles, spot & (LANES - 1), spot >> 7)
            back[at : at + rows, :] = got[:rows]


SUB_LIMITS = (FACE_SUB, EDGE_SUB, CORNER_SUB)
DOM_LIMITS = (FACE_DOM, EDGE_SUB + EZ, CORNER_SUB + 2 * EZ)


def passed_on(message, received):
    parts = [message[0:FACE_ROWS, :]]
    for kind, limit in ((1, EDGE_SUB), (2, CORNER_SUB)):
        ours, theirs = message_tiles(message, kind), message_tiles(received, kind)
        for number in range(len(ours)):
            lane = iota(ours[number].shape, 1) + number * LANES
            parts.append(jnp.where(lane < limit, ours[number], theirs[number]))
    return parts


def pass_on_kernel(message, received, *rest):
    out = rest[-1]
    at = 0
    for part in passed_on(message, received):
        out[at : at + part.shape[0], :] = part
        at += part.shape[0]


def pass_on(message, received, after=()):
    return pl.pallas_call(
        pass_on_kernel,
        in_specs=[VMEM] * 2 + [ANY] * len(after),
        out_specs=VMEM,
        out_shape=jax.ShapeDtypeStruct(message.shape, F32),
        name="pass_on",
        cost_estimate=QUICK,
        compiler_params=SMALL,
    )(message, received, *after)


def add_sub_kernel(faces, edges, corners, message, after, *outs):
    del after
    add_message(message, (faces, edges, corners), outs, SUB_LIMITS)


def add_sub(tables, message, after):
    return pl.pallas_call(
        add_sub_kernel,
        in_specs=[VMEM] * 4 + [ANY],
        out_specs=[VMEM] * 3,
        out_shape=[jax.ShapeDtypeStruct(a.shape, F32) for a in tables],
        name="add_sub",
        cost_estimate=QUICK,
        compiler_params=SMALL,
    )(*tables, message, after)


def add_dom_kernel(faces, edges, corners, message, *outs):
    add_message(message, (faces, edges, corners), outs[:3], DOM_LIMITS)
    read_message(message, outs[:3], outs[3])


def add_dom(tables, message):
    return pl.pallas_call(
        add_dom_kernel,
        in_specs=[VMEM] * 4,
        out_specs=[VMEM] * 4,
        out_shape=[jax.ShapeDtypeStruct(a.shape, F32) for a in (*tables, message)],
        name="add_dom",
        cost_estimate=QUICK,
        compiler_params=SMALL,
    )(*tables, message)


def read_sub_kernel(faces, edges, corners, message, back):
    read_message(message, (faces, edges, corners), back)


def read_sub(tables, message):
    return pl.pallas_call(
        read_sub_kernel,
        in_specs=[VMEM] * 4,
        out_specs=VMEM,
        out_shape=jax.ShapeDtypeStruct(message.shape, F32),
        name="read_sub",
        cost_estimate=QUICK,
        compiler_params=SMALL,
    )(*tables, message)


def spots(column_ref, line, rows, c, first):
    spot = jnp.broadcast_to(column_ref[line : line + 1, c * LANES : (c + 1) * LANES], (rows, LANES))
    return spot & (LANES - 1), (spot >> 7) - first


def put(ref, c, rows, values, high, count):
    line = iota(values.shape, 0)
    new = (line > 0) & (line < 7) & (high >= 0) & (high < count)
    ref[c, rows, :] = jnp.where(new, values, ref[c, rows, :])


def merge_faces(column_ref, tiles, first, image, diagonal):
    for c in range(image.shape[0]):
        for face in range(6):
            low, high = spots(column_ref, face, FACE_ROWS, c, first)
            got = gather_tiles(tiles, low, high)
            for number in range(INNER):
                rows = face_rows(face, number + 1)
                put(image, c, rows, got[number * 8 : number * 8 + 8], high[:8], len(tiles))
                put(diagonal, c, rows, got[48 + number * 8 : 56 + number * 8], high[:8], len(tiles))


def merge_edges(column_ref, tiles, first, image, diagonal):
    for c in range(image.shape[0]):
        for edge in range(12):
            low, high = spots(column_ref, 6 + edge, EDGE_ROWS, c, first)
            got = gather_tiles(tiles, low, high)
            put(image, c, edge_rows(edge), got[:8], high[:8], len(tiles))
            put(diagonal, c, edge_rows(edge), got[8:], high[:8], len(tiles))


def merge_corners(column_ref, tiles, first, image, diagonal):
    tiles = [jnp.concatenate([tile[0:2]] * 4, axis=0) for tile in tiles]
    for c in range(image.shape[0]):
        lanes = slice(c * LANES, (c + 1) * LANES)
        for group in range(2):
            spot = jnp.concatenate(
                [
                    jnp.broadcast_to(column_ref[n : n + 1, lanes], (2, LANES))
                    for n in range(18 + group * 4, 22 + group * 4)
                ],
                axis=0,
            )
            high = (spot >> 7) - first
            got = gather_tiles(tiles, spot & (LANES - 1), high)
            new = (high >= 0) & (high < len(tiles))
            for number in range(4):
                at = corner_place(group * 4 + number)
                for ref, line in ((image, 2 * number), (diagonal, 2 * number + 1)):
                    ref[c, at : at + 1, :] = jnp.where(
                        new[line : line + 1], got[line : line + 1], ref[c, at : at + 1, :]
                    )


def merge_message(column_ref, message, first_kind, image, diagonal):
    size = image.shape[0] * LANES
    starts = table_starts((3 * size, 3 * size, size))
    for kind, merge in enumerate((merge_faces, merge_edges, merge_corners)):
        first = starts[kind][first_kind] // LANES
        merge(column_ref, message_tiles(message, kind), first, image, diagonal)


def merge_own(column, tables, image, diagonal, after):
    def kernel(column, faces, edges, corners, image_in, diagonal_in, after, image, diagonal):
        del after
        image[...] = image_in[...]
        diagonal[...] = diagonal_in[...]
        merge_faces(column, table_tiles(faces), 0, image, diagonal)
        merge_edges(column, table_tiles(edges), 0, image, diagonal)
        merge_corners(column, table_tiles(corners), 0, image, diagonal)

    return pl.pallas_call(
        kernel,
        in_specs=[VMEM] * 6 + [ANY],
        out_specs=[VMEM] * 2,
        out_shape=[jax.ShapeDtypeStruct(image.shape, F32)] * 2,
        name="merge_own",
        cost_estimate=QUICK,
        compiler_params=SMALL,
    )(column, *tables, image, diagonal, after)


def merge_dom(column, message, image, diagonal, after):
    def kernel(column, message, image_in, diagonal_in, after, image, diagonal):
        del after
        image[...] = image_in[...]
        diagonal[...] = diagonal_in[...]
        merge_message(column, message, 1, image, diagonal)

    return pl.pallas_call(
        kernel,
        in_specs=[VMEM] * 4 + [ANY],
        out_specs=[VMEM] * 2,
        out_shape=[jax.ShapeDtypeStruct(image.shape, F32)] * 2,
        name="merge_dom",
        cost_estimate=QUICK,
        compiler_params=SMALL,
    )(column, message, image, diagonal, after)


def relax_kernel(column, message, image_in, diagonal_in, field, forcing, source, *rest):
    relaxed, *outs, image, diagonal = rest[-7:]
    nodes, size = relaxed.shape
    image[...] = image_in[...]
    diagonal[...] = diagonal_in[...]
    merge_message(column, message, 2, image, diagonal)
    for row in range(0, nodes, STRIP):
        rows = slice(row, row + STRIP)
        for c in range(size // LANES):
            lanes = slice(c * LANES, (c + 1) * LANES)
            step = (forcing[rows, lanes] - image[c, rows, :]) / diagonal[c, rows, :]
            relaxed[rows, lanes] = field[rows, lanes] + RELAX * step
    for pair in range(2):
        source_row = source[:, pair * LANES : (pair + 1) * LANES]
        pack_block(relaxed, 0, nodes, source_row, outs[2 * pair : 2 * pair + 2], 0)


def relax_and_pack(column, message, image, diagonal, field, forcing, source, after):
    nodes, size = field.shape
    leaving = jax.ShapeDtypeStruct((nodes // 2, LANES), F32)
    return pl.pallas_call(
        relax_kernel,
        in_specs=[VMEM] * 7 + [ANY] * len(after),
        out_specs=[VMEM] * 5,
        out_shape=[jax.ShapeDtypeStruct((nodes, size), F32)] + [leaving] * 4,
        scratch_shapes=[pltpu.VMEM((size // LANES, nodes, LANES), F32)] * 2,
        name="relax_and_pack",
        cost_estimate=QUICK,
        compiler_params=SMALL,
    )(column, message, image, diagonal, field, forcing, source, *after)


def shifted(value, axis, steps):
    count = lax.axis_size(axis)
    return lax.ppermute(value, axis, [(i, (i + steps) % count) for i in range(count)])


def swapped(to_previous, to_next, axis):
    return shifted(to_next, axis, 1), shifted(to_previous, axis, -1)


def on_device(solution, forcing, metric, entity_ids, new_owner):
    size = solution.shape[-1]
    place = devices()
    table = derivative_table(solution.shape[0] - 1)
    field = solution.reshape(-1, size)
    metric_rows = metric.reshape(-1, size)
    components = metric.shape[0]
    block = metric_rows.shape[0] // components
    late = components - EARLY
    source, landing, *messages = plan_and_pack(place, new_owner.reshape(1, size), metric_rows, block)
    sub_early = swapped(*messages, "sub")
    messages = pack(source, metric_rows, 0, EARLY, 0, block, landing, "pack_dom_early")
    dom_early = swapped(*messages, "dom")
    image, diagonal, column, *tables, dom, sub = apply_and_pack(
        place, entity_ids, field, metric_rows, messages[0], table
    )
    got_sub = shifted(sub, "sub", 1)
    messages = pack(source, metric_rows, EARLY, late, 1, block, sub, "pack_sub_late")
    sub_late = swapped(*messages, "sub")
    dom = pass_on(dom, got_sub, dom_early + sub_early)
    got_dom = shifted(dom, "dom", 1)
    tables = add_sub(tables, got_sub, dom)
    *tables, dom_back = add_dom(tables, got_dom)
    back_dom = shifted(dom_back, "dom", -1)
    messages = pack(source, metric_rows, EARLY, late, 0, block, dom_back, "pack_dom_late")
    dom_late = swapped(*messages, "dom")
    sub_back = read_sub(tables, got_sub)
    sub_back = pass_on(sub_back, back_dom)
    back_sub = shifted(sub_back, "sub", -1)
    image, diagonal = merge_own(column, tables, image, diagonal, messages[0])
    image, diagonal = merge_dom(column, back_dom, image, diagonal, sub_back)
    relaxed, *leaving = relax_and_pack(
        column, back_sub, image, diagonal, field, forcing.reshape(-1, size), source,
        dom_late + sub_late,
    )
    got_sub = swapped(*leaving[2:], "sub")
    got_dom = swapped(*leaving[:2], "dom")
    moved = land_metric(
        landing, metric_rows, dom_early + sub_early, 0, EARLY, block, None, leaving[0], "land_early"
    )
    moved = land_metric(
        landing, metric_rows, dom_late + sub_late, EARLY, late, block, moved, leaving[0], "land_late"
    )
    smoothed = land_field(landing, relaxed, got_dom + got_sub)
    return smoothed.reshape(solution.shape), moved.reshape(metric.shape)


def solution(mesh):
    placed = (
        P(None, None, None, ("dom", "sub")),
        P(None, None, None, ("dom", "sub")),
        P(None, None, None, None, ("dom", "sub")),
        P(None, ("dom", "sub")),
        P(("dom", "sub")),
    )
    return jax.shard_map(
        on_device,
        mesh=mesh,
        in_specs=placed,
        out_specs=(P(None, None, None, ("dom", "sub")), P(None, None, None, None, ("dom", "sub"))),
        check_vma=False,
    )
```

```python
import functools

import jax
import jax.numpy as jnp
import numpy as np
from jax import lax
from jax.experimental import pallas as pl
from jax.experimental.pallas import tpu as pltpu
from jax.sharding import PartitionSpec as P

EX = 4
EY = 4
EZ = 32
MOVE = 64
RELAX = 0.6
LANES = 128
INNER = 6
SUB_EARLY = 5
DOM_EARLY = 7

NT = (((1,), (1,)), ((), ()))
VMEM = pl.BlockSpec(memory_space=pltpu.VMEM)
ANY = pl.BlockSpec(memory_space=pl.ANY)
SMEM = pl.BlockSpec(memory_space=pltpu.SMEM)
QUICK = pl.CostEstimate(flops=1000, bytes_accessed=1000, transcendentals=0)
HBM = pl.BlockSpec(memory_space=pltpu.HBM)
LARGE = pltpu.CompilerParams(vmem_limit_bytes=24 << 20)
SMALL = pltpu.CompilerParams(vmem_limit_bytes=16 << 20)
STRIP = 256
F32 = jnp.float32
BF16 = jnp.bfloat16
I32 = jnp.int32


def derivative_table(order):
    count = order + 1
    points = -np.cos(np.pi * np.arange(count) / order)
    legendre = np.zeros((count, count))
    for sweep in range(80):
        legendre[:, 0] = 1.0
        legendre[:, 1] = points
        for degree in range(2, count):
            legendre[:, degree] = (
                (2 * degree - 1) * points * legendre[:, degree - 1]
                - (degree - 1) * legendre[:, degree - 2]
            ) / degree
        points = points - (points * legendre[:, order] - legendre[:, order - 1]) / (
            count * legendre[:, order]
        )
    legendre[:, 0] = 1.0
    legendre[:, 1] = points
    for degree in range(2, count):
        legendre[:, degree] = (
            (2 * degree - 1) * points * legendre[:, degree - 1]
            - (degree - 1) * legendre[:, degree - 2]
        ) / degree
    values = legendre[:, order]
    identity = np.eye(count)
    spread = points[:, None] - points[None, :] + identity
    table = values[:, None] / values[None, :] / spread
    table = table * (1.0 - identity)
    table[0, 0] = -order * count / 4.0
    table[order, order] = order * count / 4.0
    return table.astype(np.float32)


def split_np(matrix):
    high = matrix.astype(jnp.bfloat16).astype(np.float32)
    low = (matrix - high).astype(jnp.bfloat16)
    return np.concatenate([high.astype(jnp.bfloat16), low, high.astype(jnp.bfloat16)], axis=1)


def split(values):
    high = values.astype(BF16)
    low = (values - high.astype(F32)).astype(BF16)
    return high, low


def triple(values):
    high, low = split(values)
    return jnp.concatenate([high, high, low], axis=0)


def dot(left, right):
    return jnp.dot(left, right, preferred_element_type=F32)


def dot_nt(left, right):
    return lax.dot_general(left, right, NT, preferred_element_type=F32)


def iota(shape, dim):
    return lax.broadcasted_iota(I32, shape, dim)


def one_hot_rows(index_row, start, count):
    size = index_row.shape[1]
    out = []
    for base in range(0, count, LANES):
        local = (index_row - (start + base)).astype(BF16)
        rows = iota((LANES, size), 0).astype(BF16)
        out.append(
            jnp.where(rows == local, jnp.ones((LANES, size), BF16), jnp.zeros((LANES, size), BF16))
        )
    return out[0] if len(out) == 1 else jnp.concatenate(out, axis=0)


def exclusive_count(masks):
    size = masks.shape[1]
    upper = jnp.where(iota((size, size), 0) < iota((size, size), 1), 1.0, 0.0).astype(BF16)
    return dot(masks.astype(BF16), upper)


def gather_tiles(tiles, low, high):
    out = None
    for number, tile in enumerate(tiles):
        got = jnp.take_along_axis(tile, low, axis=1)
        out = got if out is None else jnp.where(high == number, got, out)
    return out


def devices():
    dom_count = lax.axis_size("dom")
    sub_count = lax.axis_size("sub")
    dom = lax.axis_index("dom")
    sub = lax.axis_index("sub")
    dom_ahead = lax.rem(dom + 1, dom_count)
    dom_behind = lax.rem(dom + dom_count - 1, dom_count)
    sub_ahead = lax.rem(sub + 1, sub_count)
    sub_behind = lax.rem(sub + sub_count - 1, sub_count)
    return jnp.stack(
        [
            dom_behind * sub_count + sub,
            dom_ahead * sub_count + sub,
            dom * sub_count + sub_behind,
            dom * sub_count + sub_ahead,
            dom * sub_count + sub,
            dom_ahead * sub_count + sub_ahead,
        ]
    ).astype(I32)


def pack_pair(top, bottom):
    left = iota(top.shape, 1) < MOVE
    first = jnp.where(left, top, pltpu.roll(bottom, MOVE, 1))
    second = jnp.where(left, pltpu.roll(top, MOVE, 1), bottom)
    return first, second


def pick_columns(ref, rows, low, high):
    tiles = [ref[rows, c : c + LANES] for c in range(0, ref.shape[1], LANES)]
    return gather_tiles(tiles, low, high)


def pack_block(ref, start, block, source_row, outs, to):
    half = block // 2
    source = jnp.broadcast_to(source_row, (half, LANES))
    low, high = source & (LANES - 1), source >> 7
    top = pick_columns(ref, slice(start, start + half), low, high)
    bottom = pick_columns(ref, slice(start + half, start + block), low, high)
    for out, message in zip(outs, pack_pair(top, bottom)):
        out[to : to + half, :] = message


def arrival_spots(landing_row):
    return jnp.concatenate([one_hot_rows(landing_row, 0, 4 * MOVE)] * 3, axis=0)


def split_exactly(values):
    parts = []
    for _ in range(3):
        parts.append(values.astype(BF16))
        values = values - parts[-1].astype(F32)
    return jnp.concatenate(parts, axis=1)


def land_block(ref, start, block, landing_row, spots, messages, ats, out, to):
    land_strips(ref, start, block // 2, 0, block // 2, landing_row, spots, messages, ats, out, to)


def land_strips(ref, start, half, from_row, to_row, landing_row, spots, messages, ats, out, to):
    rows = to_row - from_row
    parts = [message[at + from_row : at + to_row, :] for message, at in zip(messages, ats)]
    pairs = [pack_pair(parts[0], parts[1]), pack_pair(parts[2], parts[3])]
    stays = jnp.broadcast_to(landing_row < 0, (rows, landing_row.shape[1]))
    for side in range(2):
        arrived = jnp.concatenate([pairs[0][side], pairs[1][side]], axis=1)
        got = dot(split_exactly(arrived), spots)
        first = side * half + from_row
        held = ref[start + first : start + first + rows, :]
        out[to + first : to + first + rows, :] = jnp.where(stays, held, got)


def move_plan(owner, place):
    size = owner.shape[1]
    own = place[4]
    line = iota((8, size), 0)
    target = jnp.where(
        line == 0,
        place[0],
        jnp.where(line == 1, place[1], jnp.where(line == 2, place[2], place[3])),
    )
    nobody = jnp.broadcast_to(owner, (8, size))
    away = nobody != own
    masks = jnp.where(away & (((nobody == target) & (line < 4)) | (line == 4)), 1.0, 0.0)
    ranks = exclusive_count(masks)
    counts = jnp.sum(masks, axis=1, keepdims=True)
    hole = ranks[4:5]
    gone = masks[4:5] > 0.5
    column = jnp.full((1, size), -1.0, F32)
    landing = jnp.full((1, size), -1.0, F32)
    offset = jnp.zeros((1, 1), F32)
    for way in range(4):
        column = jnp.where(masks[way : way + 1] > 0.5, way * MOVE + ranks[way : way + 1], column)
        ahead = hole - offset
        here = gone & (ahead >= 0.0) & (ahead < counts[way : way + 1])
        landing = jnp.where(here, way * MOVE + ahead, landing)
        offset = offset + counts[way : way + 1]
    spots = one_hot_rows(column.astype(I32), 0, 4 * MOVE)
    element = iota((8, size), 1)
    parts = jnp.where(iota((8, size), 0) == 0, element >> 4, element & 15)
    found = dot_nt(parts.astype(BF16), spots)
    source = found[0:1] * 16.0 + found[1:2]
    return source.astype(I32), landing.astype(I32)


def fetch(source, target, sems, number, start, count, to):
    return pltpu.make_async_copy(
        source.at[pl.ds(start, count), :], target.at[pl.ds(to, count), :], sems.at[number]
    )


def send_parts(metric, first, source, outs, held, sems, block):
    half = block // 2
    for number in range(held.shape[0] // block):
        fetch(metric, held, sems, number, (first + number) * block, block, number * block).wait()
        pack_block(held, number * block, block, source, outs, number * half)


def fetch_parts(metric, first, held, sems, block):
    for number in range(held.shape[0] // block):
        fetch(metric, held, sems, number, (first + number) * block, block, number * block).start()


def plan_and_pack_kernel(place, owner_hbm, metric, source_ref, landing_ref, *rest, block):
    *outs, held, sems, owner, owner_sem = rest
    copy = pltpu.make_async_copy(owner_hbm, owner, owner_sem)
    copy.start()
    fetch_parts(metric, 0, held, sems, block)
    copy.wait()
    source, landing = move_plan(owner[...], place)
    source_ref[...] = source
    landing_ref[...] = landing
    send_parts(metric, 0, source[:, LANES:], outs, held, sems, block)


def pack_kernel(source, metric, *rest, first, pair, block):
    *outs, held, sems = rest[-4:]
    fetch_parts(metric, first, held, sems, block)
    lanes = slice(pair * LANES, (pair + 1) * LANES)
    send_parts(metric, first, source[:, lanes], outs, held, sems, block)


def sent_shapes(count, block, size):
    outs = [jax.ShapeDtypeStruct((count * block // 2, LANES), F32)] * 2
    scratch = [pltpu.VMEM((count * block, size), F32), pltpu.SemaphoreType.DMA((count,))]
    return outs, scratch


def plan_and_pack(place, owner, metric_rows, block):
    size = metric_rows.shape[1]
    outs, scratch = sent_shapes(SUB_EARLY, block, size)
    plan = [jax.ShapeDtypeStruct((1, 4 * MOVE), I32), jax.ShapeDtypeStruct((1, size), I32)]
    return pl.pallas_call(
        functools.partial(plan_and_pack_kernel, block=block),
        in_specs=[SMEM, HBM, HBM],
        out_specs=[VMEM] * 4,
        out_shape=plan + outs,
        scratch_shapes=scratch + [pltpu.VMEM((1, size), I32), pltpu.SemaphoreType.DMA],
        name="plan_and_pack",
        cost_estimate=QUICK,
        compiler_params=LARGE,
    )(place, owner, metric_rows)


def pack(source, metric_rows, first, count, pair, block, after, name):
    outs, scratch = sent_shapes(count, block, metric_rows.shape[1])
    return pl.pallas_call(
        functools.partial(pack_kernel, first=first, pair=pair, block=block),
        in_specs=[VMEM, HBM] + [ANY] * len(after),
        out_specs=[VMEM] * 2,
        out_shape=outs,
        scratch_shapes=scratch,
        name=name,
        cost_estimate=QUICK,
        compiler_params=LARGE,
    )(source, metric_rows, *after)


def land_metric_kernel(landing, metric, *rest, first, block, spots):
    *messages, out, token, held, ready, sems, out_sems = rest
    token[...] = jnp.zeros_like(token)
    columns = arrival_spots(landing[...])
    count = held.shape[0] // block
    fetch_parts(metric, first, held, sems, block)
    for number in range(count):
        start = number * block
        parts, at = spots[number]
        fetch(metric, held, sems, number, (first + number) * block, block, start).wait()
        land_block(
            held, start, block, landing[...], columns, [messages[k] for k in parts], at, ready, start
        )
        fetch(ready, out, out_sems, number, start, block, (first + number) * block).start()
    for number in range(count):
        start = number * block
        fetch(ready, out, out_sems, number, start, block, (first + number) * block).wait()


def land_metric(landing, metric_rows, dom, sub, first, count, block, before, after, name):
    size = metric_rows.shape[1]
    messages, spots = [], []
    for number in range(first, first + count):
        parts, ats = [], None
        for (early, late), limit in ((dom, DOM_EARLY), (sub, SUB_EARLY)):
            chosen, local = (early, number) if number < limit else (late, number - limit)
            for message in chosen:
                known = [k for k, other in enumerate(messages) if other is message]
                if not known:
                    messages.append(message)
                parts.append(known[0] if known else len(messages) - 1)
            ats = (ats or []) + [local * block // 2] * 2
        spots.append((parts, ats))
    operands = [landing, metric_rows, *messages, after]
    specs = [VMEM, HBM] + [VMEM] * len(messages) + [ANY]
    aliases = {}
    if before is not None:
        aliases = {len(operands): 0}
        operands.append(before)
        specs.append(HBM)
    return pl.pallas_call(
        functools.partial(land_metric_kernel, first=first, block=block, spots=spots),
        in_specs=specs,
        out_specs=[HBM, VMEM],
        out_shape=[
            jax.ShapeDtypeStruct(metric_rows.shape, F32),
            jax.ShapeDtypeStruct((8, LANES), F32),
        ],
        scratch_shapes=[
            pltpu.VMEM((count * block, size), F32),
            pltpu.VMEM((count * block, size), F32),
            pltpu.SemaphoreType.DMA((count,)),
            pltpu.SemaphoreType.DMA((count,)),
        ],
        input_output_aliases=aliases,
        name=name,
        cost_estimate=QUICK,
        compiler_params=LARGE,
    )(*operands)


def land_field_kernel(landing, relaxed, first, second, third, fourth, after, out, ready, sems):
    del after
    rows = relaxed.shape[0]
    piece = rows // 8
    half = rows // 2
    messages = (first, second, third, fourth)
    copies = []
    columns = arrival_spots(landing[...])
    for row in range(0, half, piece):
        land_strips(
            relaxed, 0, half, row, row + piece, landing[...], columns, messages, [0] * 4, ready, 0
        )
        for side in range(2):
            copies.append(fetch(ready, out, sems, len(copies), side * half + row, piece, side * half + row))
            copies[-1].start()
    for copy in copies:
        copy.wait()


def land_field(landing, relaxed, arrived, after):
    count = 8
    return pl.pallas_call(
        land_field_kernel,
        in_specs=[VMEM] * 6 + [ANY],
        out_specs=HBM,
        out_shape=jax.ShapeDtypeStruct(relaxed.shape, F32),
        scratch_shapes=[pltpu.VMEM(relaxed.shape, F32), pltpu.SemaphoreType.DMA((count,))],
        name="land_field",
        cost_estimate=QUICK,
        compiler_params=SMALL,
    )(landing, relaxed, *arrived, after)


FACE_DOM = EY * EZ
FACE_SUB = EX * EZ
EDGE_DOM = EZ * (4 * EY - 1)
EDGE_SUB = EZ * (4 * EX - 1)
CORNER_DOM = EZ * (4 * EY - 2)
CORNER_SUB = EZ * (4 * EX - 2)


def up(count):
    return -(-count // LANES) * LANES


EDGE_TILES = up(EDGE_DOM) // LANES
CORNER_TILES = up(CORNER_DOM) // LANES


def table_starts(hosted):
    edge_dom, edge_sub = hosted[1], hosted[1] + EDGE_TILES * LANES
    corner_dom, corner_sub = hosted[2], hosted[2] + CORNER_TILES * LANES
    return (
        (0, hosted[0], hosted[0] + up(FACE_DOM), hosted[0]),
        (0, edge_dom, edge_sub, edge_sub + EDGE_SUB),
        (0, corner_dom, corner_sub, corner_sub + CORNER_SUB),
    )


KINDS = (6, 12, 8)
FACE_ROWS = 2 * INNER * 8
EDGE_ROWS = 16
CORNER_ROWS = 4
CORNER_BASE = FACE_ROWS + EDGE_TILES * EDGE_ROWS
MESSAGE_ROWS = CORNER_BASE + CORNER_TILES * CORNER_ROWS


def shared_columns(ids, place, hosted):
    lines, size = ids.shape
    line = iota((lines, 1), 0)
    per = jnp.where(line < 6, hosted[0], jnp.where(line < 18, hosted[1], hosted[2]))
    owns, rows, masks = [], jnp.zeros((lines, size), I32), []
    for device in (place[4], place[1], place[3], place[5]):
        local = ids - device * per
        inside = (local >= 0) & (local < per)
        rows = jnp.where(inside, local, rows)
        owns.append(inside)
    starts = table_starts(hosted)
    lower = (iota((lines, lines), 1) < iota((lines, lines), 0)) & (
        (iota((lines, lines), 0) < 6) == (iota((lines, lines), 1) < 6)
    )
    lower = lower & ((iota((lines, lines), 0) < 18) == (iota((lines, lines), 1) < 18))
    lower = jnp.where(lower, 1.0, 0.0).astype(BF16)
    column = rows
    marks = jnp.concatenate([jnp.where(inside, 1.0, 0.0) for inside in owns[1:]], axis=0)
    ranks = exclusive_count(marks)
    for number in range(3):
        inside = owns[1 + number]
        mark = marks[number * lines : (number + 1) * lines]
        above = jnp.sum(dot(lower, mark.astype(BF16)), axis=1, keepdims=True)
        rank = (ranks[number * lines : (number + 1) * lines] + above).astype(I32)
        base = jnp.where(
            line < 6,
            starts[0][1 + number],
            jnp.where(line < 18, starts[1][1 + number], starts[2][1 + number]),
        )
        column = jnp.where(inside, base + rank, column)
    return column, rows


def scatter_two(parts, column_row, tiles):
    high, low = split(parts)
    both = jnp.concatenate([high, low], axis=0)
    size = column_row.shape[1]
    tile = jnp.broadcast_to((column_row >> 7).astype(BF16), both.shape)
    zero = jnp.zeros(both.shape, BF16)
    left = jnp.concatenate([jnp.where(tile == h, both, zero) for h in range(tiles)], axis=0)
    return dot_nt(left, one_hot_rows(column_row & (LANES - 1), 0, LANES))


def face_rows(face, inner):
    end = 7 * (face % 2)
    if face < 2:
        return pl.ds(end * 64 + inner * 8, 8)
    if face < 4:
        return pl.ds(inner * 64 + end * 8, 8)
    return pl.ds(inner * 64 + end, 8, stride=8)


def all_lanes(ref, rows):
    return jnp.concatenate([ref[c, rows, :] for c in range(ref.shape[0])], axis=1)


def face_nodes(ref, face):
    return jnp.concatenate(
        [all_lanes(ref, face_rows(face, inner)) for inner in range(1, INNER + 1)], axis=0
    )


def edge_place(edge):
    ends = (7 * (edge % 4 // 2), 7 * (edge % 2))
    if edge < 4:
        return ends[0] * 8 + ends[1], 64
    if edge < 8:
        return ends[0] * 64 + ends[1], 8
    return ends[0] * 64 + ends[1] * 8, 1


def edge_rows(edge):
    start, stride = edge_place(edge)
    return pl.ds(start, 8) if stride == 1 else pl.ds(start, 8, stride=stride)


def corner_place(corner):
    return (corner // 4) * 448 + (corner // 2 % 2) * 56 + (corner % 2) * 7


def apply_kernel(
    place,
    ids,
    solution,
    metric_hbm,
    grad_left,
    image_left,
    square_left,
    after,
    image_ref,
    diagonal_ref,
    column_ref,
    face_table,
    edge_table,
    corner_table,
    dom_out,
    sub_out,
    metric,
    flux_r,
    sems,
    *,
    table,
):
    del after
    size = image_ref.shape[0] * LANES
    count = table.shape[0]
    plane = count * count
    nodes = count * plane
    halves = 2
    part_rows = nodes // halves
    copies = [
        [
            fetch(metric_hbm, metric, sems, h * 7 + c, c * nodes + h * part_rows, part_rows,
                  c * nodes + h * part_rows)
            for c in range(7)
        ]
        for h in range(halves)
    ]
    for group in copies:
        for copy in group:
            copy.start()

    width = 2 * LANES
    node = iota((count, width), 0)
    ends = (0, count - 1)
    end_value = {0: float(table[0, 0]), count - 1: float(table[count - 1, count - 1])}
    ends_k = jnp.where(
        node == 0, end_value[0], jnp.where(node == count - 1, end_value[count - 1], 0.0)
    )
    for i in range(count):
        if i % (count // halves) == 0:
            for copy in copies[i // (count // halves)]:
                copy.wait()
        rows = slice(i * plane, (i + 1) * plane)
        for base in range(0, size, width):
            lanes = slice(base, base + width)

            grads = dot(grad_left[...], triple(solution[rows, lanes]))
            fluxes, weights = [[], []], [[], []]
            strip = 2 * count
            for start in range(0, plane, strip):
                at = slice(start, start + strip)
                part = [
                    metric[c * nodes + i * plane + start : c * nodes + i * plane + start + strip, lanes]
                    for c in range(6)
                ]
                grad_r = sum(
                    float(table[i, q])
                    * solution[q * plane + start : q * plane + start + strip, lanes]
                    for q in range(count)
                )
                grad_s, grad_t = grads[start : start + strip], grads[plane + start : plane + start + strip]
                flux_r[i * plane + start : i * plane + start + strip, lanes] = (
                    part[0] * grad_r + part[3] * grad_s + part[4] * grad_t
                )
                fluxes[0].append(split(part[3] * grad_r + part[1] * grad_s + part[5] * grad_t))
                fluxes[1].append(split(part[4] * grad_r + part[5] * grad_s + part[2] * grad_t))
                weights[0].append(split(part[1]))
                weights[1].append(split(part[2]))

            def stacked(pieces):
                pieces = pieces[0] + pieces[1]
                high = [piece[0] for piece in pieces]
                return jnp.concatenate(high + high + [piece[1] for piece in pieces], axis=0)

            image = dot(image_left[...], stacked(fluxes))
            diagonal = dot(square_left[...], stacked(weights))
            for j in range(count):
                lines = slice(j * count, (j + 1) * count)
                first = i * plane + j * count

                def here(c):
                    return metric[c * nodes + first : c * nodes + first + count, lanes]

                mass = here(6)
                total = diagonal[lines] + mass
                if j in ends:
                    total = total + here(5) * (ends_k * (2.0 * end_value[j]))
                if i in ends:
                    total = total + here(4) * (ends_k * (2.0 * end_value[i]))
                    if j in ends:
                        total = total + here(3) * (2.0 * end_value[i] * end_value[j])
                value = image[lines] + mass * solution[first : first + count, lanes]
                for c in range(width // LANES):
                    side = slice(c * LANES, (c + 1) * LANES)
                    image_ref[base // LANES + c, first : first + count, :] = value[:, side]
                    diagonal_ref[base // LANES + c, first : first + count, :] = total[:, side]
    for i in range(count):
        rows = slice(i * plane, (i + 1) * plane)
        for c in range(size // LANES):
            lanes = slice(c * LANES, (c + 1) * LANES)
            image_ref[c, rows, :] += sum(
                float(table[a, i]) * flux_r[a * plane : (a + 1) * plane, lanes]
                for a in range(count)
            )
            diagonal_ref[c, rows, :] += sum(
                float(table[a, i] * table[a, i]) * metric[a * plane : (a + 1) * plane, lanes]
                for a in range(count)
            )

    def _():
        hosted = (3 * size, 3 * size, size)
        starts = table_starts(hosted)
        column, row = shared_columns(ids[...], place, hosted)
        column_ref[...] = column
        row_high = (row >> 4).astype(F32)
        row_low = (row & 15).astype(F32)
        face_parts = []
        spot = iota((48, size), 0)
        for face in range(6):
            values = face_nodes(image_ref, face)
            values = jnp.where(spot == 0, row_high[face : face + 1], values)
            values = jnp.where(spot == 7, row_low[face : face + 1], values)
            values = jnp.concatenate([values, face_nodes(diagonal_ref, face)], axis=0)
            face_parts.append(jnp.concatenate(split(values), axis=0))
        faces_end = starts[0][2] + up(FACE_SUB)
        for base in range(0, faces_end, 2 * LANES):
            total = None
            for face in range(6):
                more = dot_nt(
                    face_parts[face], one_hot_rows(column[face : face + 1], base, 2 * LANES)
                )
                total = more if total is None else total + more
            total = total[:FACE_ROWS] + total[FACE_ROWS:]
            for side in range(2):
                tile = total[:, side * LANES : (side + 1) * LANES]
                place_column = base + side * LANES
                if place_column < starts[0][1]:
                    face_table[:, place_column : place_column + LANES] = tile
                elif place_column < starts[0][2]:
                    dom_out[0:FACE_ROWS, :] = tile
                else:
                    sub_out[0:FACE_ROWS, :] = tile
        tiles = starts[1][2] // LANES + EDGE_TILES
        total = None
        line = iota((8, size), 0)
        for edge in range(12):
            values = all_lanes(image_ref, edge_rows(edge))
            values = jnp.where(line == 0, row_high[6 + edge : 7 + edge], values)
            values = jnp.where(line == 7, row_low[6 + edge : 7 + edge], values)
            values = jnp.concatenate([values, all_lanes(diagonal_ref, edge_rows(edge))], axis=0)
            more = scatter_two(values, column[6 + edge : 7 + edge], tiles)
            total = more if total is None else total + more
        for number in range(tiles):
            first = number * 2 * EDGE_ROWS
            tile = total[first : first + EDGE_ROWS] + total[first + EDGE_ROWS : first + 2 * EDGE_ROWS]
            place_column = number * LANES
            if place_column < starts[1][1]:
                edge_table[:, place_column : place_column + LANES] = tile
            elif place_column < starts[1][2]:
                base = FACE_ROWS + (place_column - starts[1][1]) // LANES * EDGE_ROWS
                dom_out[base : base + EDGE_ROWS, :] = tile
            else:
                base = FACE_ROWS + (place_column - starts[1][2]) // LANES * EDGE_ROWS
                sub_out[base : base + EDGE_ROWS, :] = tile
        tiles = starts[2][2] // LANES + CORNER_TILES
        total = None
        for corner in range(8):
            at = corner_place(corner)
            values = jnp.concatenate(
                [
                    all_lanes(image_ref, slice(at, at + 1)),
                    all_lanes(diagonal_ref, slice(at, at + 1)),
                    row_high[18 + corner : 19 + corner],
                    row_low[18 + corner : 19 + corner],
                    jnp.zeros((4, size), F32),
                ],
                axis=0,
            )
            more = scatter_two(values, column[18 + corner : 19 + corner], tiles)
            total = more if total is None else total + more
        for number in range(tiles):
            tile = total[number * 16 : number * 16 + 8] + total[number * 16 + 8 : number * 16 + 16]
            place_column = number * LANES
            if place_column < starts[2][1]:
                corner_table[:, place_column : place_column + LANES] = tile
            elif place_column < starts[2][2]:
                base = CORNER_BASE + (place_column - starts[2][1]) // LANES * CORNER_ROWS
                dom_out[base : base + CORNER_ROWS, :] = tile[:CORNER_ROWS]
            else:
                base = CORNER_BASE + (place_column - starts[2][2]) // LANES * CORNER_ROWS
                sub_out[base : base + CORNER_ROWS, :] = tile[:CORNER_ROWS]

    _()


def apply_and_pack(place, ids, field, metric_rows, after, table):
    nodes, size = field.shape
    count = table.shape[0]
    eye = np.eye(count, dtype=np.float32)
    grad = np.concatenate([np.kron(table, eye), np.kron(eye, table)], axis=0)
    square = (table * table).astype(np.float32)
    squares = np.concatenate([np.kron(square, eye), np.kron(eye, square)], axis=0)
    lefts = [split_np(grad), split_np(grad.T), split_np(squares.T)]

    def out(*shape, dtype=F32):
        return jax.ShapeDtypeStruct(shape, dtype)

    outs = [
        out(size // LANES, nodes, LANES),
        out(size // LANES, nodes, LANES),
        out(sum(KINDS), size, dtype=I32),
        out(FACE_ROWS, 3 * size),
        out(EDGE_ROWS, 3 * size),
        out(8, size),
        out(MESSAGE_ROWS, LANES),
        out(MESSAGE_ROWS, LANES),
    ]
    return pl.pallas_call(
        functools.partial(apply_kernel, table=table),
        in_specs=[SMEM, VMEM, VMEM, HBM, VMEM, VMEM, VMEM, ANY],
        out_specs=[VMEM] * len(outs),
        out_shape=outs,
        scratch_shapes=[
            pltpu.VMEM(metric_rows.shape, F32),
            pltpu.VMEM((nodes, size), F32),
            pltpu.SemaphoreType.DMA((14,)),
        ],
        name="apply_and_pack",
        cost_estimate=QUICK,
        compiler_params=LARGE,
    )(place, ids, field, metric_rows, *[jnp.asarray(left) for left in lefts], after)


def message_parts(kind):
    if kind == 0:
        return [0], FACE_ROWS
    if kind == 1:
        return [FACE_ROWS + q * EDGE_ROWS for q in range(EDGE_TILES)], EDGE_ROWS
    return [CORNER_BASE + q * CORNER_ROWS for q in range(CORNER_TILES)], CORNER_ROWS


def message_tiles(ref, kind):
    places, rows = message_parts(kind)
    return [ref[at : at + rows, :] for at in places]


def table_tiles(ref):
    return [ref[:, c : c + LANES] for c in range(0, ref.shape[1], LANES)]


def message_values(ref, kind, limit):
    values = jnp.concatenate(message_tiles(ref, kind), axis=1)
    first = 2 if kind == 2 else 0
    second = 3 if kind == 2 else 7
    row = (values[first : first + 1] * 16.0 + values[second : second + 1]).astype(I32)
    row = jnp.where(iota(row.shape, 1) < limit, row, -1)
    if kind == 2:
        values = jnp.concatenate([values, jnp.zeros_like(values)], axis=0)
    return values, row


def add_message(ref, tables, outs, limits):
    values, row = message_values(ref, 0, limits[0])
    parts = jnp.concatenate(split(values), axis=0)
    for base in range(0, outs[0].shape[1], 2 * LANES):
        lanes = slice(base, base + 2 * LANES)
        more = dot_nt(parts, one_hot_rows(row, base, 2 * LANES))
        outs[0][:, lanes] = tables[0][:, lanes] + more[:FACE_ROWS] + more[FACE_ROWS:]
    for kind in (1, 2):
        values, row = message_values(ref, kind, limits[kind])
        rows = values.shape[0]
        count = outs[kind].shape[1] // LANES
        total = scatter_two(values, row, count)
        for number in range(count):
            lanes = slice(number * LANES, (number + 1) * LANES)
            first = number * 2 * rows
            more = total[first : first + rows] + total[first + rows : first + 2 * rows]
            outs[kind][:, lanes] = tables[kind][:, lanes] + more


def read_message(ref, tables, back):
    for kind in range(3):
        places, rows = message_parts(kind)
        row = jnp.maximum(message_values(ref, kind, 1 << 20)[1], 0)
        tiles = table_tiles(tables[kind])
        depth = tiles[0].shape[0]
        for number, at in enumerate(places):
            spot = jnp.broadcast_to(row[:, number * LANES : (number + 1) * LANES], (depth, LANES))
            got = gather_tiles(tiles, spot & (LANES - 1), spot >> 7)
            back[at : at + rows, :] = got[:rows]


SUB_LIMITS = (FACE_SUB, EDGE_SUB, CORNER_SUB)
DOM_LIMITS = (FACE_DOM, EDGE_SUB + EZ, CORNER_SUB + 2 * EZ)


def passed_on(message, received):
    parts = [message[0:FACE_ROWS, :]]
    for kind, limit in ((1, EDGE_SUB), (2, CORNER_SUB)):
        ours, theirs = message_tiles(message, kind), message_tiles(received, kind)
        for number in range(len(ours)):
            lane = iota(ours[number].shape, 1) + number * LANES
            parts.append(jnp.where(lane < limit, ours[number], theirs[number]))
    return parts


def pass_on_kernel(message, received, *rest):
    out = rest[-1]
    at = 0
    for part in passed_on(message, received):
        out[at : at + part.shape[0], :] = part
        at += part.shape[0]


def pass_on(message, received, after=()):
    return pl.pallas_call(
        pass_on_kernel,
        in_specs=[VMEM] * 2 + [ANY] * len(after),
        out_specs=VMEM,
        out_shape=jax.ShapeDtypeStruct(message.shape, F32),
        name="pass_on",
        cost_estimate=QUICK,
        compiler_params=SMALL,
    )(message, received, *after)


def add_sub_kernel(faces, edges, corners, message, after, *outs):
    del after
    add_message(message, (faces, edges, corners), outs, SUB_LIMITS)


def add_sub(tables, message, after):
    return pl.pallas_call(
        add_sub_kernel,
        in_specs=[VMEM] * 4 + [ANY],
        out_specs=[VMEM] * 3,
        out_shape=[jax.ShapeDtypeStruct(a.shape, F32) for a in tables],
        name="add_sub",
        cost_estimate=QUICK,
        compiler_params=SMALL,
    )(*tables, message, after)


def add_dom_kernel(faces, edges, corners, message, *outs):
    add_message(message, (faces, edges, corners), outs[:3], DOM_LIMITS)
    read_message(message, outs[:3], outs[3])


def add_dom(tables, message):
    return pl.pallas_call(
        add_dom_kernel,
        in_specs=[VMEM] * 4,
        out_specs=[VMEM] * 4,
        out_shape=[jax.ShapeDtypeStruct(a.shape, F32) for a in (*tables, message)],
        name="add_dom",
        cost_estimate=QUICK,
        compiler_params=SMALL,
    )(*tables, message)


def read_sub_kernel(faces, edges, corners, message, back):
    read_message(message, (faces, edges, corners), back)


def read_sub(tables, message):
    return pl.pallas_call(
        read_sub_kernel,
        in_specs=[VMEM] * 4,
        out_specs=VMEM,
        out_shape=jax.ShapeDtypeStruct(message.shape, F32),
        name="read_sub",
        cost_estimate=QUICK,
        compiler_params=SMALL,
    )(*tables, message)


def spots(column_ref, line, rows, c, first):
    spot = jnp.broadcast_to(column_ref[line : line + 1, c * LANES : (c + 1) * LANES], (rows, LANES))
    return spot & (LANES - 1), (spot >> 7) - first


def put(ref, c, rows, values, high, count):
    line = iota(values.shape, 0)
    new = (line > 0) & (line < 7) & (high >= 0) & (high < count)
    ref[c, rows, :] = jnp.where(new, values, ref[c, rows, :])


def merge_faces(column_ref, tiles, first, image, diagonal):
    for c in range(image.shape[0]):
        for face in range(6):
            low, high = spots(column_ref, face, FACE_ROWS, c, first)
            got = gather_tiles(tiles, low, high)
            for number in range(INNER):
                rows = face_rows(face, number + 1)
                put(image, c, rows, got[number * 8 : number * 8 + 8], high[:8], len(tiles))
                put(diagonal, c, rows, got[48 + number * 8 : 56 + number * 8], high[:8], len(tiles))


def merge_edges(column_ref, tiles, first, image, diagonal):
    for c in range(image.shape[0]):
        for edge in range(12):
            low, high = spots(column_ref, 6 + edge, EDGE_ROWS, c, first)
            got = gather_tiles(tiles, low, high)
            put(image, c, edge_rows(edge), got[:8], high[:8], len(tiles))
            put(diagonal, c, edge_rows(edge), got[8:], high[:8], len(tiles))


def merge_corners(column_ref, tiles, first, image, diagonal):
    tiles = [jnp.concatenate([tile[0:2]] * 4, axis=0) for tile in tiles]
    for c in range(image.shape[0]):
        lanes = slice(c * LANES, (c + 1) * LANES)
        for group in range(2):
            spot = jnp.concatenate(
                [
                    jnp.broadcast_to(column_ref[n : n + 1, lanes], (2, LANES))
                    for n in range(18 + group * 4, 22 + group * 4)
                ],
                axis=0,
            )
            high = (spot >> 7) - first
            got = gather_tiles(tiles, spot & (LANES - 1), high)
            new = (high >= 0) & (high < len(tiles))
            for number in range(4):
                at = corner_place(group * 4 + number)
                for ref, line in ((image, 2 * number), (diagonal, 2 * number + 1)):
                    ref[c, at : at + 1, :] = jnp.where(
                        new[line : line + 1], got[line : line + 1], ref[c, at : at + 1, :]
                    )


def merge_message(column_ref, message, first_kind, image, diagonal):
    size = image.shape[0] * LANES
    starts = table_starts((3 * size, 3 * size, size))
    for kind, merge in enumerate((merge_faces, merge_edges, merge_corners)):
        first = starts[kind][first_kind] // LANES
        merge(column_ref, message_tiles(message, kind), first, image, diagonal)


def merge_own(column, tables, image, diagonal, after):
    def kernel(column, faces, edges, corners, image_in, diagonal_in, *rest):
        image, diagonal = rest[-2:]
        image[...] = image_in[...]
        diagonal[...] = diagonal_in[...]
        merge_faces(column, table_tiles(faces), 0, image, diagonal)
        merge_edges(column, table_tiles(edges), 0, image, diagonal)
        merge_corners(column, table_tiles(corners), 0, image, diagonal)

    return pl.pallas_call(
        kernel,
        in_specs=[VMEM] * 6 + [ANY] * len(after),
        out_specs=[VMEM] * 2,
        out_shape=[jax.ShapeDtypeStruct(image.shape, F32)] * 2,
        name="merge_own",
        cost_estimate=QUICK,
        compiler_params=SMALL,
    )(column, *tables, image, diagonal, *after)


def merge_dom(column, message, image, diagonal, after):
    def kernel(column, message, image_in, diagonal_in, *rest):
        image, diagonal = rest[-2:]
        image[...] = image_in[...]
        diagonal[...] = diagonal_in[...]
        merge_message(column, message, 1, image, diagonal)

    return pl.pallas_call(
        kernel,
        in_specs=[VMEM] * 4 + [ANY] * len(after),
        out_specs=[VMEM] * 2,
        out_shape=[jax.ShapeDtypeStruct(image.shape, F32)] * 2,
        name="merge_dom",
        cost_estimate=QUICK,
        compiler_params=SMALL,
    )(column, message, image, diagonal, *after)


def relax_kernel(column, message, image_in, diagonal_in, field, forcing, source, *rest):
    relaxed, *outs, image, diagonal = rest[-7:]
    nodes, size = relaxed.shape
    image[...] = image_in[...]
    diagonal[...] = diagonal_in[...]
    merge_message(column, message, 2, image, diagonal)
    for row in range(0, nodes, STRIP):
        rows = slice(row, row + STRIP)
        for c in range(size // LANES):
            lanes = slice(c * LANES, (c + 1) * LANES)
            step = (forcing[rows, lanes] - image[c, rows, :]) / diagonal[c, rows, :]
            relaxed[rows, lanes] = field[rows, lanes] + RELAX * step
    for pair in range(2):
        source_row = source[:, pair * LANES : (pair + 1) * LANES]
        pack_block(relaxed, 0, nodes, source_row, outs[2 * pair : 2 * pair + 2], 0)


def relax_and_pack(column, message, image, diagonal, field, forcing, source, after):
    nodes, size = field.shape
    leaving = jax.ShapeDtypeStruct((nodes // 2, LANES), F32)
    return pl.pallas_call(
        relax_kernel,
        in_specs=[VMEM] * 7 + [ANY] * len(after),
        out_specs=[VMEM] * 5,
        out_shape=[jax.ShapeDtypeStruct((nodes, size), F32)] + [leaving] * 4,
        scratch_shapes=[pltpu.VMEM((size // LANES, nodes, LANES), F32)] * 2,
        name="relax_and_pack",
        cost_estimate=QUICK,
        compiler_params=SMALL,
    )(column, message, image, diagonal, field, forcing, source, *after)


def shifted(value, axis, steps):
    count = lax.axis_size(axis)
    return lax.ppermute(value, axis, [(i, (i + steps) % count) for i in range(count)])


def swapped(to_previous, to_next, axis):
    return shifted(to_next, axis, 1), shifted(to_previous, axis, -1)


def on_device(solution, forcing, metric, entity_ids, new_owner):
    size = solution.shape[-1]
    place = devices()
    table = derivative_table(solution.shape[0] - 1)
    field = solution.reshape(-1, size)
    metric_rows = pltpu.with_memory_space_constraint(metric.reshape(-1, size), pltpu.HBM)
    components = metric.shape[0]
    block = metric_rows.shape[0] // components
    source, landing, *messages = plan_and_pack(place, new_owner.reshape(1, size), metric_rows, block)
    sub_early = swapped(*messages, "sub")
    messages = pack(source, metric_rows, 0, DOM_EARLY, 0, block, (landing,), "pack_dom")
    dom_early = swapped(*messages, "dom")
    image, diagonal, column, *tables, dom, sub = apply_and_pack(
        place, entity_ids, field, metric_rows, messages[0], table
    )
    got_sub = shifted(sub, "sub", 1)
    messages = pack(
        source, metric_rows, SUB_EARLY, components - SUB_EARLY, 1, block, (sub,), "pack_sub_late"
    )
    sub_late = swapped(*messages, "sub")
    dom = pass_on(dom, got_sub, (*sub_early, messages[0]))
    got_dom = shifted(dom, "dom", 1)
    tables = add_sub(tables, got_sub, dom)
    *tables, dom_back = add_dom(tables, got_dom)
    back_dom = shifted(dom_back, "dom", -1)
    sub_back = read_sub(tables, got_sub)
    image, diagonal = merge_own(column, tables, image, diagonal, (dom_back, *dom_early))
    sub_back = pass_on(sub_back, back_dom)
    back_sub = shifted(sub_back, "sub", -1)
    image, diagonal = merge_dom(column, back_dom, image, diagonal, sub_late)
    dom_moves, sub_moves = (dom_early, ()), (sub_early, sub_late)
    moved, token = land_metric(
        landing, metric_rows, dom_moves, sub_moves, 0, SUB_EARLY, block, None, image, "land_early"
    )
    relaxed, *leaving = relax_and_pack(
        column, back_sub, image, diagonal, field, forcing.reshape(-1, size), source, (token,)
    )
    got_sub = swapped(*leaving[2:], "sub")
    got_dom = swapped(*leaving[:2], "dom")
    moved, token = land_metric(
        landing, metric_rows, dom_moves, sub_moves, SUB_EARLY, components - SUB_EARLY, block, moved,
        leaving[0], "land_late",
    )
    smoothed = land_field(landing, relaxed, got_dom + got_sub, token)
    return smoothed.reshape(solution.shape), moved.reshape(metric.shape)


def solution(mesh):
    placed = (
        P(None, None, None, ("dom", "sub")),
        P(None, None, None, ("dom", "sub")),
        P(None, None, None, None, ("dom", "sub")),
        P(None, ("dom", "sub")),
        P(("dom", "sub")),
    )
    return jax.shard_map(
        on_device,
        mesh=mesh,
        in_specs=placed,
        out_specs=(P(None, None, None, ("dom", "sub")), P(None, None, None, None, ("dom", "sub"))),
        check_vma=False,
    )
```

```python
import functools

import jax
import jax.numpy as jnp
import numpy as np
from jax import lax
from jax.experimental import pallas as pl
from jax.experimental.pallas import tpu as pltpu
from jax.sharding import PartitionSpec as P

EX = 4
EY = 4
EZ = 32
MOVE = 64
RELAX = 0.6
LANES = 128
INNER = 6
SUB_EARLY = 5
DOM_EARLY = 7

NT = (((1,), (1,)), ((), ()))
VMEM = pl.BlockSpec(memory_space=pltpu.VMEM)
ANY = pl.BlockSpec(memory_space=pl.ANY)
SMEM = pl.BlockSpec(memory_space=pltpu.SMEM)
QUICK = pl.CostEstimate(flops=1000, bytes_accessed=1000, transcendentals=0)
HBM = pl.BlockSpec(memory_space=pltpu.HBM)
LARGE = pltpu.CompilerParams(vmem_limit_bytes=24 << 20)
SMALL = pltpu.CompilerParams(vmem_limit_bytes=16 << 20)
STRIP = 256
F32 = jnp.float32
BF16 = jnp.bfloat16
I32 = jnp.int32


def derivative_table(order):
    count = order + 1
    points = -np.cos(np.pi * np.arange(count) / order)
    legendre = np.zeros((count, count))
    for sweep in range(80):
        legendre[:, 0] = 1.0
        legendre[:, 1] = points
        for degree in range(2, count):
            legendre[:, degree] = (
                (2 * degree - 1) * points * legendre[:, degree - 1]
                - (degree - 1) * legendre[:, degree - 2]
            ) / degree
        points = points - (points * legendre[:, order] - legendre[:, order - 1]) / (
            count * legendre[:, order]
        )
    legendre[:, 0] = 1.0
    legendre[:, 1] = points
    for degree in range(2, count):
        legendre[:, degree] = (
            (2 * degree - 1) * points * legendre[:, degree - 1]
            - (degree - 1) * legendre[:, degree - 2]
        ) / degree
    values = legendre[:, order]
    identity = np.eye(count)
    spread = points[:, None] - points[None, :] + identity
    table = values[:, None] / values[None, :] / spread
    table = table * (1.0 - identity)
    table[0, 0] = -order * count / 4.0
    table[order, order] = order * count / 4.0
    return table.astype(np.float32)


def split_np(matrix):
    high = matrix.astype(jnp.bfloat16).astype(np.float32)
    low = (matrix - high).astype(jnp.bfloat16)
    return np.concatenate([high.astype(jnp.bfloat16), low, high.astype(jnp.bfloat16)], axis=1)


def split(values):
    high = values.astype(BF16)
    low = (values - high.astype(F32)).astype(BF16)
    return high, low


def triple(values):
    high, low = split(values)
    return jnp.concatenate([high, high, low], axis=0)


def dot(left, right):
    return jnp.dot(left, right, preferred_element_type=F32)


def dot_nt(left, right):
    return lax.dot_general(left, right, NT, preferred_element_type=F32)


def iota(shape, dim):
    return lax.broadcasted_iota(I32, shape, dim)


def one_hot_rows(index_row, start, count):
    size = index_row.shape[1]
    out = []
    for base in range(0, count, LANES):
        local = (index_row - (start + base)).astype(BF16)
        rows = iota((LANES, size), 0).astype(BF16)
        out.append(
            jnp.where(rows == local, jnp.ones((LANES, size), BF16), jnp.zeros((LANES, size), BF16))
        )
    return out[0] if len(out) == 1 else jnp.concatenate(out, axis=0)


def exclusive_count(masks):
    size = masks.shape[1]
    upper = jnp.where(iota((size, size), 0) < iota((size, size), 1), 1.0, 0.0).astype(BF16)
    return dot(masks.astype(BF16), upper)


def gather_tiles(tiles, low, high):
    out = None
    for number, tile in enumerate(tiles):
        got = jnp.take_along_axis(tile, low, axis=1)
        out = got if out is None else jnp.where(high == number, got, out)
    return out


def devices():
    dom_count = lax.axis_size("dom")
    sub_count = lax.axis_size("sub")
    dom = lax.axis_index("dom")
    sub = lax.axis_index("sub")
    dom_ahead = lax.rem(dom + 1, dom_count)
    dom_behind = lax.rem(dom + dom_count - 1, dom_count)
    sub_ahead = lax.rem(sub + 1, sub_count)
    sub_behind = lax.rem(sub + sub_count - 1, sub_count)
    return jnp.stack(
        [
            dom_behind * sub_count + sub,
            dom_ahead * sub_count + sub,
            dom * sub_count + sub_behind,
            dom * sub_count + sub_ahead,
            dom * sub_count + sub,
            dom_ahead * sub_count + sub_ahead,
        ]
    ).astype(I32)


def pack_pair(top, bottom):
    left = iota(top.shape, 1) < MOVE
    first = jnp.where(left, top, pltpu.roll(bottom, MOVE, 1))
    second = jnp.where(left, pltpu.roll(top, MOVE, 1), bottom)
    return first, second


def pick_columns(ref, rows, low, high):
    tiles = [ref[rows, c : c + LANES] for c in range(0, ref.shape[1], LANES)]
    return gather_tiles(tiles, low, high)


def pack_block(ref, start, block, source_row, outs, to):
    half = block // 2
    source = jnp.broadcast_to(source_row, (half, LANES))
    low, high = source & (LANES - 1), source >> 7
    top = pick_columns(ref, slice(start, start + half), low, high)
    bottom = pick_columns(ref, slice(start + half, start + block), low, high)
    for out, message in zip(outs, pack_pair(top, bottom)):
        out[to : to + half, :] = message


def arrival_spots(landing_row):
    return jnp.concatenate([one_hot_rows(landing_row, 0, 4 * MOVE)] * 3, axis=0)


def split_exactly(values):
    parts = []
    for _ in range(3):
        parts.append(values.astype(BF16))
        values = values - parts[-1].astype(F32)
    return jnp.concatenate(parts, axis=1)


def land_block(ref, start, block, landing_row, spots, messages, ats, out, to):
    land_strips(ref, start, block // 2, 0, block // 2, landing_row, spots, messages, ats, out, to)


def land_strips(ref, start, half, from_row, to_row, landing_row, spots, messages, ats, out, to):
    rows = to_row - from_row
    parts = [message[at + from_row : at + to_row, :] for message, at in zip(messages, ats)]
    pairs = [pack_pair(parts[0], parts[1]), pack_pair(parts[2], parts[3])]
    stays = jnp.broadcast_to(landing_row < 0, (rows, landing_row.shape[1]))
    for side in range(2):
        arrived = jnp.concatenate([pairs[0][side], pairs[1][side]], axis=1)
        got = dot(split_exactly(arrived), spots)
        first = side * half + from_row
        held = ref[start + first : start + first + rows, :]
        out[to + first : to + first + rows, :] = jnp.where(stays, held, got)


def move_plan(owner, place):
    size = owner.shape[1]
    own = place[4]
    line = iota((8, size), 0)
    target = jnp.where(
        line == 0,
        place[0],
        jnp.where(line == 1, place[1], jnp.where(line == 2, place[2], place[3])),
    )
    nobody = jnp.broadcast_to(owner, (8, size))
    away = nobody != own
    masks = jnp.where(away & (((nobody == target) & (line < 4)) | (line == 4)), 1.0, 0.0)
    ranks = exclusive_count(masks)
    counts = jnp.sum(masks, axis=1, keepdims=True)
    hole = ranks[4:5]
    gone = masks[4:5] > 0.5
    column = jnp.full((1, size), -1.0, F32)
    landing = jnp.full((1, size), -1.0, F32)
    offset = jnp.zeros((1, 1), F32)
    for way in range(4):
        column = jnp.where(masks[way : way + 1] > 0.5, way * MOVE + ranks[way : way + 1], column)
        ahead = hole - offset
        here = gone & (ahead >= 0.0) & (ahead < counts[way : way + 1])
        landing = jnp.where(here, way * MOVE + ahead, landing)
        offset = offset + counts[way : way + 1]
    spots = one_hot_rows(column.astype(I32), 0, 4 * MOVE)
    element = iota((8, size), 1)
    parts = jnp.where(iota((8, size), 0) == 0, element >> 4, element & 15)
    found = dot_nt(parts.astype(BF16), spots)
    source = found[0:1] * 16.0 + found[1:2]
    return source.astype(I32), landing.astype(I32)


def fetch(source, target, sems, number, start, count, to):
    return pltpu.make_async_copy(
        source.at[pl.ds(start, count), :], target.at[pl.ds(to, count), :], sems.at[number]
    )


def send_part(held, first, number, source, outs, block):
    pack_block(held, (first + number) * block, block, source, outs, number * block // 2)


def plan_and_pack_kernel(
    place, owner_hbm, metric, source_ref, landing_ref, first_out, second_out, held, sems, owner,
    owner_sem, *, block,
):
    copy = pltpu.make_async_copy(owner_hbm, owner, owner_sem)
    copy.start()
    count = held.shape[0] // block
    copies = [fetch(metric, held, sems, c, c * block, block, c * block) for c in range(count)]
    for part in copies:
        part.start()
    copy.wait()
    source, landing = move_plan(owner[...], place)
    source_ref[...] = source
    landing_ref[...] = landing
    for number, part in enumerate(copies):
        part.wait()
        if number < SUB_EARLY:
            send_part(held, 0, number, source[:, LANES:], (first_out, second_out), block)


def pack_kernel(source, held, *rest, first, pair, block):
    outs = rest[-2:]
    lanes = slice(pair * LANES, (pair + 1) * LANES)
    for number in range(outs[0].shape[0] * 2 // block):
        send_part(held, first, number, source[:, lanes], outs, block)


def sent_shapes(count, block):
    return [jax.ShapeDtypeStruct((count * block // 2, LANES), F32)] * 2


def plan_and_pack(place, owner, metric_rows, block):
    rows, size = metric_rows.shape
    outs = sent_shapes(SUB_EARLY, block) + [jax.ShapeDtypeStruct((rows, size), F32)]
    plan = [jax.ShapeDtypeStruct((1, 4 * MOVE), I32), jax.ShapeDtypeStruct((1, size), I32)]
    return pl.pallas_call(
        functools.partial(plan_and_pack_kernel, block=block),
        in_specs=[SMEM, HBM, HBM],
        out_specs=[VMEM] * 5,
        out_shape=plan + outs,
        scratch_shapes=[
            pltpu.SemaphoreType.DMA((rows // block,)),
            pltpu.VMEM((1, size), I32),
            pltpu.SemaphoreType.DMA,
        ],
        name="plan_and_pack",
        cost_estimate=QUICK,
        compiler_params=LARGE,
    )(place, owner, metric_rows)


def pack(source, metric_rows, first, count, pair, block, after, name):
    outs = sent_shapes(count, block)
    return pl.pallas_call(
        functools.partial(pack_kernel, first=first, pair=pair, block=block),
        in_specs=[VMEM, VMEM] + [ANY] * len(after),
        out_specs=[VMEM] * 2,
        out_shape=outs,
        name=name,
        cost_estimate=QUICK,
        compiler_params=LARGE,
    )(source, metric_rows, *after)


def land_metric_kernel(landing, held, *rest, first, block, spots):
    *messages, out, token, ready, sems = rest
    token[...] = jnp.zeros_like(token)
    columns = arrival_spots(landing[...])
    copies = []
    for number in range(ready.shape[0] // block):
        start = number * block
        source = (first + number) * block
        parts, at = spots[number]
        land_block(
            held, source, block, landing[...], columns, [messages[k] for k in parts], at, ready, start
        )
        copies.append(fetch(ready, out, sems, number, start, block, source))
        copies[-1].start()
    for copy in copies:
        copy.wait()


def land_metric(landing, metric_rows, dom, sub, first, count, block, before, after, name):
    size = metric_rows.shape[1]
    messages, spots = [], []
    for number in range(first, first + count):
        parts, ats = [], None
        for (early, late), limit in ((dom, DOM_EARLY), (sub, SUB_EARLY)):
            chosen, local = (early, number) if number < limit else (late, number - limit)
            for message in chosen:
                known = [k for k, other in enumerate(messages) if other is message]
                if not known:
                    messages.append(message)
                parts.append(known[0] if known else len(messages) - 1)
            ats = (ats or []) + [local * block // 2] * 2
        spots.append((parts, ats))
    operands = [landing, metric_rows, *messages, after]
    specs = [VMEM, VMEM] + [VMEM] * len(messages) + [ANY]
    aliases = {}
    if before is not None:
        aliases = {len(operands): 0}
        operands.append(before)
        specs.append(HBM)
    return pl.pallas_call(
        functools.partial(land_metric_kernel, first=first, block=block, spots=spots),
        in_specs=specs,
        out_specs=[HBM, VMEM],
        out_shape=[
            jax.ShapeDtypeStruct(metric_rows.shape, F32),
            jax.ShapeDtypeStruct((8, LANES), F32),
        ],
        scratch_shapes=[
            pltpu.VMEM((count * block, size), F32),
            pltpu.SemaphoreType.DMA((count,)),
        ],
        input_output_aliases=aliases,
        name=name,
        cost_estimate=QUICK,
        compiler_params=LARGE,
    )(*operands)


def land_field_kernel(landing, relaxed, first, second, third, fourth, after, out, ready, sems):
    del after
    rows = relaxed.shape[0]
    piece = rows // 8
    half = rows // 2
    messages = (first, second, third, fourth)
    copies = []
    columns = arrival_spots(landing[...])
    for row in range(0, half, piece):
        land_strips(
            relaxed, 0, half, row, row + piece, landing[...], columns, messages, [0] * 4, ready, 0
        )
        for side in range(2):
            copies.append(fetch(ready, out, sems, len(copies), side * half + row, piece, side * half + row))
            copies[-1].start()
    for copy in copies:
        copy.wait()


def land_field(landing, relaxed, arrived, after):
    count = 8
    return pl.pallas_call(
        land_field_kernel,
        in_specs=[VMEM] * 6 + [ANY],
        out_specs=HBM,
        out_shape=jax.ShapeDtypeStruct(relaxed.shape, F32),
        scratch_shapes=[pltpu.VMEM(relaxed.shape, F32), pltpu.SemaphoreType.DMA((count,))],
        name="land_field",
        cost_estimate=QUICK,
        compiler_params=SMALL,
    )(landing, relaxed, *arrived, after)


FACE_DOM = EY * EZ
FACE_SUB = EX * EZ
EDGE_DOM = EZ * (4 * EY - 1)
EDGE_SUB = EZ * (4 * EX - 1)
CORNER_DOM = EZ * (4 * EY - 2)
CORNER_SUB = EZ * (4 * EX - 2)


def up(count):
    return -(-count // LANES) * LANES


EDGE_TILES = up(EDGE_DOM) // LANES
CORNER_TILES = up(CORNER_DOM) // LANES


def table_starts(hosted):
    edge_dom, edge_sub = hosted[1], hosted[1] + EDGE_TILES * LANES
    corner_dom, corner_sub = hosted[2], hosted[2] + CORNER_TILES * LANES
    return (
        (0, hosted[0], hosted[0] + up(FACE_DOM), hosted[0]),
        (0, edge_dom, edge_sub, edge_sub + EDGE_SUB),
        (0, corner_dom, corner_sub, corner_sub + CORNER_SUB),
    )


KINDS = (6, 12, 8)
FACE_ROWS = 2 * INNER * 8
EDGE_ROWS = 16
CORNER_ROWS = 4
CORNER_BASE = FACE_ROWS + EDGE_TILES * EDGE_ROWS
MESSAGE_ROWS = CORNER_BASE + CORNER_TILES * CORNER_ROWS


def shared_columns(ids, place, hosted):
    lines, size = ids.shape
    line = iota((lines, 1), 0)
    per = jnp.where(line < 6, hosted[0], jnp.where(line < 18, hosted[1], hosted[2]))
    owns, rows, masks = [], jnp.zeros((lines, size), I32), []
    for device in (place[4], place[1], place[3], place[5]):
        local = ids - device * per
        inside = (local >= 0) & (local < per)
        rows = jnp.where(inside, local, rows)
        owns.append(inside)
    starts = table_starts(hosted)
    lower = (iota((lines, lines), 1) < iota((lines, lines), 0)) & (
        (iota((lines, lines), 0) < 6) == (iota((lines, lines), 1) < 6)
    )
    lower = lower & ((iota((lines, lines), 0) < 18) == (iota((lines, lines), 1) < 18))
    lower = jnp.where(lower, 1.0, 0.0).astype(BF16)
    column = rows
    marks = jnp.concatenate([jnp.where(inside, 1.0, 0.0) for inside in owns[1:]], axis=0)
    ranks = exclusive_count(marks)
    for number in range(3):
        inside = owns[1 + number]
        mark = marks[number * lines : (number + 1) * lines]
        above = jnp.sum(dot(lower, mark.astype(BF16)), axis=1, keepdims=True)
        rank = (ranks[number * lines : (number + 1) * lines] + above).astype(I32)
        base = jnp.where(
            line < 6,
            starts[0][1 + number],
            jnp.where(line < 18, starts[1][1 + number], starts[2][1 + number]),
        )
        column = jnp.where(inside, base + rank, column)
    return column, rows


def scatter_two(parts, column_row, tiles):
    high, low = split(parts)
    both = jnp.concatenate([high, low], axis=0)
    size = column_row.shape[1]
    tile = jnp.broadcast_to((column_row >> 7).astype(BF16), both.shape)
    zero = jnp.zeros(both.shape, BF16)
    left = jnp.concatenate([jnp.where(tile == h, both, zero) for h in range(tiles)], axis=0)
    return dot_nt(left, one_hot_rows(column_row & (LANES - 1), 0, LANES))


def face_rows(face, inner):
    end = 7 * (face % 2)
    if face < 2:
        return pl.ds(end * 64 + inner * 8, 8)
    if face < 4:
        return pl.ds(inner * 64 + end * 8, 8)
    return pl.ds(inner * 64 + end, 8, stride=8)


def all_lanes(ref, rows):
    return jnp.concatenate([ref[c, rows, :] for c in range(ref.shape[0])], axis=1)


def face_nodes(ref, face):
    return jnp.concatenate(
        [all_lanes(ref, face_rows(face, inner)) for inner in range(1, INNER + 1)], axis=0
    )


def edge_place(edge):
    ends = (7 * (edge % 4 // 2), 7 * (edge % 2))
    if edge < 4:
        return ends[0] * 8 + ends[1], 64
    if edge < 8:
        return ends[0] * 64 + ends[1], 8
    return ends[0] * 64 + ends[1] * 8, 1


def edge_rows(edge):
    start, stride = edge_place(edge)
    return pl.ds(start, 8) if stride == 1 else pl.ds(start, 8, stride=stride)


def corner_place(corner):
    return (corner // 4) * 448 + (corner // 2 % 2) * 56 + (corner % 2) * 7


def apply_kernel(
    place,
    ids,
    solution,
    metric,
    grad_left,
    image_left,
    square_left,
    after,
    image_ref,
    diagonal_ref,
    column_ref,
    face_table,
    edge_table,
    corner_table,
    dom_out,
    sub_out,
    flux_r,
    *,
    table,
):
    del after
    size = image_ref.shape[0] * LANES
    count = table.shape[0]
    plane = count * count
    nodes = count * plane
    width = 2 * LANES
    node = iota((count, width), 0)
    ends = (0, count - 1)
    end_value = {0: float(table[0, 0]), count - 1: float(table[count - 1, count - 1])}
    ends_k = jnp.where(
        node == 0, end_value[0], jnp.where(node == count - 1, end_value[count - 1], 0.0)
    )
    for i in range(count):
        rows = slice(i * plane, (i + 1) * plane)
        for base in range(0, size, width):
            lanes = slice(base, base + width)

            grads = dot(grad_left[...], triple(solution[rows, lanes]))
            fluxes, weights = [[], []], [[], []]
            strip = 2 * count
            for start in range(0, plane, strip):
                at = slice(start, start + strip)
                part = [
                    metric[c * nodes + i * plane + start : c * nodes + i * plane + start + strip, lanes]
                    for c in range(6)
                ]
                grad_r = sum(
                    float(table[i, q])
                    * solution[q * plane + start : q * plane + start + strip, lanes]
                    for q in range(count)
                )
                grad_s, grad_t = grads[start : start + strip], grads[plane + start : plane + start + strip]
                flux_r[i * plane + start : i * plane + start + strip, lanes] = (
                    part[0] * grad_r + part[3] * grad_s + part[4] * grad_t
                )
                fluxes[0].append(split(part[3] * grad_r + part[1] * grad_s + part[5] * grad_t))
                fluxes[1].append(split(part[4] * grad_r + part[5] * grad_s + part[2] * grad_t))
                weights[0].append(split(part[1]))
                weights[1].append(split(part[2]))

            def stacked(pieces):
                pieces = pieces[0] + pieces[1]
                high = [piece[0] for piece in pieces]
                return jnp.concatenate(high + high + [piece[1] for piece in pieces], axis=0)

            image = dot(image_left[...], stacked(fluxes))
            diagonal = dot(square_left[...], stacked(weights))
            for j in range(count):
                lines = slice(j * count, (j + 1) * count)
                first = i * plane + j * count

                def here(c):
                    return metric[c * nodes + first : c * nodes + first + count, lanes]

                mass = here(6)
                total = diagonal[lines] + mass
                if j in ends:
                    total = total + here(5) * (ends_k * (2.0 * end_value[j]))
                if i in ends:
                    total = total + here(4) * (ends_k * (2.0 * end_value[i]))
                    if j in ends:
                        total = total + here(3) * (2.0 * end_value[i] * end_value[j])
                value = image[lines] + mass * solution[first : first + count, lanes]
                for c in range(width // LANES):
                    side = slice(c * LANES, (c + 1) * LANES)
                    image_ref[base // LANES + c, first : first + count, :] = value[:, side]
                    diagonal_ref[base // LANES + c, first : first + count, :] = total[:, side]
    for i in range(count):
        rows = slice(i * plane, (i + 1) * plane)
        for c in range(size // LANES):
            lanes = slice(c * LANES, (c + 1) * LANES)
            image_ref[c, rows, :] += sum(
                float(table[a, i]) * flux_r[a * plane : (a + 1) * plane, lanes]
                for a in range(count)
            )
            diagonal_ref[c, rows, :] += sum(
                float(table[a, i] * table[a, i]) * metric[a * plane : (a + 1) * plane, lanes]
                for a in range(count)
            )

    def _():
        hosted = (3 * size, 3 * size, size)
        starts = table_starts(hosted)
        column, row = shared_columns(ids[...], place, hosted)
        column_ref[...] = column
        row_high = (row >> 4).astype(F32)
        row_low = (row & 15).astype(F32)
        face_parts = []
        spot = iota((48, size), 0)
        for face in range(6):
            values = face_nodes(image_ref, face)
            values = jnp.where(spot == 0, row_high[face : face + 1], values)
            values = jnp.where(spot == 7, row_low[face : face + 1], values)
            values = jnp.concatenate([values, face_nodes(diagonal_ref, face)], axis=0)
            face_parts.append(jnp.concatenate(split(values), axis=0))
        faces_end = starts[0][2] + up(FACE_SUB)
        for base in range(0, faces_end, 2 * LANES):
            total = None
            for face in range(6):
                more = dot_nt(
                    face_parts[face], one_hot_rows(column[face : face + 1], base, 2 * LANES)
                )
                total = more if total is None else total + more
            total = total[:FACE_ROWS] + total[FACE_ROWS:]
            for side in range(2):
                tile = total[:, side * LANES : (side + 1) * LANES]
                place_column = base + side * LANES
                if place_column < starts[0][1]:
                    face_table[:, place_column : place_column + LANES] = tile
                elif place_column < starts[0][2]:
                    dom_out[0:FACE_ROWS, :] = tile
                else:
                    sub_out[0:FACE_ROWS, :] = tile
        tiles = starts[1][2] // LANES + EDGE_TILES
        total = None
        line = iota((8, size), 0)
        for edge in range(12):
            values = all_lanes(image_ref, edge_rows(edge))
            values = jnp.where(line == 0, row_high[6 + edge : 7 + edge], values)
            values = jnp.where(line == 7, row_low[6 + edge : 7 + edge], values)
            values = jnp.concatenate([values, all_lanes(diagonal_ref, edge_rows(edge))], axis=0)
            more = scatter_two(values, column[6 + edge : 7 + edge], tiles)
            total = more if total is None else total + more
        for number in range(tiles):
            first = number * 2 * EDGE_ROWS
            tile = total[first : first + EDGE_ROWS] + total[first + EDGE_ROWS : first + 2 * EDGE_ROWS]
            place_column = number * LANES
            if place_column < starts[1][1]:
                edge_table[:, place_column : place_column + LANES] = tile
            elif place_column < starts[1][2]:
                base = FACE_ROWS + (place_column - starts[1][1]) // LANES * EDGE_ROWS
                dom_out[base : base + EDGE_ROWS, :] = tile
            else:
                base = FACE_ROWS + (place_column - starts[1][2]) // LANES * EDGE_ROWS
                sub_out[base : base + EDGE_ROWS, :] = tile
        tiles = starts[2][2] // LANES + CORNER_TILES
        total = None
        for corner in range(8):
            at = corner_place(corner)
            values = jnp.concatenate(
                [
                    all_lanes(image_ref, slice(at, at + 1)),
                    all_lanes(diagonal_ref, slice(at, at + 1)),
                    row_high[18 + corner : 19 + corner],
                    row_low[18 + corner : 19 + corner],
                    jnp.zeros((4, size), F32),
                ],
                axis=0,
            )
            more = scatter_two(values, column[18 + corner : 19 + corner], tiles)
            total = more if total is None else total + more
        for number in range(tiles):
            tile = total[number * 16 : number * 16 + 8] + total[number * 16 + 8 : number * 16 + 16]
            place_column = number * LANES
            if place_column < starts[2][1]:
                corner_table[:, place_column : place_column + LANES] = tile
            elif place_column < starts[2][2]:
                base = CORNER_BASE + (place_column - starts[2][1]) // LANES * CORNER_ROWS
                dom_out[base : base + CORNER_ROWS, :] = tile[:CORNER_ROWS]
            else:
                base = CORNER_BASE + (place_column - starts[2][2]) // LANES * CORNER_ROWS
                sub_out[base : base + CORNER_ROWS, :] = tile[:CORNER_ROWS]

    _()


def apply_and_pack(place, ids, field, metric_rows, after, table):
    nodes, size = field.shape
    count = table.shape[0]
    eye = np.eye(count, dtype=np.float32)
    grad = np.concatenate([np.kron(table, eye), np.kron(eye, table)], axis=0)
    square = (table * table).astype(np.float32)
    squares = np.concatenate([np.kron(square, eye), np.kron(eye, square)], axis=0)
    lefts = [split_np(grad), split_np(grad.T), split_np(squares.T)]

    def out(*shape, dtype=F32):
        return jax.ShapeDtypeStruct(shape, dtype)

    outs = [
        out(size // LANES, nodes, LANES),
        out(size // LANES, nodes, LANES),
        out(sum(KINDS), size, dtype=I32),
        out(FACE_ROWS, 3 * size),
        out(EDGE_ROWS, 3 * size),
        out(8, size),
        out(MESSAGE_ROWS, LANES),
        out(MESSAGE_ROWS, LANES),
    ]
    return pl.pallas_call(
        functools.partial(apply_kernel, table=table),
        in_specs=[SMEM] + [VMEM] * 6 + [ANY],
        out_specs=[VMEM] * len(outs),
        out_shape=outs,
        scratch_shapes=[
            pltpu.VMEM((nodes, size), F32),
        ],
        name="apply_and_pack",
        cost_estimate=QUICK,
        compiler_params=LARGE,
    )(place, ids, field, metric_rows, *[jnp.asarray(left) for left in lefts], after)


def message_parts(kind):
    if kind == 0:
        return [0], FACE_ROWS
    if kind == 1:
        return [FACE_ROWS + q * EDGE_ROWS for q in range(EDGE_TILES)], EDGE_ROWS
    return [CORNER_BASE + q * CORNER_ROWS for q in range(CORNER_TILES)], CORNER_ROWS


def message_tiles(ref, kind):
    places, rows = message_parts(kind)
    return [ref[at : at + rows, :] for at in places]


def table_tiles(ref):
    return [ref[:, c : c + LANES] for c in range(0, ref.shape[1], LANES)]


def message_values(ref, kind, limit):
    values = jnp.concatenate(message_tiles(ref, kind), axis=1)
    first = 2 if kind == 2 else 0
    second = 3 if kind == 2 else 7
    row = (values[first : first + 1] * 16.0 + values[second : second + 1]).astype(I32)
    row = jnp.where(iota(row.shape, 1) < limit, row, -1)
    if kind == 2:
        values = jnp.concatenate([values, jnp.zeros_like(values)], axis=0)
    return values, row


def add_message(ref, tables, outs, limits):
    values, row = message_values(ref, 0, limits[0])
    parts = jnp.concatenate(split(values), axis=0)
    for base in range(0, outs[0].shape[1], 2 * LANES):
        lanes = slice(base, base + 2 * LANES)
        more = dot_nt(parts, one_hot_rows(row, base, 2 * LANES))
        outs[0][:, lanes] = tables[0][:, lanes] + more[:FACE_ROWS] + more[FACE_ROWS:]
    for kind in (1, 2):
        values, row = message_values(ref, kind, limits[kind])
        rows = values.shape[0]
        count = outs[kind].shape[1] // LANES
        total = scatter_two(values, row, count)
        for number in range(count):
            lanes = slice(number * LANES, (number + 1) * LANES)
            first = number * 2 * rows
            more = total[first : first + rows] + total[first + rows : first + 2 * rows]
            outs[kind][:, lanes] = tables[kind][:, lanes] + more


def read_message(ref, tables, back):
    for kind in range(3):
        places, rows = message_parts(kind)
        row = jnp.maximum(message_values(ref, kind, 1 << 20)[1], 0)
        tiles = table_tiles(tables[kind])
        depth = tiles[0].shape[0]
        for number, at in enumerate(places):
            spot = jnp.broadcast_to(row[:, number * LANES : (number + 1) * LANES], (depth, LANES))
            got = gather_tiles(tiles, spot & (LANES - 1), spot >> 7)
            back[at : at + rows, :] = got[:rows]


SUB_LIMITS = (FACE_SUB, EDGE_SUB, CORNER_SUB)
DOM_LIMITS = (FACE_DOM, EDGE_SUB + EZ, CORNER_SUB + 2 * EZ)


def passed_on(message, received):
    parts = [message[0:FACE_ROWS, :]]
    for kind, limit in ((1, EDGE_SUB), (2, CORNER_SUB)):
        ours, theirs = message_tiles(message, kind), message_tiles(received, kind)
        for number in range(len(ours)):
            lane = iota(ours[number].shape, 1) + number * LANES
            parts.append(jnp.where(lane < limit, ours[number], theirs[number]))
    return parts


def pass_on_kernel(message, received, *rest):
    out = rest[-1]
    at = 0
    for part in passed_on(message, received):
        out[at : at + part.shape[0], :] = part
        at += part.shape[0]


def pass_on(message, received, after=()):
    return pl.pallas_call(
        pass_on_kernel,
        in_specs=[VMEM] * 2 + [ANY] * len(after),
        out_specs=VMEM,
        out_shape=jax.ShapeDtypeStruct(message.shape, F32),
        name="pass_on",
        cost_estimate=QUICK,
        compiler_params=SMALL,
    )(message, received, *after)


def add_sub_kernel(faces, edges, corners, message, after, *outs):
    del after
    add_message(message, (faces, edges, corners), outs, SUB_LIMITS)


def add_sub(tables, message, after):
    return pl.pallas_call(
        add_sub_kernel,
        in_specs=[VMEM] * 4 + [ANY],
        out_specs=[VMEM] * 3,
        out_shape=[jax.ShapeDtypeStruct(a.shape, F32) for a in tables],
        name="add_sub",
        cost_estimate=QUICK,
        compiler_params=SMALL,
    )(*tables, message, after)


def add_dom_kernel(faces, edges, corners, message, *outs):
    add_message(message, (faces, edges, corners), outs[:3], DOM_LIMITS)
    read_message(message, outs[:3], outs[3])


def add_dom(tables, message):
    return pl.pallas_call(
        add_dom_kernel,
        in_specs=[VMEM] * 4,
        out_specs=[VMEM] * 4,
        out_shape=[jax.ShapeDtypeStruct(a.shape, F32) for a in (*tables, message)],
        name="add_dom",
        cost_estimate=QUICK,
        compiler_params=SMALL,
    )(*tables, message)


def read_sub_kernel(faces, edges, corners, message, back):
    read_message(message, (faces, edges, corners), back)


def read_sub(tables, message):
    return pl.pallas_call(
        read_sub_kernel,
        in_specs=[VMEM] * 4,
        out_specs=VMEM,
        out_shape=jax.ShapeDtypeStruct(message.shape, F32),
        name="read_sub",
        cost_estimate=QUICK,
        compiler_params=SMALL,
    )(*tables, message)


def spots(column_ref, line, rows, c, first):
    spot = jnp.broadcast_to(column_ref[line : line + 1, c * LANES : (c + 1) * LANES], (rows, LANES))
    return spot & (LANES - 1), (spot >> 7) - first


def put(ref, c, rows, values, high, count):
    line = iota(values.shape, 0)
    new = (line > 0) & (line < 7) & (high >= 0) & (high < count)
    ref[c, rows, :] = jnp.where(new, values, ref[c, rows, :])


def merge_faces(column_ref, tiles, first, image, diagonal):
    for c in range(image.shape[0]):
        for face in range(6):
            low, high = spots(column_ref, face, FACE_ROWS, c, first)
            got = gather_tiles(tiles, low, high)
            for number in range(INNER):
                rows = face_rows(face, number + 1)
                put(image, c, rows, got[number * 8 : number * 8 + 8], high[:8], len(tiles))
                put(diagonal, c, rows, got[48 + number * 8 : 56 + number * 8], high[:8], len(tiles))


def merge_edges(column_ref, tiles, first, image, diagonal):
    for c in range(image.shape[0]):
        for edge in range(12):
            low, high = spots(column_ref, 6 + edge, EDGE_ROWS, c, first)
            got = gather_tiles(tiles, low, high)
            put(image, c, edge_rows(edge), got[:8], high[:8], len(tiles))
            put(diagonal, c, edge_rows(edge), got[8:], high[:8], len(tiles))


def merge_corners(column_ref, tiles, first, image, diagonal):
    tiles = [jnp.concatenate([tile[0:2]] * 4, axis=0) for tile in tiles]
    for c in range(image.shape[0]):
        lanes = slice(c * LANES, (c + 1) * LANES)
        for group in range(2):
            spot = jnp.concatenate(
                [
                    jnp.broadcast_to(column_ref[n : n + 1, lanes], (2, LANES))
                    for n in range(18 + group * 4, 22 + group * 4)
                ],
                axis=0,
            )
            high = (spot >> 7) - first
            got = gather_tiles(tiles, spot & (LANES - 1), high)
            new = (high >= 0) & (high < len(tiles))
            for number in range(4):
                at = corner_place(group * 4 + number)
                for ref, line in ((image, 2 * number), (diagonal, 2 * number + 1)):
                    ref[c, at : at + 1, :] = jnp.where(
                        new[line : line + 1], got[line : line + 1], ref[c, at : at + 1, :]
                    )


def merge_message(column_ref, message, first_kind, image, diagonal):
    size = image.shape[0] * LANES
    starts = table_starts((3 * size, 3 * size, size))
    for kind, merge in enumerate((merge_faces, merge_edges, merge_corners)):
        first = starts[kind][first_kind] // LANES
        merge(column_ref, message_tiles(message, kind), first, image, diagonal)


def merge_own(column, tables, image, diagonal, after):
    def kernel(column, faces, edges, corners, image_in, diagonal_in, *rest):
        image, diagonal = rest[-2:]
        image[...] = image_in[...]
        diagonal[...] = diagonal_in[...]
        merge_faces(column, table_tiles(faces), 0, image, diagonal)
        merge_edges(column, table_tiles(edges), 0, image, diagonal)
        merge_corners(column, table_tiles(corners), 0, image, diagonal)

    return pl.pallas_call(
        kernel,
        in_specs=[VMEM] * 6 + [ANY] * len(after),
        out_specs=[VMEM] * 2,
        out_shape=[jax.ShapeDtypeStruct(image.shape, F32)] * 2,
        name="merge_own",
        cost_estimate=QUICK,
        compiler_params=SMALL,
    )(column, *tables, image, diagonal, *after)


def merge_dom(column, message, image, diagonal, after):
    def kernel(column, message, image_in, diagonal_in, *rest):
        image, diagonal = rest[-2:]
        image[...] = image_in[...]
        diagonal[...] = diagonal_in[...]
        merge_message(column, message, 1, image, diagonal)

    return pl.pallas_call(
        kernel,
        in_specs=[VMEM] * 4 + [ANY] * len(after),
        out_specs=[VMEM] * 2,
        out_shape=[jax.ShapeDtypeStruct(image.shape, F32)] * 2,
        name="merge_dom",
        cost_estimate=QUICK,
        compiler_params=SMALL,
    )(column, message, image, diagonal, *after)


def relax_kernel(column, message, image_in, diagonal_in, field, forcing, source, *rest):
    relaxed, *outs, image, diagonal = rest[-7:]
    nodes, size = relaxed.shape
    image[...] = image_in[...]
    diagonal[...] = diagonal_in[...]
    merge_message(column, message, 2, image, diagonal)
    for row in range(0, nodes, STRIP):
        rows = slice(row, row + STRIP)
        for c in range(size // LANES):
            lanes = slice(c * LANES, (c + 1) * LANES)
            step = (forcing[rows, lanes] - image[c, rows, :]) / diagonal[c, rows, :]
            relaxed[rows, lanes] = field[rows, lanes] + RELAX * step
    for pair in range(2):
        source_row = source[:, pair * LANES : (pair + 1) * LANES]
        pack_block(relaxed, 0, nodes, source_row, outs[2 * pair : 2 * pair + 2], 0)


def relax_and_pack(column, message, image, diagonal, field, forcing, source, after):
    nodes, size = field.shape
    leaving = jax.ShapeDtypeStruct((nodes // 2, LANES), F32)
    return pl.pallas_call(
        relax_kernel,
        in_specs=[VMEM] * 7 + [ANY] * len(after),
        out_specs=[VMEM] * 5,
        out_shape=[jax.ShapeDtypeStruct((nodes, size), F32)] + [leaving] * 4,
        scratch_shapes=[pltpu.VMEM((size // LANES, nodes, LANES), F32)] * 2,
        name="relax_and_pack",
        cost_estimate=QUICK,
        compiler_params=SMALL,
    )(column, message, image, diagonal, field, forcing, source, *after)


def shifted(value, axis, steps):
    count = lax.axis_size(axis)
    return lax.ppermute(value, axis, [(i, (i + steps) % count) for i in range(count)])


def swapped(to_previous, to_next, axis):
    return shifted(to_next, axis, 1), shifted(to_previous, axis, -1)


def on_device(solution, forcing, metric, entity_ids, new_owner):
    size = solution.shape[-1]
    place = devices()
    table = derivative_table(solution.shape[0] - 1)
    field = solution.reshape(-1, size)
    metric_rows = pltpu.with_memory_space_constraint(metric.reshape(-1, size), pltpu.HBM)
    components = metric.shape[0]
    block = metric_rows.shape[0] // components
    source, landing, *messages, metric_rows = plan_and_pack(
        place, new_owner.reshape(1, size), metric_rows, block
    )
    sub_early = swapped(*messages, "sub")
    messages = pack(source, metric_rows, 0, DOM_EARLY, 0, block, (landing,), "pack_dom")
    dom_early = swapped(*messages, "dom")
    image, diagonal, column, *tables, dom, sub = apply_and_pack(
        place, entity_ids, field, metric_rows, messages[0], table
    )
    got_sub = shifted(sub, "sub", 1)
    messages = pack(
        source, metric_rows, SUB_EARLY, components - SUB_EARLY, 1, block, (sub,), "pack_sub_late"
    )
    sub_late = swapped(*messages, "sub")
    dom = pass_on(dom, got_sub, (*sub_early, messages[0]))
    got_dom = shifted(dom, "dom", 1)
    tables = add_sub(tables, got_sub, dom)
    *tables, dom_back = add_dom(tables, got_dom)
    back_dom = shifted(dom_back, "dom", -1)
    sub_back = read_sub(tables, got_sub)
    image, diagonal = merge_own(column, tables, image, diagonal, (dom_back, *dom_early))
    sub_back = pass_on(sub_back, back_dom)
    back_sub = shifted(sub_back, "sub", -1)
    image, diagonal = merge_dom(column, back_dom, image, diagonal, sub_late)
    dom_moves, sub_moves = (dom_early, ()), (sub_early, sub_late)
    relaxed, *leaving = relax_and_pack(
        column, back_sub, image, diagonal, field, forcing.reshape(-1, size), source,
        (image,),
    )
    moved, token = land_metric(
        landing, metric_rows, dom_moves, sub_moves, 0, SUB_EARLY, block, None, leaving[0], "land_early"
    )
    got_sub = swapped(*leaving[2:], "sub")
    got_dom = swapped(*leaving[:2], "dom")
    moved, token = land_metric(
        landing, metric_rows, dom_moves, sub_moves, SUB_EARLY, components - SUB_EARLY, block, moved,
        leaving[0], "land_late",
    )
    smoothed = land_field(landing, relaxed, got_dom + got_sub, token)
    return smoothed.reshape(solution.shape), moved.reshape(metric.shape)


def solution(mesh):
    placed = (
        P(None, None, None, ("dom", "sub")),
        P(None, None, None, ("dom", "sub")),
        P(None, None, None, None, ("dom", "sub")),
        P(None, ("dom", "sub")),
        P(("dom", "sub")),
    )
    return jax.shard_map(
        on_device,
        mesh=mesh,
        in_specs=placed,
        out_specs=(P(None, None, None, ("dom", "sub")), P(None, None, None, None, ("dom", "sub"))),
        check_vma=False,
    )
```

```python
import functools

import jax
import jax.numpy as jnp
import numpy as np
from jax import lax
from jax.experimental import pallas as pl
from jax.experimental.pallas import tpu as pltpu
from jax.sharding import PartitionSpec as P

EX = 4
EY = 4
EZ = 32
MOVE = 64
RELAX = 0.6
LANES = 128
INNER = 6
SUB_EARLY = 4
DOM_EARLY = 7

NT = (((1,), (1,)), ((), ()))
VMEM = pl.BlockSpec(memory_space=pltpu.VMEM)
ANY = pl.BlockSpec(memory_space=pl.ANY)
SMEM = pl.BlockSpec(memory_space=pltpu.SMEM)
QUICK = pl.CostEstimate(flops=1000, bytes_accessed=1000, transcendentals=0)
HBM = pl.BlockSpec(memory_space=pltpu.HBM)
LARGE = pltpu.CompilerParams(vmem_limit_bytes=24 << 20)
SMALL = pltpu.CompilerParams(vmem_limit_bytes=16 << 20)
STRIP = 256
F32 = jnp.float32
BF16 = jnp.bfloat16
I32 = jnp.int32


def derivative_table(order):
    count = order + 1
    points = -np.cos(np.pi * np.arange(count) / order)
    legendre = np.zeros((count, count))
    for sweep in range(80):
        legendre[:, 0] = 1.0
        legendre[:, 1] = points
        for degree in range(2, count):
            legendre[:, degree] = (
                (2 * degree - 1) * points * legendre[:, degree - 1]
                - (degree - 1) * legendre[:, degree - 2]
            ) / degree
        points = points - (points * legendre[:, order] - legendre[:, order - 1]) / (
            count * legendre[:, order]
        )
    legendre[:, 0] = 1.0
    legendre[:, 1] = points
    for degree in range(2, count):
        legendre[:, degree] = (
            (2 * degree - 1) * points * legendre[:, degree - 1]
            - (degree - 1) * legendre[:, degree - 2]
        ) / degree
    values = legendre[:, order]
    identity = np.eye(count)
    spread = points[:, None] - points[None, :] + identity
    table = values[:, None] / values[None, :] / spread
    table = table * (1.0 - identity)
    table[0, 0] = -order * count / 4.0
    table[order, order] = order * count / 4.0
    return table.astype(np.float32)


def split_np(matrix):
    high = matrix.astype(jnp.bfloat16).astype(np.float32)
    low = (matrix - high).astype(jnp.bfloat16)
    return np.concatenate([high.astype(jnp.bfloat16), low, high.astype(jnp.bfloat16)], axis=1)


def split(values):
    high = values.astype(BF16)
    low = (values - high.astype(F32)).astype(BF16)
    return high, low


def triple(values):
    high, low = split(values)
    return jnp.concatenate([high, high, low], axis=0)


def dot(left, right):
    return jnp.dot(left, right, preferred_element_type=F32)


def dot_nt(left, right):
    return lax.dot_general(left, right, NT, preferred_element_type=F32)


def iota(shape, dim):
    return lax.broadcasted_iota(I32, shape, dim)


def one_hot_rows(index_row, start, count):
    size = index_row.shape[1]
    out = []
    for base in range(0, count, LANES):
        local = (index_row - (start + base)).astype(BF16)
        rows = iota((LANES, size), 0).astype(BF16)
        out.append(
            jnp.where(rows == local, jnp.ones((LANES, size), BF16), jnp.zeros((LANES, size), BF16))
        )
    return out[0] if len(out) == 1 else jnp.concatenate(out, axis=0)


def exclusive_count(masks):
    size = masks.shape[1]
    upper = jnp.where(iota((size, size), 0) < iota((size, size), 1), 1.0, 0.0).astype(BF16)
    return dot(masks.astype(BF16), upper)


def gather_tiles(tiles, low, high):
    out = None
    for number, tile in enumerate(tiles):
        got = jnp.take_along_axis(tile, low, axis=1)
        out = got if out is None else jnp.where(high == number, got, out)
    return out


def devices():
    dom_count = lax.axis_size("dom")
    sub_count = lax.axis_size("sub")
    dom = lax.axis_index("dom")
    sub = lax.axis_index("sub")
    dom_ahead = lax.rem(dom + 1, dom_count)
    dom_behind = lax.rem(dom + dom_count - 1, dom_count)
    sub_ahead = lax.rem(sub + 1, sub_count)
    sub_behind = lax.rem(sub + sub_count - 1, sub_count)
    return jnp.stack(
        [
            dom_behind * sub_count + sub,
            dom_ahead * sub_count + sub,
            dom * sub_count + sub_behind,
            dom * sub_count + sub_ahead,
            dom * sub_count + sub,
            dom_ahead * sub_count + sub_ahead,
        ]
    ).astype(I32)


def pack_pair(top, bottom):
    left = iota(top.shape, 1) < MOVE
    first = jnp.where(left, top, pltpu.roll(bottom, MOVE, 1))
    second = jnp.where(left, pltpu.roll(top, MOVE, 1), bottom)
    return first, second


def pick_columns(ref, rows, low, high):
    tiles = [ref[rows, c : c + LANES] for c in range(0, ref.shape[1], LANES)]
    return gather_tiles(tiles, low, high)


def pack_block(ref, start, block, source_row, outs, to):
    half = block // 2
    source = jnp.broadcast_to(source_row, (half, LANES))
    low, high = source & (LANES - 1), source >> 7
    top = pick_columns(ref, slice(start, start + half), low, high)
    bottom = pick_columns(ref, slice(start + half, start + block), low, high)
    for out, message in zip(outs, pack_pair(top, bottom)):
        out[to : to + half, :] = message


def arrival_spots(landing_row):
    return jnp.concatenate([one_hot_rows(landing_row, 0, 4 * MOVE)] * 3, axis=0)


def split_exactly(values):
    parts = []
    for _ in range(3):
        parts.append(values.astype(BF16))
        values = values - parts[-1].astype(F32)
    return jnp.concatenate(parts, axis=1)


def land_block(ref, start, block, landing_row, spots, messages, ats, out, to):
    land_strips(ref, start, block // 2, 0, block // 2, landing_row, spots, messages, ats, out, to)


def land_strips(ref, start, half, from_row, to_row, landing_row, spots, messages, ats, out, to):
    rows = to_row - from_row
    parts = [message[at + from_row : at + to_row, :] for message, at in zip(messages, ats)]
    pairs = [pack_pair(parts[0], parts[1]), pack_pair(parts[2], parts[3])]
    stays = jnp.broadcast_to(landing_row < 0, (rows, landing_row.shape[1]))
    arrived = [jnp.concatenate([pairs[0][side], pairs[1][side]], axis=1) for side in range(2)]
    got = dot(split_exactly(jnp.concatenate(arrived, axis=0)), spots)
    for side in range(2):
        first = side * half + from_row
        held = ref[start + first : start + first + rows, :]
        out[to + first : to + first + rows, :] = jnp.where(
            stays, held, got[side * rows : (side + 1) * rows]
        )


def move_plan(owner, place):
    size = owner.shape[1]
    own = place[4]
    line = iota((8, size), 0)
    target = jnp.where(
        line == 0,
        place[0],
        jnp.where(line == 1, place[1], jnp.where(line == 2, place[2], place[3])),
    )
    nobody = jnp.broadcast_to(owner, (8, size))
    away = nobody != own
    masks = jnp.where(away & (((nobody == target) & (line < 4)) | (line == 4)), 1.0, 0.0)
    ranks = exclusive_count(masks)
    counts = jnp.sum(masks, axis=1, keepdims=True)
    hole = ranks[4:5]
    gone = masks[4:5] > 0.5
    column = jnp.full((1, size), -1.0, F32)
    landing = jnp.full((1, size), -1.0, F32)
    offset = jnp.zeros((1, 1), F32)
    for way in range(4):
        column = jnp.where(masks[way : way + 1] > 0.5, way * MOVE + ranks[way : way + 1], column)
        ahead = hole - offset
        here = gone & (ahead >= 0.0) & (ahead < counts[way : way + 1])
        landing = jnp.where(here, way * MOVE + ahead, landing)
        offset = offset + counts[way : way + 1]
    spots = one_hot_rows(column.astype(I32), 0, 4 * MOVE)
    element = iota((8, size), 1)
    parts = jnp.where(iota((8, size), 0) == 0, element >> 4, element & 15)
    found = dot_nt(parts.astype(BF16), spots)
    source = found[0:1] * 16.0 + found[1:2]
    return source.astype(I32), landing.astype(I32)


def fetch(source, target, sems, number, start, count, to):
    return pltpu.make_async_copy(
        source.at[pl.ds(start, count), :], target.at[pl.ds(to, count), :], sems.at[number]
    )


def send_part(held, first, number, source, outs, block):
    pack_block(held, (first + number) * block, block, source, outs, number * block // 2)


def plan_and_pack_kernel(
    place, owner_hbm, metric, source_ref, landing_ref, first_out, second_out, held, sems, owner,
    owner_sem, *, block,
):
    copy = pltpu.make_async_copy(owner_hbm, owner, owner_sem)
    copy.start()
    count = held.shape[0] // block
    copies = [fetch(metric, held, sems, c, c * block, block, c * block) for c in range(count)]
    for part in copies:
        part.start()
    copy.wait()
    source, landing = move_plan(owner[...], place)
    source_ref[...] = source
    landing_ref[...] = landing
    for number, part in enumerate(copies):
        part.wait()
        if number < SUB_EARLY:
            send_part(held, 0, number, source[:, LANES:], (first_out, second_out), block)


def pack_kernel(source, held, *rest, first, pair, block):
    outs = rest[-2:]
    lanes = slice(pair * LANES, (pair + 1) * LANES)
    for number in range(outs[0].shape[0] * 2 // block):
        send_part(held, first, number, source[:, lanes], outs, block)


def sent_shapes(count, block):
    return [jax.ShapeDtypeStruct((count * block // 2, LANES), F32)] * 2


def plan_and_pack(place, owner, metric_rows, block):
    rows, size = metric_rows.shape
    outs = sent_shapes(SUB_EARLY, block) + [jax.ShapeDtypeStruct((rows, size), F32)]
    plan = [jax.ShapeDtypeStruct((1, 4 * MOVE), I32), jax.ShapeDtypeStruct((1, size), I32)]
    return pl.pallas_call(
        functools.partial(plan_and_pack_kernel, block=block),
        in_specs=[SMEM, HBM, HBM],
        out_specs=[VMEM] * 5,
        out_shape=plan + outs,
        scratch_shapes=[
            pltpu.SemaphoreType.DMA((rows // block,)),
            pltpu.VMEM((1, size), I32),
            pltpu.SemaphoreType.DMA,
        ],
        name="plan_and_pack",
        cost_estimate=QUICK,
        compiler_params=LARGE,
    )(place, owner, metric_rows)


def pack(source, metric_rows, first, count, pair, block, after, name):
    outs = sent_shapes(count, block)
    return pl.pallas_call(
        functools.partial(pack_kernel, first=first, pair=pair, block=block),
        in_specs=[VMEM, VMEM] + [ANY] * len(after),
        out_specs=[VMEM] * 2,
        out_shape=outs,
        name=name,
        cost_estimate=QUICK,
        compiler_params=LARGE,
    )(source, metric_rows, *after)


def land_metric_kernel(landing, held, *rest, first, block, spots):
    *messages, out, token, ready, sems = rest
    token[...] = jnp.zeros_like(token)
    columns = arrival_spots(landing[...])
    copies = []
    for number in range(ready.shape[0] // block):
        start = number * block
        source = (first + number) * block
        parts, at = spots[number]
        land_block(
            held, source, block, landing[...], columns, [messages[k] for k in parts], at, ready, start
        )
        copies.append(fetch(ready, out, sems, number, start, block, source))
        copies[-1].start()
    for copy in copies:
        copy.wait()


def land_metric(landing, metric_rows, dom, sub, first, count, block, before, after, name):
    size = metric_rows.shape[1]
    messages, spots = [], []
    for number in range(first, first + count):
        parts, ats = [], None
        for (early, late), limit in ((dom, DOM_EARLY), (sub, SUB_EARLY)):
            chosen, local = (early, number) if number < limit else (late, number - limit)
            for message in chosen:
                known = [k for k, other in enumerate(messages) if other is message]
                if not known:
                    messages.append(message)
                parts.append(known[0] if known else len(messages) - 1)
            ats = (ats or []) + [local * block // 2] * 2
        spots.append((parts, ats))
    operands = [landing, metric_rows, *messages, after]
    specs = [VMEM, VMEM] + [VMEM] * len(messages) + [ANY]
    aliases = {}
    if before is not None:
        aliases = {len(operands): 0}
        operands.append(before)
        specs.append(HBM)
    return pl.pallas_call(
        functools.partial(land_metric_kernel, first=first, block=block, spots=spots),
        in_specs=specs,
        out_specs=[HBM, VMEM],
        out_shape=[
            jax.ShapeDtypeStruct(metric_rows.shape, F32),
            jax.ShapeDtypeStruct((8, LANES), F32),
        ],
        scratch_shapes=[
            pltpu.VMEM((count * block, size), F32),
            pltpu.SemaphoreType.DMA((count,)),
        ],
        input_output_aliases=aliases,
        name=name,
        cost_estimate=QUICK,
        compiler_params=LARGE,
    )(*operands)


def land_field_kernel(landing, relaxed, first, second, third, fourth, after, out, ready, sems):
    del after
    rows = relaxed.shape[0]
    piece = rows // 8
    half = rows // 2
    messages = (first, second, third, fourth)
    copies = []
    columns = arrival_spots(landing[...])
    for row in range(0, half, piece):
        land_strips(
            relaxed, 0, half, row, row + piece, landing[...], columns, messages, [0] * 4, ready, 0
        )
        for side in range(2):
            copies.append(fetch(ready, out, sems, len(copies), side * half + row, piece, side * half + row))
            copies[-1].start()
    for copy in copies:
        copy.wait()


def land_field(landing, relaxed, arrived, after):
    count = 8
    return pl.pallas_call(
        land_field_kernel,
        in_specs=[VMEM] * 6 + [ANY],
        out_specs=HBM,
        out_shape=jax.ShapeDtypeStruct(relaxed.shape, F32),
        scratch_shapes=[pltpu.VMEM(relaxed.shape, F32), pltpu.SemaphoreType.DMA((count,))],
        name="land_field",
        cost_estimate=QUICK,
        compiler_params=SMALL,
    )(landing, relaxed, *arrived, after)


FACE_DOM = EY * EZ
FACE_SUB = EX * EZ
EDGE_DOM = EZ * (4 * EY - 1)
EDGE_SUB = EZ * (4 * EX - 1)
CORNER_DOM = EZ * (4 * EY - 2)
CORNER_SUB = EZ * (4 * EX - 2)


def up(count):
    return -(-count // LANES) * LANES


EDGE_TILES = up(EDGE_DOM) // LANES
CORNER_TILES = up(CORNER_DOM) // LANES


def table_starts(hosted):
    edge_dom, edge_sub = hosted[1], hosted[1] + EDGE_TILES * LANES
    corner_dom, corner_sub = hosted[2], hosted[2] + CORNER_TILES * LANES
    return (
        (0, hosted[0], hosted[0] + up(FACE_DOM), hosted[0]),
        (0, edge_dom, edge_sub, edge_sub + EDGE_SUB),
        (0, corner_dom, corner_sub, corner_sub + CORNER_SUB),
    )


KINDS = (6, 12, 8)
FACE_ROWS = 2 * INNER * 8
EDGE_ROWS = 16
CORNER_ROWS = 4
CORNER_BASE = FACE_ROWS + EDGE_TILES * EDGE_ROWS
MESSAGE_ROWS = CORNER_BASE + CORNER_TILES * CORNER_ROWS


def shared_columns(ids, place, hosted):
    lines, size = ids.shape
    line = iota((lines, 1), 0)
    per = jnp.where(line < 6, hosted[0], jnp.where(line < 18, hosted[1], hosted[2]))
    owns, rows, masks = [], jnp.zeros((lines, size), I32), []
    for device in (place[4], place[1], place[3], place[5]):
        local = ids - device * per
        inside = (local >= 0) & (local < per)
        rows = jnp.where(inside, local, rows)
        owns.append(inside)
    starts = table_starts(hosted)
    lower = (iota((lines, lines), 1) < iota((lines, lines), 0)) & (
        (iota((lines, lines), 0) < 6) == (iota((lines, lines), 1) < 6)
    )
    lower = lower & ((iota((lines, lines), 0) < 18) == (iota((lines, lines), 1) < 18))
    lower = jnp.where(lower, 1.0, 0.0).astype(BF16)
    column = rows
    marks = jnp.concatenate([jnp.where(inside, 1.0, 0.0) for inside in owns[1:]], axis=0)
    ranks = exclusive_count(marks)
    for number in range(3):
        inside = owns[1 + number]
        mark = marks[number * lines : (number + 1) * lines]
        above = jnp.sum(dot(lower, mark.astype(BF16)), axis=1, keepdims=True)
        rank = (ranks[number * lines : (number + 1) * lines] + above).astype(I32)
        base = jnp.where(
            line < 6,
            starts[0][1 + number],
            jnp.where(line < 18, starts[1][1 + number], starts[2][1 + number]),
        )
        column = jnp.where(inside, base + rank, column)
    return column, rows


def scatter_two(parts, column_row, tiles):
    high, low = split(parts)
    both = jnp.concatenate([high, low], axis=0)
    size = column_row.shape[1]
    tile = jnp.broadcast_to((column_row >> 7).astype(BF16), both.shape)
    zero = jnp.zeros(both.shape, BF16)
    left = jnp.concatenate([jnp.where(tile == h, both, zero) for h in range(tiles)], axis=0)
    return dot_nt(left, one_hot_rows(column_row & (LANES - 1), 0, LANES))


def face_rows(face, inner):
    end = 7 * (face % 2)
    if face < 2:
        return pl.ds(end * 64 + inner * 8, 8)
    if face < 4:
        return pl.ds(inner * 64 + end * 8, 8)
    return pl.ds(inner * 64 + end, 8, stride=8)


def all_lanes(ref, rows):
    return jnp.concatenate([ref[c, rows, :] for c in range(ref.shape[0])], axis=1)


def face_nodes(ref, face):
    return jnp.concatenate(
        [all_lanes(ref, face_rows(face, inner)) for inner in range(1, INNER + 1)], axis=0
    )


def edge_place(edge):
    ends = (7 * (edge % 4 // 2), 7 * (edge % 2))
    if edge < 4:
        return ends[0] * 8 + ends[1], 64
    if edge < 8:
        return ends[0] * 64 + ends[1], 8
    return ends[0] * 64 + ends[1] * 8, 1


def edge_rows(edge):
    start, stride = edge_place(edge)
    return pl.ds(start, 8) if stride == 1 else pl.ds(start, 8, stride=stride)


def corner_place(corner):
    return (corner // 4) * 448 + (corner // 2 % 2) * 56 + (corner % 2) * 7


def apply_kernel(
    place,
    ids,
    solution,
    metric,
    grad_left,
    image_left,
    square_left,
    after,
    image_ref,
    diagonal_ref,
    column_ref,
    face_table,
    edge_table,
    corner_table,
    dom_out,
    sub_out,
    flux_r,
    *,
    table,
):
    del after
    size = image_ref.shape[0] * LANES
    count = table.shape[0]
    plane = count * count
    nodes = count * plane
    width = 2 * LANES
    node = iota((count, width), 0)
    ends = (0, count - 1)
    end_value = {0: float(table[0, 0]), count - 1: float(table[count - 1, count - 1])}
    ends_k = jnp.where(
        node == 0, end_value[0], jnp.where(node == count - 1, end_value[count - 1], 0.0)
    )
    for i in range(count):
        rows = slice(i * plane, (i + 1) * plane)
        for base in range(0, size, width):
            lanes = slice(base, base + width)

            grads = dot(grad_left[...], triple(solution[rows, lanes]))
            fluxes, weights = [[], []], [[], []]
            strip = 2 * count
            for start in range(0, plane, strip):
                at = slice(start, start + strip)
                part = [
                    metric[c * nodes + i * plane + start : c * nodes + i * plane + start + strip, lanes]
                    for c in range(6)
                ]
                grad_r = sum(
                    float(table[i, q])
                    * solution[q * plane + start : q * plane + start + strip, lanes]
                    for q in range(count)
                )
                grad_s, grad_t = grads[start : start + strip], grads[plane + start : plane + start + strip]
                flux_r[i * plane + start : i * plane + start + strip, lanes] = (
                    part[0] * grad_r + part[3] * grad_s + part[4] * grad_t
                )
                fluxes[0].append(split(part[3] * grad_r + part[1] * grad_s + part[5] * grad_t))
                fluxes[1].append(split(part[4] * grad_r + part[5] * grad_s + part[2] * grad_t))
                weights[0].append(split(part[1]))
                weights[1].append(split(part[2]))

            def stacked(pieces):
                pieces = pieces[0] + pieces[1]
                high = [piece[0] for piece in pieces]
                return jnp.concatenate(high + high + [piece[1] for piece in pieces], axis=0)

            image = dot(image_left[...], stacked(fluxes))
            diagonal = dot(square_left[...], stacked(weights))
            for j in range(count):
                lines = slice(j * count, (j + 1) * count)
                first = i * plane + j * count

                def here(c):
                    return metric[c * nodes + first : c * nodes + first + count, lanes]

                mass = here(6)
                total = diagonal[lines] + mass
                if j in ends:
                    total = total + here(5) * (ends_k * (2.0 * end_value[j]))
                if i in ends:
                    total = total + here(4) * (ends_k * (2.0 * end_value[i]))
                    if j in ends:
                        total = total + here(3) * (2.0 * end_value[i] * end_value[j])
                value = image[lines] + mass * solution[first : first + count, lanes]
                for c in range(width // LANES):
                    side = slice(c * LANES, (c + 1) * LANES)
                    image_ref[base // LANES + c, first : first + count, :] = value[:, side]
                    diagonal_ref[base // LANES + c, first : first + count, :] = total[:, side]
    for i in range(count):
        rows = slice(i * plane, (i + 1) * plane)
        for c in range(size // LANES):
            lanes = slice(c * LANES, (c + 1) * LANES)
            image_ref[c, rows, :] += sum(
                float(table[a, i]) * flux_r[a * plane : (a + 1) * plane, lanes]
                for a in range(count)
            )
            diagonal_ref[c, rows, :] += sum(
                float(table[a, i] * table[a, i]) * metric[a * plane : (a + 1) * plane, lanes]
                for a in range(count)
            )

    def _():
        hosted = (3 * size, 3 * size, size)
        starts = table_starts(hosted)
        column, row = shared_columns(ids[...], place, hosted)
        column_ref[...] = column
        row_high = (row >> 4).astype(F32)
        row_low = (row & 15).astype(F32)
        face_parts = []
        spot = iota((48, size), 0)
        for face in range(6):
            values = face_nodes(image_ref, face)
            values = jnp.where(spot == 0, row_high[face : face + 1], values)
            values = jnp.where(spot == 7, row_low[face : face + 1], values)
            values = jnp.concatenate([values, face_nodes(diagonal_ref, face)], axis=0)
            face_parts.append(jnp.concatenate(split(values), axis=0))
        faces_end = starts[0][2] + up(FACE_SUB)
        for base in range(0, faces_end, 2 * LANES):
            total = None
            for face in range(6):
                more = dot_nt(
                    face_parts[face], one_hot_rows(column[face : face + 1], base, 2 * LANES)
                )
                total = more if total is None else total + more
            total = total[:FACE_ROWS] + total[FACE_ROWS:]
            for side in range(2):
                tile = total[:, side * LANES : (side + 1) * LANES]
                place_column = base + side * LANES
                if place_column < starts[0][1]:
                    face_table[:, place_column : place_column + LANES] = tile
                elif place_column < starts[0][2]:
                    dom_out[0:FACE_ROWS, :] = tile
                else:
                    sub_out[0:FACE_ROWS, :] = tile
        tiles = starts[1][2] // LANES + EDGE_TILES
        total = None
        line = iota((8, size), 0)
        for edge in range(12):
            values = all_lanes(image_ref, edge_rows(edge))
            values = jnp.where(line == 0, row_high[6 + edge : 7 + edge], values)
            values = jnp.where(line == 7, row_low[6 + edge : 7 + edge], values)
            values = jnp.concatenate([values, all_lanes(diagonal_ref, edge_rows(edge))], axis=0)
            more = scatter_two(values, column[6 + edge : 7 + edge], tiles)
            total = more if total is None else total + more
        for number in range(tiles):
            first = number * 2 * EDGE_ROWS
            tile = total[first : first + EDGE_ROWS] + total[first + EDGE_ROWS : first + 2 * EDGE_ROWS]
            place_column = number * LANES
            if place_column < starts[1][1]:
                edge_table[:, place_column : place_column + LANES] = tile
            elif place_column < starts[1][2]:
                base = FACE_ROWS + (place_column - starts[1][1]) // LANES * EDGE_ROWS
                dom_out[base : base + EDGE_ROWS, :] = tile
            else:
                base = FACE_ROWS + (place_column - starts[1][2]) // LANES * EDGE_ROWS
                sub_out[base : base + EDGE_ROWS, :] = tile
        tiles = starts[2][2] // LANES + CORNER_TILES
        total = None
        for corner in range(8):
            at = corner_place(corner)
            values = jnp.concatenate(
                [
                    all_lanes(image_ref, slice(at, at + 1)),
                    all_lanes(diagonal_ref, slice(at, at + 1)),
                    row_high[18 + corner : 19 + corner],
                    row_low[18 + corner : 19 + corner],
                    jnp.zeros((4, size), F32),
                ],
                axis=0,
            )
            more = scatter_two(values, column[18 + corner : 19 + corner], tiles)
            total = more if total is None else total + more
        for number in range(tiles):
            tile = total[number * 16 : number * 16 + 8] + total[number * 16 + 8 : number * 16 + 16]
            place_column = number * LANES
            if place_column < starts[2][1]:
                corner_table[:, place_column : place_column + LANES] = tile
            elif place_column < starts[2][2]:
                base = CORNER_BASE + (place_column - starts[2][1]) // LANES * CORNER_ROWS
                dom_out[base : base + CORNER_ROWS, :] = tile[:CORNER_ROWS]
            else:
                base = CORNER_BASE + (place_column - starts[2][2]) // LANES * CORNER_ROWS
                sub_out[base : base + CORNER_ROWS, :] = tile[:CORNER_ROWS]

    _()


def apply_and_pack(place, ids, field, metric_rows, after, table):
    nodes, size = field.shape
    count = table.shape[0]
    eye = np.eye(count, dtype=np.float32)
    grad = np.concatenate([np.kron(table, eye), np.kron(eye, table)], axis=0)
    square = (table * table).astype(np.float32)
    squares = np.concatenate([np.kron(square, eye), np.kron(eye, square)], axis=0)
    lefts = [split_np(grad), split_np(grad.T), split_np(squares.T)]

    def out(*shape, dtype=F32):
        return jax.ShapeDtypeStruct(shape, dtype)

    outs = [
        out(size // LANES, nodes, LANES),
        out(size // LANES, nodes, LANES),
        out(sum(KINDS), size, dtype=I32),
        out(FACE_ROWS, 3 * size),
        out(EDGE_ROWS, 3 * size),
        out(8, size),
        out(MESSAGE_ROWS, LANES),
        out(MESSAGE_ROWS, LANES),
    ]
    return pl.pallas_call(
        functools.partial(apply_kernel, table=table),
        in_specs=[SMEM] + [VMEM] * 6 + [ANY],
        out_specs=[VMEM] * len(outs),
        out_shape=outs,
        scratch_shapes=[
            pltpu.VMEM((nodes, size), F32),
        ],
        name="apply_and_pack",
        cost_estimate=QUICK,
        compiler_params=LARGE,
    )(place, ids, field, metric_rows, *[jnp.asarray(left) for left in lefts], after)


def message_parts(kind):
    if kind == 0:
        return [0], FACE_ROWS
    if kind == 1:
        return [FACE_ROWS + q * EDGE_ROWS for q in range(EDGE_TILES)], EDGE_ROWS
    return [CORNER_BASE + q * CORNER_ROWS for q in range(CORNER_TILES)], CORNER_ROWS


def message_tiles(ref, kind):
    places, rows = message_parts(kind)
    return [ref[at : at + rows, :] for at in places]


def table_tiles(ref):
    return [ref[:, c : c + LANES] for c in range(0, ref.shape[1], LANES)]


def message_values(ref, kind, limit):
    values = jnp.concatenate(message_tiles(ref, kind), axis=1)
    first = 2 if kind == 2 else 0
    second = 3 if kind == 2 else 7
    row = (values[first : first + 1] * 16.0 + values[second : second + 1]).astype(I32)
    row = jnp.where(iota(row.shape, 1) < limit, row, -1)
    if kind == 2:
        values = jnp.concatenate([values, jnp.zeros_like(values)], axis=0)
    return values, row


def add_message(ref, tables, outs, limits):
    values, row = message_values(ref, 0, limits[0])
    parts = jnp.concatenate(split(values), axis=0)
    for base in range(0, outs[0].shape[1], 2 * LANES):
        lanes = slice(base, base + 2 * LANES)
        more = dot_nt(parts, one_hot_rows(row, base, 2 * LANES))
        outs[0][:, lanes] = tables[0][:, lanes] + more[:FACE_ROWS] + more[FACE_ROWS:]
    for kind in (1, 2):
        values, row = message_values(ref, kind, limits[kind])
        rows = values.shape[0]
        count = outs[kind].shape[1] // LANES
        total = scatter_two(values, row, count)
        for number in range(count):
            lanes = slice(number * LANES, (number + 1) * LANES)
            first = number * 2 * rows
            more = total[first : first + rows] + total[first + rows : first + 2 * rows]
            outs[kind][:, lanes] = tables[kind][:, lanes] + more


def read_message(ref, tables, back):
    for kind in range(3):
        places, rows = message_parts(kind)
        row = jnp.maximum(message_values(ref, kind, 1 << 20)[1], 0)
        tiles = table_tiles(tables[kind])
        depth = tiles[0].shape[0]
        for number, at in enumerate(places):
            spot = jnp.broadcast_to(row[:, number * LANES : (number + 1) * LANES], (depth, LANES))
            got = gather_tiles(tiles, spot & (LANES - 1), spot >> 7)
            back[at : at + rows, :] = got[:rows]


SUB_LIMITS = (FACE_SUB, EDGE_SUB, CORNER_SUB)
DOM_LIMITS = (FACE_DOM, EDGE_SUB + EZ, CORNER_SUB + 2 * EZ)


def passed_on(message, received):
    parts = [message[0:FACE_ROWS, :]]
    for kind, limit in ((1, EDGE_SUB), (2, CORNER_SUB)):
        ours, theirs = message_tiles(message, kind), message_tiles(received, kind)
        for number in range(len(ours)):
            lane = iota(ours[number].shape, 1) + number * LANES
            parts.append(jnp.where(lane < limit, ours[number], theirs[number]))
    return parts


def pass_on_kernel(message, received, *rest):
    out = rest[-1]
    at = 0
    for part in passed_on(message, received):
        out[at : at + part.shape[0], :] = part
        at += part.shape[0]


def pass_on(message, received, after=()):
    return pl.pallas_call(
        pass_on_kernel,
        in_specs=[VMEM] * 2 + [ANY] * len(after),
        out_specs=VMEM,
        out_shape=jax.ShapeDtypeStruct(message.shape, F32),
        name="pass_on",
        cost_estimate=QUICK,
        compiler_params=SMALL,
    )(message, received, *after)


def add_sub_kernel(faces, edges, corners, message, after, *outs):
    del after
    add_message(message, (faces, edges, corners), outs, SUB_LIMITS)


def add_sub(tables, message, after):
    return pl.pallas_call(
        add_sub_kernel,
        in_specs=[VMEM] * 4 + [ANY],
        out_specs=[VMEM] * 3,
        out_shape=[jax.ShapeDtypeStruct(a.shape, F32) for a in tables],
        name="add_sub",
        cost_estimate=QUICK,
        compiler_params=SMALL,
    )(*tables, message, after)


def add_dom_kernel(faces, edges, corners, message, *outs):
    add_message(message, (faces, edges, corners), outs[:3], DOM_LIMITS)
    read_message(message, outs[:3], outs[3])


def add_dom(tables, message):
    return pl.pallas_call(
        add_dom_kernel,
        in_specs=[VMEM] * 4,
        out_specs=[VMEM] * 4,
        out_shape=[jax.ShapeDtypeStruct(a.shape, F32) for a in (*tables, message)],
        name="add_dom",
        cost_estimate=QUICK,
        compiler_params=SMALL,
    )(*tables, message)


def read_sub_kernel(faces, edges, corners, message, back):
    read_message(message, (faces, edges, corners), back)


def read_sub(tables, message):
    return pl.pallas_call(
        read_sub_kernel,
        in_specs=[VMEM] * 4,
        out_specs=VMEM,
        out_shape=jax.ShapeDtypeStruct(message.shape, F32),
        name="read_sub",
        cost_estimate=QUICK,
        compiler_params=SMALL,
    )(*tables, message)


def spots(column_ref, line, rows, c, first):
    spot = jnp.broadcast_to(column_ref[line : line + 1, c * LANES : (c + 1) * LANES], (rows, LANES))
    return spot & (LANES - 1), (spot >> 7) - first


def put(ref, c, rows, values, high, count):
    line = iota(values.shape, 0)
    new = (line > 0) & (line < 7) & (high >= 0) & (high < count)
    ref[c, rows, :] = jnp.where(new, values, ref[c, rows, :])


def merge_faces(column_ref, tiles, first, image, diagonal):
    for c in range(image.shape[0]):
        for face in range(6):
            low, high = spots(column_ref, face, FACE_ROWS, c, first)
            got = gather_tiles(tiles, low, high)
            for number in range(INNER):
                rows = face_rows(face, number + 1)
                put(image, c, rows, got[number * 8 : number * 8 + 8], high[:8], len(tiles))
                put(diagonal, c, rows, got[48 + number * 8 : 56 + number * 8], high[:8], len(tiles))


def merge_edges(column_ref, tiles, first, image, diagonal):
    for c in range(image.shape[0]):
        for edge in range(12):
            low, high = spots(column_ref, 6 + edge, EDGE_ROWS, c, first)
            got = gather_tiles(tiles, low, high)
            put(image, c, edge_rows(edge), got[:8], high[:8], len(tiles))
            put(diagonal, c, edge_rows(edge), got[8:], high[:8], len(tiles))


def merge_corners(column_ref, tiles, first, image, diagonal):
    tiles = [jnp.concatenate([tile[0:2]] * 4, axis=0) for tile in tiles]
    for c in range(image.shape[0]):
        lanes = slice(c * LANES, (c + 1) * LANES)
        for group in range(2):
            spot = jnp.concatenate(
                [
                    jnp.broadcast_to(column_ref[n : n + 1, lanes], (2, LANES))
                    for n in range(18 + group * 4, 22 + group * 4)
                ],
                axis=0,
            )
            high = (spot >> 7) - first
            got = gather_tiles(tiles, spot & (LANES - 1), high)
            new = (high >= 0) & (high < len(tiles))
            for number in range(4):
                at = corner_place(group * 4 + number)
                for ref, line in ((image, 2 * number), (diagonal, 2 * number + 1)):
                    ref[c, at : at + 1, :] = jnp.where(
                        new[line : line + 1], got[line : line + 1], ref[c, at : at + 1, :]
                    )


def merge_message(column_ref, message, first_kind, image, diagonal):
    size = image.shape[0] * LANES
    starts = table_starts((3 * size, 3 * size, size))
    for kind, merge in enumerate((merge_faces, merge_edges, merge_corners)):
        first = starts[kind][first_kind] // LANES
        merge(column_ref, message_tiles(message, kind), first, image, diagonal)


def merge_own(column, tables, image, diagonal, after):
    def kernel(column, faces, edges, corners, image_in, diagonal_in, *rest):
        image, diagonal = rest[-2:]
        image[...] = image_in[...]
        diagonal[...] = diagonal_in[...]
        merge_faces(column, table_tiles(faces), 0, image, diagonal)
        merge_edges(column, table_tiles(edges), 0, image, diagonal)
        merge_corners(column, table_tiles(corners), 0, image, diagonal)

    return pl.pallas_call(
        kernel,
        in_specs=[VMEM] * 6 + [ANY] * len(after),
        out_specs=[VMEM] * 2,
        out_shape=[jax.ShapeDtypeStruct(image.shape, F32)] * 2,
        name="merge_own",
        cost_estimate=QUICK,
        compiler_params=SMALL,
    )(column, *tables, image, diagonal, *after)


def merge_dom(column, message, image, diagonal, after):
    def kernel(column, message, image_in, diagonal_in, *rest):
        image, diagonal = rest[-2:]
        image[...] = image_in[...]
        diagonal[...] = diagonal_in[...]
        merge_message(column, message, 1, image, diagonal)

    return pl.pallas_call(
        kernel,
        in_specs=[VMEM] * 4 + [ANY] * len(after),
        out_specs=[VMEM] * 2,
        out_shape=[jax.ShapeDtypeStruct(image.shape, F32)] * 2,
        name="merge_dom",
        cost_estimate=QUICK,
        compiler_params=SMALL,
    )(column, message, image, diagonal, *after)


def relax_kernel(column, message, image_in, diagonal_in, field, forcing, source, *rest):
    relaxed, *outs, image, diagonal = rest[-7:]
    nodes, size = relaxed.shape
    image[...] = image_in[...]
    diagonal[...] = diagonal_in[...]
    merge_message(column, message, 2, image, diagonal)
    for row in range(0, nodes, STRIP):
        rows = slice(row, row + STRIP)
        for c in range(size // LANES):
            lanes = slice(c * LANES, (c + 1) * LANES)
            step = (forcing[rows, lanes] - image[c, rows, :]) / diagonal[c, rows, :]
            relaxed[rows, lanes] = field[rows, lanes] + RELAX * step
    for pair in range(2):
        source_row = source[:, pair * LANES : (pair + 1) * LANES]
        pack_block(relaxed, 0, nodes, source_row, outs[2 * pair : 2 * pair + 2], 0)


def relax_and_pack(column, message, image, diagonal, field, forcing, source, after):
    nodes, size = field.shape
    leaving = jax.ShapeDtypeStruct((nodes // 2, LANES), F32)
    return pl.pallas_call(
        relax_kernel,
        in_specs=[VMEM] * 7 + [ANY] * len(after),
        out_specs=[VMEM] * 5,
        out_shape=[jax.ShapeDtypeStruct((nodes, size), F32)] + [leaving] * 4,
        scratch_shapes=[pltpu.VMEM((size // LANES, nodes, LANES), F32)] * 2,
        name="relax_and_pack",
        cost_estimate=QUICK,
        compiler_params=SMALL,
    )(column, message, image, diagonal, field, forcing, source, *after)


def shifted(value, axis, steps):
    count = lax.axis_size(axis)
    return lax.ppermute(value, axis, [(i, (i + steps) % count) for i in range(count)])


def swapped(to_previous, to_next, axis):
    return shifted(to_next, axis, 1), shifted(to_previous, axis, -1)


def on_device(solution, forcing, metric, entity_ids, new_owner):
    size = solution.shape[-1]
    place = devices()
    table = derivative_table(solution.shape[0] - 1)
    field = solution.reshape(-1, size)
    metric_rows = pltpu.with_memory_space_constraint(metric.reshape(-1, size), pltpu.HBM)
    components = metric.shape[0]
    block = metric_rows.shape[0] // components
    source, landing, *messages, metric_rows = plan_and_pack(
        place, new_owner.reshape(1, size), metric_rows, block
    )
    sub_early = swapped(*messages, "sub")
    messages = pack(source, metric_rows, 0, DOM_EARLY, 0, block, (landing,), "pack_dom")
    dom_early = swapped(*messages, "dom")
    image, diagonal, column, *tables, dom, sub = apply_and_pack(
        place, entity_ids, field, metric_rows, messages[0], table
    )
    got_sub = shifted(sub, "sub", 1)
    messages = pack(
        source, metric_rows, SUB_EARLY, components - SUB_EARLY, 1, block, (sub,), "pack_sub_late"
    )
    sub_late = swapped(*messages, "sub")
    dom = pass_on(dom, got_sub, (*sub_early, messages[0]))
    got_dom = shifted(dom, "dom", 1)
    tables = add_sub(tables, got_sub, dom)
    *tables, dom_back = add_dom(tables, got_dom)
    back_dom = shifted(dom_back, "dom", -1)
    sub_back = read_sub(tables, got_sub)
    image, diagonal = merge_own(column, tables, image, diagonal, (dom_back,))
    sub_back = pass_on(sub_back, back_dom)
    back_sub = shifted(sub_back, "sub", -1)
    image, diagonal = merge_dom(column, back_dom, image, diagonal, sub_late)
    dom_moves, sub_moves = (dom_early, ()), (sub_early, sub_late)
    relaxed, *leaving = relax_and_pack(
        column, back_sub, image, diagonal, field, forcing.reshape(-1, size), source,
        (image,),
    )
    got_sub = swapped(*leaving[2:], "sub")
    got_dom = swapped(*leaving[:2], "dom")
    moved, token = land_metric(
        landing, metric_rows, dom_moves, sub_moves, 0, components, block, None, leaving[0],
        "land_metric",
    )
    smoothed = land_field(landing, relaxed, got_dom + got_sub, token)
    return smoothed.reshape(solution.shape), moved.reshape(metric.shape)


def solution(mesh):
    placed = (
        P(None, None, None, ("dom", "sub")),
        P(None, None, None, ("dom", "sub")),
        P(None, None, None, None, ("dom", "sub")),
        P(None, ("dom", "sub")),
        P(("dom", "sub")),
    )
    return jax.shard_map(
        on_device,
        mesh=mesh,
        in_specs=placed,
        out_specs=(P(None, None, None, ("dom", "sub")), P(None, None, None, None, ("dom", "sub"))),
        check_vma=False,
    )
```
